32 devices in a mesh: section: 2 (over x), dp: 8 (over z, core), head: 2 (over y).
Axes of the slice: x: 2, y: 2, z: 4, core: 2. Of those that a mesh axis runs over, the one named last changes fastest.
Arguments:
- tokens: bfloat16 [2, 2, 8192, 512], P('section', None, ('dp', 'head')), may hold values from -6 to 6
- self_routes: int32 [2, 2, 8192, 2], P('section', None, 'dp'), may hold values from 0 to 3, all different within a row
- cross_routes: int32 [2, 8192, 2], P(None, 'dp'), may hold values from 0 to 3, all different within a row
- lengths: int32 [2, 2, 8], P(None, None, 'dp'), may hold values from 512 to 1024
- cotangent: bfloat16 [2, 8192, 512], P(None, ('dp', 'head')), may hold values from -6 to 6
- norm_attn: bfloat16 [512], P('dp'), may hold values from 0.5 to 1.5
- norm_ffn: bfloat16 [512], P('dp'), may hold values from 0.5 to 1.5
- norm_final: bfloat16 [512], P('dp'), may hold values from 0.5 to 1.5
- norm_cross: bfloat16 [512], P('dp'), may hold values from 0.5 to 1.5
- router: bfloat16 [512, 4], P('dp'), may hold values from -0.125 to 0.125
- query_weight: bfloat16 [4, 512, 64], P('head', 'dp'), may hold values from -0.25 to 0.25
- key_weight: bfloat16 [512, 64], P('dp'), may hold values from -0.25 to 0.25
- value_weight: bfloat16 [512, 64], P('dp'), may hold values from -0.25 to 0.25
- output_weight: bfloat16 [4, 64, 512], P('head', None, 'dp'), may hold values from -6 to 6
- up_weight: bfloat16 [512, 2048], P('dp', 'head'), may hold values from -0.25 to 0.25
- down_weight: bfloat16 [2048, 512], P('head', 'dp'), may hold values from -0.125 to 0.125
- cross_router: bfloat16 [512, 4], P('dp'), may hold values from -0.125 to 0.125
- cross_query: bfloat16 [4, 512, 64], P('head', 'dp'), may hold values from -0.25 to 0.25
- cross_key: bfloat16 [512, 64], P('dp'), may hold values from -0.25 to 0.25
- cross_value: bfloat16 [512, 64], P('dp'), may hold values from -0.25 to 0.25
- cross_output: bfloat16 [4, 64, 512], P('head', None, 'dp'), may hold values from -6 to 6
Outputs:
- outputs: bfloat16 [2, 2, 8192, 512], P('section', None, ('dp', 'head'))
- input_grads: float32 [2, 2, 8192, 512], P('section', None, ('dp', 'head'))
- grad_norm_attn: float32 [512], P('dp')
- grad_norm_ffn: float32 [512], P('dp')
- grad_norm_final: float32 [512], P('dp')
- grad_norm_cross: float32 [512], P('dp')
- grad_router: float32 [512, 4], P('dp')
- grad_query_weight: float32 [4, 512, 64], P('head', 'dp')
- grad_key_weight: float32 [512, 64], P('dp')
- grad_value_weight: float32 [512, 64], P('dp')
- grad_output_weight: float32 [4, 64, 512], P('head', None, 'dp')
- grad_up_weight: float32 [512, 2048], P('dp', 'head')
- down_weight_gradient: float32 [2048, 512], P('head', 'dp')
- grad_cross_router: float32 [512, 4], P('dp')
- grad_cross_query: float32 [4, 512, 64], P('head', 'dp')
- grad_cross_key: float32 [512, 64], P('dp')
- grad_cross_value: float32 [512, 64], P('dp')
- grad_cross_output: float32 [4, 64, 512], P('head', None, 'dp')
The draws below stay inside these ranges and needn't reach their ends.
Inputs may be any that keep to these rules, and one draw needn't show every extreme that they name: `self_routes`: each token names two different experts. `cross_routes`: each token names two different experts.
All inputs are finite; a program needn't handle non-finite values.
Results may differ from the reference program's by a relative error of at most 0.024.
Values may be sent and summed in bfloat16 or wider, within the bound.
A program may use at most 256 MiB of HBM per device.

```python
import math
import jax
import jax.numpy as jnp
from jax import lax

D = 512
FF = 2048
HS = 64
E = 4
SEQ = 1024
MICRO = 2
ROWS = 8192
SEQS_MB = 8


def touch_ends(entries, rng, least, high):
    shape = entries.shape
    index_at = [jax.random.randint(jax.random.fold_in(rng, axis), (), 0, shape[axis]) for axis in range(len(shape))]
    entries = entries.at[tuple(index_at)].set(least)
    longest = shape.index(max(shape))
    index_at[longest] = (index_at[longest] + 1) % shape[longest]
    return entries.at[tuple(index_at)].set(high)


def levels(rng, shape, split, least, top_value):
    def one(position, shards_of):
        heights = jax.random.uniform(jax.random.fold_in(jax.random.fold_in(rng, 6), position), (shards_of,), jnp.float32, least / len(split), top_value / len(split))
        return jnp.repeat(jnp.exp(heights), shape[position] // shards_of).reshape((-1,) + (1,) * (len(shape) - position - 1))

    loudness = one(*split[0])
    for cut in split[1:]:
        loudness = loudness * one(*cut)
    return loudness


def different_ones(stream_key, rows, count, top, lift):
    sequence = jax.random.permutation(jax.random.fold_in(stream_key, 1), count)
    favour = sequence
    for power in range(3):
        favour = favour * favour // count
    favour = favour * lift // count
    chance = jax.random.randint(jax.random.fold_in(stream_key, 2), (rows, count), 0, 4096) + favour
    holders = jax.random.permutation(jax.random.fold_in(stream_key, 3), rows)[jnp.arange(count) % rows]
    chance = jnp.where(jnp.arange(rows)[:, None] == holders[None, :], 1 << 14, chance)
    priority = chance * count + jnp.arange(count)
    return lax.top_k(priority.astype(jnp.int32), top)[1].astype(jnp.int32)


def normal_values(stream_key, shape, spread, limit, cuts=(), held_as=jnp.bfloat16):
    entries = jax.random.normal(stream_key, shape, jnp.float32) * spread
    if len(cuts) > 0:
        entries = levels(stream_key, shape, cuts, -0.22, 0.18) * entries
    return jnp.clip(entries, min=-limit, max=limit).astype(held_as)


def setup_inputs(seed: int = 0) -> dict:
    key_of = jax.random.split(jax.random.key(seed), 22)
    return {
        "tokens": normal_values(key_of[0], (2, MICRO, ROWS, D), 1.0, 6.0, ((0, 2), (2, 16))),
        "self_routes": different_ones(key_of[1], 2 * MICRO * ROWS, E, 2, 4096).reshape((2, MICRO, ROWS, 2)),
        "cross_routes": different_ones(key_of[2], MICRO * ROWS, E, 2, 4096).reshape((MICRO, ROWS, 2)),
        "lengths": touch_ends(jax.random.randint(key_of[3], (2, MICRO, SEQS_MB), SEQ // 2, SEQ + 1), jax.random.fold_in(key_of[3], 1), SEQ // 2, SEQ).astype(jnp.int32),
        "cotangent": normal_values(key_of[4], (MICRO, ROWS, D), 1.0, 6.0, ((1, 16),)),
        "norm_attn": jnp.clip(1.0 + 0.1 * jax.random.normal(key_of[5], (D,), jnp.float32), 0.5, 1.5).astype(jnp.bfloat16),
        "norm_ffn": jnp.clip(1.0 + 0.1 * jax.random.normal(key_of[6], (D,), jnp.float32), 0.5, 1.5).astype(jnp.bfloat16),
        "norm_final": jnp.clip(1.0 + 0.1 * jax.random.normal(key_of[7], (D,), jnp.float32), 0.5, 1.5).astype(jnp.bfloat16),
        "norm_cross": jnp.clip(1.0 + 0.1 * jax.random.normal(key_of[8], (D,), jnp.float32), 0.5, 1.5).astype(jnp.bfloat16),
        "router": normal_values(key_of[9], (D, E), (4 * D) ** -0.5, 0.125, ((0, 8),)),
        "query_weight": normal_values(key_of[10], (E, D, HS), D ** -0.5, 0.25, ((0, 2), (1, 8))),
        "key_weight": normal_values(key_of[11], (D, HS), D ** -0.5, 0.25, ((0, 8),)),
        "value_weight": normal_values(key_of[12], (D, HS), D ** -0.5, 0.25, ((0, 8),)),
        "output_weight": normal_values(key_of[13], (E, HS, D), 1 ** -0.5, 6.0, ((0, 2), (2, 8))),
        "up_weight": normal_values(key_of[14], (D, FF), D ** -0.5, 0.25, ((0, 8), (1, 2))),
        "down_weight": normal_values(key_of[15], (FF, D), FF ** -0.5, 0.125, ((0, 2), (1, 8))),
        "cross_router": normal_values(key_of[16], (D, E), (4 * D) ** -0.5, 0.125, ((0, 8),)),
        "cross_query": normal_values(key_of[17], (E, D, HS), D ** -0.5, 0.25, ((0, 2), (1, 8))),
        "cross_key": normal_values(key_of[18], (D, HS), D ** -0.5, 0.25, ((0, 8),)),
        "cross_value": normal_values(key_of[19], (D, HS), D ** -0.5, 0.25, ((0, 8),)),
        "cross_output": normal_values(key_of[20], (E, HS, D), 1 ** -0.5, 6.0, ((0, 2), (2, 8))),
    }


EPSILON = 1e-05
PRECISE = lax.Precision.HIGHEST
NEGATIVE_FAR = -1e+30

@jax.custom_vjp
def low(v):
    return lax.optimization_barrier(v.astype(jnp.bfloat16)).astype(jnp.float32)

@jax.custom_vjp
def low_back(v):
    return v

def low_keep(v):
    return (low(v), None)

def low_pass(kept, grad):
    return (grad,)

def back_keep(v):
    return (v, None)

def back_low(kept, grad):
    return (low(grad),)
low.defvjp(low_keep, low_pass)
low_back.defvjp(back_keep, back_low)

def product(left, right):
    return jnp.dot(left, right, precision=PRECISE)

def layer_norm(rows, gain):
    center = lax.optimization_barrier(jnp.mean(rows, -1, keepdims=True))
    centred = rows - center
    return centred * lax.rsqrt(lax.optimization_barrier(jnp.mean(centred * centred, -1, keepdims=True)) + EPSILON) * gain

def gate_grid(logits, routes):
    onehot = (routes[:, :, None] == jnp.arange(logits.shape[1], dtype=jnp.int32)[None, None, :]).astype(jnp.float32)
    chosen = lax.optimization_barrier(jnp.sum(onehot * logits[:, None, :], -1))
    gate_values = jax.nn.softmax(chosen, -1)
    return lax.optimization_barrier(jnp.sum(onehot * gate_values[:, :, None], 1))

def mixture(normed, source, router_w, query_w, key_w, value_w, output_w, routes, allowed):
    scale = 1.0 / math.sqrt(query_w.shape[2])
    grid = gate_grid(product(normed, router_w), routes)
    key_rows = low_back(low(product(source, key_w)))
    value_rows = low_back(low(product(source, value_w)))

    def expert(pieces):
        query_one, output_one, column = pieces
        queries = low_back(low(product(normed, query_one)))
        scores = low_back(product(queries, key_rows.T) * scale)
        scores = jnp.where(allowed, scores, NEGATIVE_FAR)
        chances = jax.nn.softmax(scores, -1)
        attended = low_back(product(low(chances), value_rows))
        gated = low_back(low(column[:, None] * attended))
        return product(gated, output_one)
    branches = lax.map(jax.checkpoint(expert), (query_w, output_w, grid.T))
    return low_back(lax.optimization_barrier(jnp.sum(branches, 0)))

def feed(normed, up_w, down_w):
    hidden = low_back(product(normed, up_w))
    return low_back(product(low(jax.nn.gelu(hidden, approximate=True)), down_w))

def pair_layers(params, source, target, route_src, route_tgt, route_cross, length_src, length_tgt):
    norm_attn, norm_ffn, norm_final, norm_cross, router, query_weight, key_weight, value_weight, output_weight, up_weight, down_weight, cross_router, cross_query, cross_key, cross_value, cross_output = params
    places = jnp.arange(source.shape[0], dtype=jnp.int32)
    source_keys = places[None, :] < length_src
    target_keys = (places[None, :] <= places[:, None]) & (places[None, :] < length_tgt)
    normed = low(layer_norm(source, norm_attn))
    hidden = source + mixture(normed, normed, router, query_weight, key_weight, value_weight, output_weight, route_src, source_keys)
    hidden = hidden + feed(low(layer_norm(hidden, norm_ffn)), up_weight, down_weight)
    memory = low_back(low(layer_norm(hidden, norm_final)))
    normed = low(layer_norm(target, norm_attn))
    upper = target + mixture(normed, normed, router, query_weight, key_weight, value_weight, output_weight, route_tgt, target_keys)
    normed = low(layer_norm(upper, norm_cross))
    upper = upper + mixture(normed, memory, cross_router, cross_query, cross_key, cross_value, cross_output, route_cross, source_keys)
    upper = upper + feed(low(layer_norm(upper, norm_ffn)), up_weight, down_weight)
    return (memory, upper)

def reference(tokens, self_routes, cross_routes, lengths, cotangent, norm_attn, norm_ffn, norm_final, norm_cross, router, query_weight, key_weight, value_weight, output_weight, up_weight, down_weight, cross_router, cross_query, cross_key, cross_value, cross_output):
    params = tuple((weight.astype(jnp.float32) for weight in (norm_attn, norm_ffn, norm_final, norm_cross, router, query_weight, key_weight, value_weight, output_weight, up_weight, down_weight, cross_router, cross_query, cross_key, cross_value, cross_output)))
    width = tokens.shape[3]
    count = MICRO * ROWS // SEQ
    sources = tokens[0].astype(jnp.float32).reshape(count, SEQ, width)
    targets = tokens[1].astype(jnp.float32).reshape(count, SEQ, width)
    routes_src = self_routes[0].reshape(count, SEQ, 2)
    routes_tgt = self_routes[1].reshape(count, SEQ, 2)
    routes_cross = cross_routes.reshape(count, SEQ, 2)
    lengths_src = lengths[0].reshape(count)
    lengths_tgt = lengths[1].reshape(count)
    one_pair = jax.checkpoint(pair_layers)

    def forward(weights, src_all, tgt_all):

        def advance(carry, pieces):
            return (carry, one_pair(weights, *pieces))
        _, stacked = lax.scan(advance, jnp.zeros((), jnp.float32), (src_all, tgt_all, routes_src, routes_tgt, routes_cross, lengths_src, lengths_tgt))
        return stacked
    (memory, upper), pull = jax.vjp(forward, params, sources, targets)
    grad_params, source_gradient, grad_tgt = pull((jnp.zeros_like(memory), cotangent.astype(jnp.float32).reshape(count, SEQ, width)))
    grad_attn, grad_ffn, grad_final, grad_cross, grad_router, grad_query, grad_key, grad_value, grad_output, grad_up, grad_down, grad_crouter, grad_cquery, grad_ckey, grad_cvalue, grad_coutput = grad_params
    outputs = jnp.stack([memory, upper]).reshape(2, MICRO, ROWS, width).astype(jnp.bfloat16)
    input_grads = jnp.stack([source_gradient, grad_tgt]).reshape(2, MICRO, ROWS, width)
    return (outputs, input_grads, grad_attn, grad_ffn, grad_final, grad_cross, grad_router, grad_query, grad_key, grad_value, grad_output, grad_up, grad_down, grad_crouter, grad_cquery, grad_ckey, grad_cvalue, grad_coutput)
```

```python
import functools
import math

import jax
import jax.numpy as jnp
from jax import lax
from jax.experimental import pallas as pl
from jax.experimental.pallas import tpu as pltpu
from jax.sharding import PartitionSpec as P

EPSILON = 1e-05
FAR = -1e30
F32 = jnp.float32
BF16 = jnp.bfloat16
MESH = pl.DeviceIdType.MESH
NN = (((1,), (0,)), ((), ()))
NT = (((1,), (1,)), ((), ()))
TN = (((0,), (0,)), ((), ()))


def mm(a, b, dims=NN):
    return lax.dot_general(a, b, dims, preferred_element_type=F32)


def chunks(total, size, body):
    def step(i, carry):
        body(pl.ds(pl.multiple_of(i * size, size), size))
        return carry

    lax.fori_loop(0, total // size, step, 0)


def norm_parts(x):
    centred = x - jnp.mean(x, -1, keepdims=True)
    rstd = lax.rsqrt(jnp.mean(centred * centred, -1, keepdims=True) + EPSILON)
    return centred * rstd, rstd


def norm_back(x, gain, dz):
    xhat, rstd = norm_parts(x)
    dxh = dz * gain
    dx = (
        dxh
        - jnp.mean(dxh, -1, keepdims=True)
        - xhat * jnp.mean(dxh * xhat, -1, keepdims=True)
    ) * rstd
    return dx, jnp.sum(dz * xhat, 0, keepdims=True)


class Rows:
    def __init__(self, q, h):
        at = 0
        for name, size in (
            ("q", q), ("kv", 2 * h), ("r", 16), ("o", q),
            ("cq", q), ("cr", 16), ("ckv", 2 * h), ("co", q), ("gain", 16),
        ):
            setattr(self, name, slice(at, at + size))
            at += size
        self.total = at
        self.self_in = slice(self.q.start, self.r.stop)
        self.cross_in = slice(self.cq.start, self.cr.stop)


def layer_kernel(
    rows, experts, hs,
    src_ref, tgt_ref, mask_ref, lens_ref, ct_ref, wa_ref, up_ref, down_ref,
    mem_ref, y_ref, dsrc_ref, dtgt_ref, ga_ref, gup_ref, gdown_ref,
    a1, qT, kvT, kT, vT, kA, vA, qA, dA, gate, prob, attT, rl, hT, dT, dkv,
    mid, top, fa, b2, act, gp, work, workb, gacc, kvs, kvr, send_sem, recv_sem,
):
    R, W = src_ref.shape
    T = 2 * R
    FF = up_ref.shape[1]
    QR = experts * hs
    half = lax.axis_index("head")
    peer = {"head": 1 - half}
    LC = 128
    FC = 512
    scale = 1.0 / math.sqrt(hs)
    ENC, DEC, CROSS = 0, 1, 2

    barrier = pltpu.get_barrier_semaphore()
    pl.semaphore_signal(barrier, inc=1, device_id=peer, device_id_type=MESH)
    pl.semaphore_wait(barrier, 1)

    def exchange(slot):
        return pltpu.make_async_remote_copy(
            src_ref=kvs.at[slot], dst_ref=kvr.at[slot],
            send_sem=send_sem.at[slot], recv_sem=recv_sem.at[slot],
            device_id=peer, device_id_type=MESH,
        )

    def gain(k):
        at = rows.gain.start
        return wa_ref[at : at + 16, :].astype(F32)[k : k + 1, :]

    gacc[...] = jnp.zeros_like(gacc)

    def norm_to(source, out, base, k):
        g = gain(k)

        def body(s):
            xhat, _ = norm_parts(source[s, :].astype(F32))
            out[pl.ds(base + s.start, LC), :] = (xhat * g).astype(BF16)

        chunks(R, LC, body)

    def gates(m, logits):
        named = mask_ref[8 * m : 8 * m + experts, :]
        l = jnp.where(named > 0, logits[0:experts], FAR)
        p = jnp.exp(l - jnp.max(l, 0, keepdims=True)) * named
        gate[m, 0:experts, :] = p / jnp.sum(p, 0, keepdims=True)

    def set_keys(m, length_row):
        lane = lax.broadcasted_iota(jnp.int32, (1, T), 1)
        pos = jnp.where(lane < R, lane + half * R, lane - R + (1 - half) * R).astype(F32)
        length = lens_ref[length_row : length_row + 1, 0:1]
        outside = jnp.where(pos < length, 0.0, FAR)
        kT[m, 0:hs, :] = kvT[m, 0:hs, :]
        sub = lax.broadcasted_iota(jnp.int32, (128 - hs, T), 0)
        kT[m, hs:128, :] = jnp.where(sub == 0, outside, 0.0).astype(BF16)
        vT[m, 0:hs, :] = kvT[m, hs : 2 * hs, :]
        vT[m, hs:128, :] = jnp.where(sub < 2, 1.0, 0.0).astype(BF16)
        kA[m] = kT[m].astype(F32).T.astype(BF16)
        vA[m] = vT[m].astype(F32).T.astype(BF16)

    sub = lax.broadcasted_iota(jnp.int32, (128 - hs, R), 0)
    qA[hs:128, :] = jnp.where(sub == 0, 1.0, 0.0).astype(BF16)
    dA[hs:128, :] = jnp.zeros((128 - hs, R), BF16)

    def attend(m, causal):
        def one(e, carry):
            qA[0:hs, :] = qT[m, e]
            scores = mm(kA[m], qA[...])
            if causal:
                k = lax.broadcasted_iota(jnp.int32, (T, 1), 0)
                k = jnp.where(k < R, k + half * R, k - R + (1 - half) * R)
                q = lax.broadcasted_iota(jnp.int32, (1, R), 1) + half * R
                scores = jnp.where(k <= q, scores, FAR)
            p = jnp.exp(scores - jnp.max(scores, 0, keepdims=True)).astype(BF16)
            prob[m, e] = p
            out = mm(vT[m, 0 : hs + 16, :], p)
            inverse = 1.0 / out[hs : hs + 1, :]
            attended = out[0:hs, :] * inverse
            attT[m, e] = attended
            rl[m, pl.ds(e, 1), :] = inverse
            hT[m, pl.ds(pl.multiple_of(e * hs, hs), hs), :] = (
                gate[m, pl.ds(e, 1), :] * attended
            ).astype(BF16)
            return carry

        lax.fori_loop(0, experts, one, 0)

    def attend_back(m, dout, wo):
        dH = mm(wa_ref[wo, :], dout, NT).astype(BF16)
        ga = mm(hT[m], dout)
        work[0:QR, :] = dH.astype(F32)
        dkv[...] = jnp.zeros_like(dkv)

        def one(e, carry):
            d = work[pl.ds(pl.multiple_of(e * hs, hs), hs), 0:R]
            dg = jnp.sum(d * attT[m, e], 0, keepdims=True)
            g = gate[m, pl.ds(e, 1), :]
            inverse = rl[m, pl.ds(e, 1), :]
            gate[m, pl.ds(experts + e, 1), :] = dg
            da = (d * (g * inverse)).astype(BF16)
            delta = g * dg * inverse
            high = delta.astype(BF16).astype(F32)
            row = lax.broadcasted_iota(jnp.int32, (16, R), 0)
            dA[0:hs, :] = da
            dA[hs : hs + 16, :] = jnp.where(
                row == 0, -high, jnp.where(row == 1, high - delta, 0.0)
            ).astype(BF16)
            p = prob[m, e]
            ds = (p.astype(F32) * mm(vA[m], dA[...])).astype(BF16)
            dq = mm(kT[m, 0:hs, :], ds) * scale
            dT[m, pl.ds(pl.multiple_of(e * hs, hs), hs), :] = dq.astype(BF16)
            dkv[0:hs, :] += mm(qT[m, e], ds, NT)
            dkv[hs : 2 * hs, :] += mm(da, p, NT)
            return carry

        lax.fori_loop(0, experts, one, 0)
        g = gate[m, 0:experts, :]
        dg = gate[m, experts : 2 * experts, :]
        dl = g * (dg - jnp.sum(g * dg, 0, keepdims=True))
        dT[m, QR : QR + 16, :] = jnp.concatenate(
            [dl, jnp.zeros((16 - experts, R), F32)], 0
        ).astype(BF16)
        return ga

    def feed(m, out):
        c0 = math.sqrt(2.0 / math.pi)

        def body(i, carry):
            cols = pl.ds(pl.multiple_of(i * FC, FC), FC)
            u = mm(fa[pl.ds(m * R, R), :], up_ref[:, cols])
            u2 = u * u
            t = jnp.tanh(c0 * u * (1.0 + 0.044715 * u2))
            half_up = 0.5 * (1.0 + t)
            a = (u * half_up).astype(BF16)
            act[pl.ds(m * R, R), cols] = a
            gp[pl.ds(m * R, R), cols] = (
                half_up + 0.5 * u * (1.0 - t * t) * (c0 * (1.0 + 3 * 0.044715 * u2))
            ).astype(BF16)
            part = mm(a, down_ref[:, cols], NT)

            @pl.when(i == 0)
            def _():
                out[...] = part

            @pl.when(i > 0)
            def _():
                out[...] += part

            return carry

        lax.fori_loop(0, FF // FC, body, 0)

    def feed_back(m, dout, out):
        def body(i, carry):
            cols = pl.ds(pl.multiple_of(i * FC, FC), FC)
            d = mm(dout[...], down_ref[:, cols])
            d = (d * gp[pl.ds(m * R, R), cols].astype(F32)).astype(BF16)
            gp[pl.ds(m * R, R), cols] = d
            part = mm(d, up_ref[:, cols], NT)

            @pl.when(i == 0)
            def _():
                out[...] = part

            @pl.when(i > 0)
            def _():
                out[...] += part

            return carry

        lax.fori_loop(0, FF // FC, body, 0)

    def norm_back_into(x, k, dz, add, outs):
        g = gain(k)

        def body(s):
            dx, dg = norm_back(x[s, :].astype(F32), g, dz[s, :])
            gacc[k : k + 1, :] += dg
            total = dx if add is None else add[s, :].astype(F32) + dx
            for out in outs:
                out[s, :] = total.astype(out.dtype)

        chunks(R, LC, body)

    norm_to(src_ref, a1, 0, 0)
    norm_to(tgt_ref, a1, R, 0)
    for m in (ENC, DEC):
        kvs[m] = mm(wa_ref[rows.kv, :], a1[m * R : (m + 1) * R, :], NT).astype(BF16)
        exchange(m).start()
    for m in (ENC, DEC):
        z = mm(wa_ref[rows.self_in, :], a1[m * R : (m + 1) * R, :], NT)
        qT[m] = (z[0:QR].astype(BF16).astype(F32) * scale).astype(BF16).reshape(experts, hs, R)
        gates(m, z[QR + 2 * hs :])
    for m in (ENC, DEC):
        kvT[m, :, 0:R] = kvs[m]
        exchange(m).wait()
        kvT[m, :, R:T] = kvr[m]
        set_keys(m, m)

    attend(ENC, False)
    mid[ENC] = src_ref[...].astype(F32) + mm(hT[ENC], wa_ref[rows.o, :], TN)
    norm_to(mid.at[ENC], fa, 0, 1)
    feed(0, top.at[ENC])
    top[ENC] += mid[ENC]
    norm_to(top.at[ENC], mem_ref, 0, 2)
    kvs[CROSS] = mm(wa_ref[rows.ckv, :], mem_ref[...], NT).astype(BF16)
    exchange(CROSS).start()

    attend(DEC, True)
    mid[DEC] = tgt_ref[...].astype(F32) + mm(hT[DEC], wa_ref[rows.o, :], TN)
    norm_to(mid.at[DEC], b2, 0, 3)
    z = mm(wa_ref[rows.cross_in, :], b2[...], NT)
    qT[CROSS] = (z[0:QR].astype(BF16).astype(F32) * scale).astype(BF16).reshape(experts, hs, R)
    gates(CROSS, z[QR:])
    kvT[CROSS, :, 0:R] = kvs[CROSS]
    exchange(CROSS).wait()
    kvT[CROSS, :, R:T] = kvr[CROSS]
    set_keys(CROSS, 0)
    attend(CROSS, False)
    top[DEC] = mid[DEC] + mm(hT[CROSS], wa_ref[rows.co, :], TN)
    norm_to(top.at[DEC], fa, R, 1)
    feed(1, work)
    y_ref[...] = (top[DEC] + work[...]).astype(BF16)

    feed_back(1, ct_ref, work)
    norm_back_into(top.at[DEC], 1, work, ct_ref, (top.at[DEC], workb.at[1]))
    ga_ref[rows.co, :] = attend_back(CROSS, workb[1], rows.co).astype(BF16)
    kvs[3] = dkv[:, R:T].astype(BF16)
    exchange(3).start()
    ga_ref[rows.cross_in, :] = mm(dT[CROSS, 0 : QR + 16, :], b2[...]).astype(BF16)
    work[...] = mm(dT[CROSS, 0 : QR + 16, :], wa_ref[rows.cross_in, :], TN)
    norm_back_into(mid.at[DEC], 3, work, top.at[DEC], (top.at[DEC], workb.at[1]))
    exchange(3).wait()
    dkvc = (dkv[:, 0:R] + kvr[3].astype(F32)).astype(BF16)
    ga_ref[rows.ckv, :] = mm(dkvc, mem_ref[...]).astype(BF16)
    work[...] = mm(dkvc, wa_ref[rows.ckv, :], TN).astype(BF16).astype(F32)
    norm_back_into(top.at[ENC], 2, work, None, (top.at[ENC], workb.at[0]))
    feed_back(0, workb.at[0], work)

    def weights(i, carry):
        cols = pl.ds(pl.multiple_of(i * FC, FC), FC)
        gup_ref[:, cols] = mm(fa[...], gp[:, cols], TN).astype(BF16)
        gdown_ref[:, cols] = (
            mm(workb[0], act[0:R, cols], TN) + mm(ct_ref[...], act[R:T, cols], TN)
        ).astype(BF16)
        return carry

    lax.fori_loop(0, FF // FC, weights, 0)
    norm_back_into(mid.at[ENC], 1, work, top.at[ENC], (top.at[ENC], workb.at[0]))

    go = attend_back(DEC, workb[1], rows.o)
    kvs[5] = dkv[:, R:T].astype(BF16)
    exchange(5).start()
    work[0 : 2 * hs, :] = dkv[:, 0:R]
    dT[DEC, QR + 16 : QR + 16 + 2 * hs, :] = work[0 : 2 * hs, :].astype(BF16)
    kept = dkv[:, 0:R]
    go += attend_back(ENC, workb[0], rows.o)
    ga_ref[rows.o, :] = go.astype(BF16)
    kvs[4] = dkv[:, R:T].astype(BF16)
    exchange(4).start()
    own = (dkv[:, 0:R], kept)
    for m, slot in ((DEC, 5), (ENC, 4)):
        exchange(slot).wait()
        dT[m, QR + 16 : QR + 16 + 2 * hs, :] = (own[m] + kvr[slot].astype(F32)).astype(BF16)
    for part, at in ((rows.q, 0), (rows.r, QR), (rows.kv, QR + 16)):
        n = part.stop - part.start
        ga_ref[part, :] = (
            mm(dT[ENC, at : at + n, :], a1[0:R, :]) + mm(dT[DEC, at : at + n, :], a1[R:T, :])
        ).astype(BF16)
    for m, x, out in ((DEC, tgt_ref, dtgt_ref), (ENC, src_ref, dsrc_ref)):
        work[...] = sum(
            mm(dT[m, at : at + part.stop - part.start, :], wa_ref[part, :], TN)
            for part, at in ((rows.q, 0), (rows.r, QR), (rows.kv, QR + 16))
        )
        norm_back_into(x, 0, work, top.at[m], (out,))
    ga_ref[rows.gain, :] = gacc[...].astype(BF16)


def run_layers(rows, experts, hs, src, tgt, mask, lens, ct, wa, up, down):
    R, W = src.shape
    T, FF, QR = 2 * R, up.shape[1], experts * hs
    vm = pltpu.VMEM
    return pl.pallas_call(
        functools.partial(layer_kernel, rows, experts, hs),
        out_shape=(
            jax.ShapeDtypeStruct((R, W), BF16),
            jax.ShapeDtypeStruct((R, W), BF16),
            jax.ShapeDtypeStruct((R, W), F32),
            jax.ShapeDtypeStruct((R, W), F32),
            jax.ShapeDtypeStruct((rows.total, W), BF16),
            jax.ShapeDtypeStruct((W, FF), BF16),
            jax.ShapeDtypeStruct((W, FF), BF16),
        ),
        in_specs=[pl.BlockSpec(memory_space=vm)] * 8,
        out_specs=[pl.BlockSpec(memory_space=vm)] * 7,
        scratch_shapes=[
            vm((T, W), BF16),
            vm((3, experts, hs, R), BF16),
            vm((3, 2 * hs, T), BF16),
            vm((3, 128, T), BF16),
            vm((3, 128, T), BF16),
            vm((3, T, 128), BF16),
            vm((3, T, 128), BF16),
            vm((128, R), BF16),
            vm((128, R), BF16),
            vm((3, 2 * experts, R), F32),
            vm((3, experts, T, R), BF16),
            vm((3, experts, hs, R), F32),
            vm((3, 8, R), F32),
            vm((3, QR, R), BF16),
            vm((3, QR + 16 + 2 * hs, R), BF16),
            vm((2 * hs, T), F32),
            vm((2, R, W), F32),
            vm((2, R, W), F32),
            vm((T, W), BF16),
            vm((R, W), BF16),
            vm((T, FF), BF16),
            vm((T, FF), BF16),
            vm((R, W), F32),
            vm((2, R, W), BF16),
            vm((16, W), F32),
            vm((6, 2 * hs, R), BF16),
            vm((6, 2 * hs, R), BF16),
            pltpu.SemaphoreType.DMA((6,)),
            pltpu.SemaphoreType.DMA((6,)),
        ],
        compiler_params=pltpu.CompilerParams(
            collective_id=0, has_side_effects=True, vmem_limit_bytes=60 * 2**20
        ),
    )(src, tgt, mask, lens, ct, wa, up, down)


def on_device(
    tokens, self_routes, cross_routes, lengths, cotangent,
    norm_attn, norm_ffn, norm_final, norm_cross,
    router, query_weight, key_weight, value_weight, output_weight, up_weight, down_weight,
    cross_router, cross_query, cross_key, cross_value, cross_output,
):
    section = lax.axis_index("section")
    half = lax.axis_index("head")
    dp = lax.axis_size("dp")
    heads = lax.axis_size("head")
    local, W = tokens.shape[2:]
    el, _, hs = query_weight.shape
    experts = el * heads
    D = query_weight.shape[1]
    rows = Rows(experts * hs, hs)
    swap = [(0, 1), (1, 0)]

    def named(routes):
        ids = jnp.arange(experts, dtype=jnp.int32)[:, None]
        m = ((routes[:, 0][None] == ids) | (routes[:, 1][None] == ids)).astype(F32)
        return jnp.concatenate([m, jnp.zeros((8 - experts, m.shape[1]), F32)], 0)

    def mine(a, axis=0):
        return lax.dynamic_slice_in_dim(a, half * local, local, axis)

    def pick(a, k):
        return lax.dynamic_index_in_dim(a, k, 0, keepdims=False)

    own, other = pick(tokens[0], section), pick(tokens[0], 1 - section)
    routes = mine(self_routes[0], 1)
    own_named, other_named = named(pick(routes, section)), named(pick(routes, 1 - section))
    other = lax.ppermute(other, "section", swap)
    other_named = lax.ppermute(other_named.astype(BF16), "section", swap).astype(F32)
    first = section == 0
    src, tgt = jnp.where(first, own, other), jnp.where(first, other, own)
    mask = jnp.concatenate(
        [
            jnp.where(first, own_named, other_named),
            jnp.where(first, other_named, own_named),
            named(mine(pick(cross_routes, section))),
        ],
        0,
    )
    lens = jnp.broadcast_to(
        jnp.pad(lengths[:, section, 0].astype(F32), (0, 6))[:, None], (8, 128)
    )
    ct = pick(cotangent, section)

    def flat(w):
        return jnp.swapaxes(w, 1, 2).reshape(el * hs, D)

    def pad16(w):
        return jnp.pad(w, ((0, 16 - w.shape[0]), (0, 0)))

    split = jnp.concatenate(
        [
            flat(query_weight), output_weight.reshape(el * hs, D),
            flat(cross_query), cross_output.reshape(el * hs, D),
        ], 0,
    )
    whole = jnp.concatenate(
        [
            key_weight.T, value_weight.T, pad16(router.T),
            cross_key.T, cross_value.T, pad16(cross_router.T),
            pad16(jnp.stack([norm_attn, norm_ffn, norm_final, norm_cross])),
        ], 0,
    )
    n = el * hs
    split = lax.all_gather(lax.all_gather(split, "dp", axis=1, tiled=True), "head", axis=0)
    whole = lax.all_gather(whole, "dp", axis=1, tiled=True)
    q, o, cq, co = (split[:, k * n : (k + 1) * n].reshape(heads * n, W) for k in range(4))
    k2 = 2 * hs
    wa = jnp.concatenate(
        [
            q, whole[: k2 + 16], o, cq,
            whole[2 * k2 + 16 : 2 * k2 + 32], whole[k2 + 16 : 2 * k2 + 16], co,
            whole[2 * k2 + 32 :],
        ], 0,
    )
    ffn = jnp.stack([up_weight, down_weight.T])
    ffn = lax.all_gather(
        lax.all_gather(ffn, "dp", axis=1, tiled=True), "head", axis=2, tiled=True
    )

    memory, y, dsrc, dtgt, ga, gup, gdown = run_layers(
        rows, experts, hs, src, tgt, mask, lens, ct, wa, ffn[0], ffn[1]
    )

    def placed(s, t):
        keep, send = jnp.where(first, s, t), jnp.where(first, t, s).astype(BF16)
        came = lax.ppermute(send, "section", swap).astype(keep.dtype)
        return jnp.where(first, jnp.stack([keep, came]), jnp.stack([came, keep]))

    outputs = placed(memory, y)
    input_grads = placed(dsrc, dtgt)

    def scattered(a, axis):
        return lax.psum_scatter(a, "dp", scatter_dimension=axis, tiled=True)

    gffn = lax.psum_scatter(
        jnp.stack([gup, gdown]), "head", scatter_dimension=2, tiled=True
    )
    gffn = lax.psum(scattered(gffn, 1), "section").astype(F32)
    gs = jnp.concatenate([ga[r].reshape(heads, n, W) for r in (rows.q, rows.o, rows.cq, rows.co)], 1)
    gs = lax.psum_scatter(gs, "head", scatter_dimension=0, tiled=True)[0]
    gw = lax.psum(
        jnp.concatenate([ga[r] for r in (rows.kv, rows.r, rows.ckv, rows.cr, rows.gain)], 0), "head"
    )
    small = lax.psum(scattered(jnp.concatenate([gs, gw], 0), 1), "section").astype(F32)
    gq, go, gcq, gco = (small[k * n : (k + 1) * n].reshape(el, hs, D) for k in range(4))
    rest = small[4 * n :]
    gains = rest[2 * k2 + 32 :]
    return (
        outputs[None], input_grads[None],
        gains[0], gains[1], gains[2], gains[3],
        rest[k2 : k2 + experts].T, jnp.swapaxes(gq, 1, 2), rest[0:hs].T, rest[hs:k2].T, go,
        gffn[0], gffn[1].T,
        rest[2 * k2 + 16 : 2 * k2 + 16 + experts].T, jnp.swapaxes(gcq, 1, 2),
        rest[k2 + 16 : k2 + 16 + hs].T, rest[k2 + 16 + hs : 2 * k2 + 16].T, gco,
    )


def solution(mesh):
    rows = P("section", None, ("dp", "head"), None)
    vector, tall = P("dp"), P("dp", None)
    query, out = P("head", "dp", None), P("head", None, "dp")
    weights = (
        vector, vector, vector, vector,
        tall, query, tall, tall, out, P("dp", "head"), P("head", "dp"),
        tall, query, tall, tall, out,
    )
    return jax.shard_map(
        on_device,
        mesh=mesh,
        in_specs=(
            rows, P("section", None, "dp", None), P(None, "dp", None), P(None, None, "dp"),
            P(None, ("dp", "head"), None), *weights,
        ),
        out_specs=(rows, rows, *weights),
        check_vma=False,
    )
```

```python
import functools
import math

import jax
import jax.numpy as jnp
from jax import lax
from jax.experimental import pallas as pl
from jax.experimental.pallas import tpu as pltpu
from jax.sharding import PartitionSpec as P

EPSILON = 1e-05
FAR = -1e30
F32 = jnp.float32
BF16 = jnp.bfloat16
MESH = pl.DeviceIdType.MESH
NN = (((1,), (0,)), ((), ()))
NT = (((1,), (1,)), ((), ()))
TN = (((0,), (0,)), ((), ()))


def mm(a, b, dims=NN):
    return lax.dot_general(a, b, dims, preferred_element_type=F32)


def chunks(total, size, body):
    def step(i, carry):
        body(pl.ds(pl.multiple_of(i * size, size), size))
        return carry

    lax.fori_loop(0, total // size, step, 0)


def norm_parts(x):
    centred = x - jnp.mean(x, -1, keepdims=True)
    rstd = lax.rsqrt(jnp.mean(centred * centred, -1, keepdims=True) + EPSILON)
    return centred * rstd, rstd


def norm_back(x, gain, dz):
    xhat, rstd = norm_parts(x)
    dxh = dz * gain
    dx = (
        dxh
        - jnp.mean(dxh, -1, keepdims=True)
        - xhat * jnp.mean(dxh * xhat, -1, keepdims=True)
    ) * rstd
    return dx, jnp.sum(dz * xhat, 0, keepdims=True)


class Rows:
    def __init__(self, q, h):
        at = 0
        for name, size in (
            ("q", q), ("kv", 2 * h), ("r", 16), ("o", q),
            ("cq", q), ("cr", 16), ("ckv", 2 * h), ("co", q), ("gain", 16),
        ):
            setattr(self, name, slice(at, at + size))
            at += size
        self.total = at
        self.self_in = slice(self.q.start, self.r.stop)
        self.cross_in = slice(self.cq.start, self.cr.stop)


SELF, CROSSED, BLOCKS = 0, 6, 11
KV, MISC, CKV = 2, 3, 8


def layer_kernel(
    experts, hs, zs,
    tok, msk, xmsk, lens, ct_hbm, wsh, fsh,
    out_rows, out_grads, g_small, fin,
    mine, other, omsk, ct, wd, wa, ffn, a1, qT, kT, vT, kA, vA, qA, dA, gate, prob, attT, rl, hT, dT,
    dkv, mid, top, fa, b2, mem, act, gp, work, workb, gacc, gaT, gd, kvs, kvr, sent, came,
    rc, rx, ry, rx2, ry2, rz, sc, sx, sy, sg, sz, sfin, ssem, rsem, csem,
):
    R, W = mine.shape
    T = 2 * R
    FFH = ffn.shape[-1]
    nz, Dh = ffn.shape[2], ffn.shape[5]
    QR = experts * hs
    rows = Rows(QR, hs)
    LC, FC = 128, 512
    NC = rc.shape[0]
    CW = FFH // NC
    ENC, DEC, CROSS = 0, 1, 2
    scale = 1.0 / math.sqrt(hs)

    s, d, half = lax.axis_index("section"), lax.axis_index("dp"), lax.axis_index("head")
    zv, core = d // zs, d % 2
    to_x, to_y = {"section": 1 - s}, {"head": 1 - half}
    to_c = {"dp": d + 1 - 2 * core}
    to_z = [{"dp": (zv + k) % nz * zs + d % zs} for k in range(1, nz)]

    barrier = pltpu.get_barrier_semaphore()
    everyone = [to_x, to_y, to_c] + to_z
    for peer in everyone:
        pl.semaphore_signal(barrier, inc=1, device_id=peer, device_id_type=MESH)
    pl.semaphore_wait(barrier, len(everyone))

    started = []

    def push(src, dst, peer):
        k = len(started)
        copy = pltpu.make_async_remote_copy(
            src_ref=src, dst_ref=dst, send_sem=ssem.at[k], recv_sem=rsem.at[k],
            device_id=peer, device_id_type=MESH,
        )
        copy.start()
        started.append(copy)
        return copy

    left = []

    def waited_sends():
        for copy in started[len(left) :]:
            copy.wait_send()
            left.append(copy)

    queue = []

    def pump(n=1):
        for _ in range(n):
            if queue:
                queue.pop(0)[1]()

    def until(name):
        while any(k == name for k, _ in queue):
            queue.pop(0)[1]()

    mine_copy = pltpu.make_async_copy(tok.at[s], mine, csem.at[1])
    mine_copy.start()
    tokens_in = [push(tok.at[1 - s], other, to_x), push(msk.at[1 - s], omsk, to_x)]
    ct_copy = pltpu.make_async_copy(ct_hbm.at[s], ct, csem.at[0])
    ct_copy.start()

    q_own, q_far = 4 * half, 4 * (1 - half)
    c_own, c_far = CROSSED + 3 * half, CROSSED + 3 * (1 - half)
    groups = {
        "early": ((0, 2, KV), (2, 1, q_own)),
        "late": ((3, 1, q_own + 1), (4, 1, CKV), (5, 2, c_own)),
    }
    for at, n, to in groups["early"] + groups["late"]:
        wd[pl.ds(to, n), zv, core] = wsh[at : at + n]
    ffn[:, half, zv, core] = fsh[...]

    def z_push(group):
        return [
            push(wsh.at[at : at + n], wd.at[pl.ds(to, n), zv, core], peer)
            for peer in to_z
            for at, n, to in groups[group]
        ]

    def gather(group, split, far, shared):
        arrivals = z_push(group)
        over = {}

        def to_core(block, n):
            part = wd.at[pl.ds(block, n), :, core]
            return push(part, part, to_c)

        def one():
            for copy in arrivals:
                copy.wait_recv()
            over["y"] = []
            for block, n in split:
                part = wd.at[pl.ds(block, n), :, core]
                over["y"].append(push(part, part, to_y))
            over["c"] = [to_core(block, n) for block, n in split + shared]

        def two():
            for copy in over["y"]:
                copy.wait_recv()
            over["c"] += [to_core(block, n) for block, n in far]

        def three():
            for copy in over["c"]:
                copy.wait_recv()

        return [(group, one), (group, two), (group, three)]

    queue += gather("early", [(q_own, 1)], [(q_far, 1)], [(KV, 2)])
    pump(1)
    queue += gather(
        "late", [(q_own + 1, 1), (c_own, 2)], [(q_far + 1, 1), (c_far, 2)], [(CKV, 1)]
    )
    ffn_z = [push(fsh, ffn.at[:, half, zv, core], peer) for peer in to_z]
    ffn_y, ffn_c = {}, []

    def ffn_on(k):
        def run():
            if k > 0:
                ffn_z[k - 1].wait_recv()
            part = ffn.at[:, half, (zv - k + nz) % nz, core]
            ffn_y[k] = push(part, part, to_y)
            ffn_c.append(push(part, part, to_c))

        return ("ffn", run)

    def ffn_far(k):
        def run():
            ffn_y[k].wait_recv()
            part = ffn.at[:, 1 - half, (zv - k + nz) % nz, core]
            ffn_c.append(push(part, part, to_c))

        return ("ffn", run)

    def ffn_end():
        for copy in ffn_c:
            copy.wait_recv()

    ffn_events = [ffn_on(k) for k in range(1, nz)]
    for k in range(nz):
        ffn_events.insert(2 * k + 1, ffn_far(k))
    ffn_on(0)[1]()
    queue += ffn_events + [("ffn", ffn_end)]

    def block(b):
        return wd[b].reshape(W, 128).astype(F32).T.astype(BF16)

    def head_rows(part, b0, b1):
        n = (part.stop - part.start) // 2
        wa[part.start : part.start + n, :] = block(b0)
        wa[part.start + n : part.stop, :] = block(b1)

    def exchange(slot):
        return push(kvs.at[slot % 3], kvr.at[slot], to_y)

    def gain(k):
        at = rows.gain.start
        return wa[at : at + 16, :].astype(F32)[k : k + 1, :]

    def norm_to(source, out, k):
        g = gain(k)

        def body(c):
            xhat, _ = norm_parts(source[c, :].astype(F32))
            out[c, :] = (xhat * g).astype(BF16)

        chunks(R, LC, body)

    def gates(m, named, logits):
        named = named[0:16, :].astype(F32)[0:experts]
        l = jnp.where(named > 0, logits[0:experts], FAR)
        p = jnp.exp(l - jnp.max(l, 0, keepdims=True)) * named
        gate[m, 0:experts, :] = p / jnp.sum(p, 0, keepdims=True)

    def set_keys(m, slot, length):
        lane = lax.broadcasted_iota(jnp.int32, (1, T), 1)
        pos = jnp.where(lane < R, lane + half * R, lane - R + (1 - half) * R).astype(F32)
        outside = jnp.where(pos < length, 0.0, FAR)
        for to, at in ((kT, 0), (vT, hs)):
            to[m, 0:hs, 0:R] = kvs[slot, at : at + hs, :]
            to[m, 0:hs, R:T] = kvr[slot, at : at + hs, :]
        sub = lax.broadcasted_iota(jnp.int32, (128 - hs, T), 0)
        kT[m, hs:128, :] = jnp.where(sub == 0, outside, 0.0).astype(BF16)
        vT[m, hs:128, :] = jnp.where(sub < 2, 1.0, 0.0).astype(BF16)
        kA[m] = kT[m].astype(F32).T.astype(BF16)
        vA[m] = vT[m].astype(F32).T.astype(BF16)

    sub = lax.broadcasted_iota(jnp.int32, (128 - hs, R), 0)
    qA[hs:128, :] = jnp.where(sub == 0, 1.0, 0.0).astype(BF16)
    dA[hs:128, :] = jnp.zeros((128 - hs, R), BF16)
    gacc[...] = jnp.zeros_like(gacc)

    def over_experts(one, pumps):
        for e in range(experts):
            one(e, 0)
            pump(pumps)

    def attend(m, reach, pumps=1):
        def one(e, carry):
            qA[0:hs, :] = qT[m, e]
            scores = mm(kA[m], qA[...])
            if reach is not None:
                k = lax.broadcasted_iota(jnp.int32, (T, 1), 0)
                k = jnp.where(k < R, k + half * R, k - R + (1 - half) * R)
                q = lax.broadcasted_iota(jnp.int32, (1, R), 1) + half * R + reach
                scores = jnp.where(k <= q, scores, FAR)
            p = jnp.exp(scores - jnp.max(scores, 0, keepdims=True)).astype(BF16)
            prob[m, e] = p
            out = mm(vT[m, 0 : hs + 16, :], p)
            inverse = 1.0 / out[hs : hs + 1, :]
            attended = out[0:hs, :] * inverse
            attT[m, e] = attended
            rl[m, e : e + 1, :] = inverse
            hT[m, e * hs : (e + 1) * hs, :] = (gate[m, e : e + 1, :] * attended).astype(BF16)
            return carry

        over_experts(one, pumps)

    def attend_back(m, dout, wo, pumps=1):
        dH = mm(wa[wo, :], dout, NT).astype(BF16)
        go = mm(hT[m], dout)
        work[0:QR, 0:R] = dH.astype(F32)

        def one(e, carry):
            span = slice(e * hs, (e + 1) * hs)
            dh = work[span, 0:R]
            dg = jnp.sum(dh * attT[m, e], 0, keepdims=True)
            g = gate[m, e : e + 1, :]
            inverse = rl[m, e : e + 1, :]
            gate[m, experts + e : experts + e + 1, :] = dg
            da = (dh * (g * inverse)).astype(BF16)
            delta = g * dg * inverse
            high = delta.astype(BF16).astype(F32)
            row = lax.broadcasted_iota(jnp.int32, (16, R), 0)
            dA[0:hs, :] = da
            dA[hs : hs + 16, :] = jnp.where(
                row == 0, -high, jnp.where(row == 1, high - delta, 0.0)
            ).astype(BF16)
            p = prob[m, e]
            ds = (p.astype(F32) * mm(vA[m], dA[...])).astype(BF16)
            dT[m, span, :] = (mm(kT[m, 0:hs, :], ds) * scale).astype(BF16)
            dk, dv = mm(qT[m, e], ds, NT), mm(da, p, NT)
            if e == 0:
                dkv[0:hs, :], dkv[hs : 2 * hs, :] = dk, dv
            else:
                dkv[0:hs, :] += dk
                dkv[hs : 2 * hs, :] += dv
            return carry

        over_experts(one, pumps)
        g = gate[m, 0:experts, :]
        dg = gate[m, experts : 2 * experts, :]
        dl = g * (dg - jnp.sum(g * dg, 0, keepdims=True))
        dT[m, QR : QR + 16, :] = jnp.concatenate(
            [dl, jnp.zeros((16 - experts, R), F32)], 0
        ).astype(BF16)
        return go

    def ffn_cols(mat, i):
        n = FFH // FC
        cols = pl.ds(pl.multiple_of(i % n * FC, FC), FC)
        return ffn[mat, i // n, :, :, :, :, cols].reshape(W, FC)

    def feed(m, out):
        c0 = math.sqrt(2.0 / math.pi)

        def body(i, carry):
            cols = pl.ds(pl.multiple_of(i * FC, FC), FC)
            u = mm(fa[m], ffn_cols(0, i))
            u2 = u * u
            t = jnp.tanh(c0 * u * (1.0 + 0.044715 * u2))
            half_up = 0.5 * (1.0 + t)
            a = (u * half_up).astype(BF16)
            act[m, :, cols] = a
            gp[m, :, cols] = (
                half_up + 0.5 * u * (1.0 - t * t) * (c0 * (1.0 + 3 * 0.044715 * u2))
            ).astype(BF16)
            part = mm(a, ffn_cols(1, i), NT)

            @pl.when(i == 0)
            def _():
                out[...] = part

            @pl.when(i > 0)
            def _():
                out[...] += part

            return carry

        lax.fori_loop(0, 2 * FFH // FC, body, 0)

    def feed_back(m, dout, out):
        def body(i, carry):
            cols = pl.ds(pl.multiple_of(i * FC, FC), FC)
            dh = mm(dout[...], ffn_cols(1, i))
            dh = (dh * gp[m, :, cols].astype(F32)).astype(BF16)
            gp[m, :, cols] = dh
            part = mm(dh, ffn_cols(0, i), NT)

            @pl.when(i == 0)
            def _():
                out[...] = part

            @pl.when(i > 0)
            def _():
                out[...] += part

            return carry

        lax.fori_loop(0, 2 * FFH // FC, body, 0)

    def norm_back_into(x, k, dz, add, outs):
        g = gain(k)

        def body(c):
            dx, dg = norm_back(x[c, :].astype(F32), g, dz[c, :])
            gacc[k : k + 1, :] += dg
            total = dx if add is None else add[c, :].astype(F32) + dx
            for out in outs:
                out[c, :] = total.astype(out.dtype)

        chunks(R, LC, body)

    def grad_block(b, t):
        gd[b] = t.T.astype(BF16).reshape(nz, 2, 2, Dh, 128)

    def summed(parts):
        total = parts[0][...].astype(F32)
        for part in parts[1:]:
            total = total + part[...].astype(F32)
        return total.astype(BF16)

    until("early")
    mt = block(MISC)
    wa[rows.r, :], wa[rows.cr, :], wa[rows.gain, :] = mt[0:16], mt[16:32], mt[32:48]
    wa[rows.kv, :] = block(KV)
    head_rows(rows.q, 0, 4)

    def project(m, slot, x, named):
        norm_to(x, a1.at[m], 0)
        kvs[slot] = mm(wa[rows.kv, :], a1[m], NT).astype(BF16)
        copy = exchange(slot)
        z = mm(wa[rows.self_in, :], a1[m], NT)
        qT[m] = (z[0:QR].astype(BF16).astype(F32) * scale).astype(BF16).reshape(experts, hs, R)
        gates(m, named, z[QR + 2 * hs :])
        return copy

    here, there = s, 1 - s
    mine_copy.wait()
    kv_here = project(here, 0, mine, msk.at[s])
    for copy in tokens_in:
        copy.wait_recv()
    kv_there = project(there, 1, other, omsk)
    for m, slot, copy in ((here, 0, kv_here), (there, 1, kv_there)):
        copy.wait_recv()
        set_keys(m, slot, lens[m, 0:1, 0:1])
        attend(m, (1 - m) * T)
    until("late")
    head_rows(rows.o, 1, 5)
    head_rows(rows.cq, CROSSED, CROSSED + 3)
    head_rows(rows.co, CROSSED + 1, CROSSED + 4)
    wa[rows.ckv, :] = block(CKV)
    for m, x in ((here, mine), (there, other)):
        mid[m] = x[...].astype(F32) + mm(hT[m], wa[rows.o, :], TN)
    norm_to(mid.at[DEC], b2, 3)
    norm_to(mid.at[ENC], fa.at[ENC], 1)
    until("ffn")
    feed(ENC, top.at[ENC])
    top[ENC] += mid[ENC]
    norm_to(top.at[ENC], mem, 2)
    kvs[2] = mm(wa[rows.ckv, :], mem[...], NT).astype(BF16)
    kv_cross = exchange(2)
    z = mm(wa[rows.cross_in, :], b2[...], NT)
    qT[CROSS] = (z[0:QR].astype(BF16).astype(F32) * scale).astype(BF16).reshape(experts, hs, R)
    gates(CROSS, xmsk, z[QR:])
    kv_cross.wait_recv()
    set_keys(CROSS, 2, lens[0, 0:1, 0:1])
    attend(CROSS, None)
    top[DEC] = mid[DEC] + mm(hT[CROSS], wa[rows.co, :], TN)
    norm_to(top.at[DEC], fa.at[DEC], 1)
    feed(DEC, work)
    first = s == 0
    y = (top[DEC] + work[...]).astype(BF16)
    out_rows[s] = jnp.where(first, mem[...], y)
    sent[0] = jnp.where(first, y, mem[...])
    rows_in = push(sent.at[0], out_rows.at[s], to_x)

    ct_copy.wait()
    feed_back(DEC, ct, work)
    norm_back_into(top.at[DEC], 1, work, ct, (top.at[DEC], workb.at[DEC]))
    go = attend_back(CROSS, workb[DEC], rows.co)
    waited_sends()
    kvs[0] = dkv[:, R:T].astype(BF16)
    back_cross = exchange(3)
    grad_block(CROSSED + 1, go[0:128])
    grad_block(CROSSED + 4, go[128:256])
    t = mm(dT[CROSS, 0 : QR + 16, :], b2[...])
    grad_block(CROSSED, t[0:128])
    grad_block(CROSSED + 3, t[128:256])
    gaT[16:32, :] = t[QR : QR + 16]
    work[...] = mm(dT[CROSS, 0 : QR + 16, :], wa[rows.cross_in, :], TN)
    norm_back_into(mid.at[DEC], 3, work, top.at[DEC], (top.at[DEC], workb.at[DEC]))
    back_cross.wait_recv()
    dkvc = (dkv[:, 0:R] + kvr[3].astype(F32)).astype(BF16)
    grad_block(CKV, mm(dkvc, mem[...]))

    def reduce_small(base, nb, n, k):
        st = {}

        def p1():
            st["c"] = push(
                gd.at[base : base + nb, :, 1 - core], sc.at[k, 0:nb], to_c
            )

        def p2():
            st["c"].wait_recv()
            own = gd.at[base : base + nb, :, core]
            own[...] = summed([own, sc.at[k, 0:nb]])
            st["x"] = push(gd.at[base : base + nb, :, core, 1 - s], sx.at[k, 0:nb], to_x)

        def p3():
            st["x"].wait_recv()
            own = gd.at[base : base + nb, :, core, s]
            own[...] = summed([own, sx.at[k, 0:nb]])
            st["y"] = push(
                gd.at[pl.ds(base + 2 * (1 - half), n), :, core, s], sy.at[k, 0:n], to_y
            )

        def p4():
            st["y"].wait_recv()
            sg[k, 0:n] = summed(
                [gd.at[pl.ds(base + 2 * half, n), :, core, s], sy.at[k, 0:n]]
            )
            st["z"] = [
                push(sg.at[k, 0:n, (zv + j) % nz], sz.at[k, j - 1, 0:n], to_z[j - 1])
                for j in range(1, nz)
            ]

        def p5():
            for copy in st["z"]:
                copy.wait_recv()
            sfin[k, 0:n, s] = summed(
                [sg.at[k, 0:n, zv]]
                + [sz.at[k, j, 0:n] for j in range(nz - 1)]
            )
            part = sfin.at[k, 0:n, s]
            st["f"] = push(part, part, to_x)

        def p6():
            st["f"].wait_recv()

        return [("small", p) for p in (p1, p2, p3, p4, p5, p6)]

    def reduce_ffn(i):
        cols = slice(i * CW, (i + 1) * CW)
        st = {}

        def p1():
            st["c"] = push(ffn.at[:, :, :, 1 - core, :, :, cols], rc.at[i], to_c)

        def p2():
            st["c"].wait_recv()
            own = ffn.at[:, :, :, core, :, :, cols]
            own[...] = summed([own, rc.at[i]])
            st["x"] = push(ffn.at[0, :, :, core, 1 - s, :, cols], rx.at[i], to_x)
            st["y"] = push(ffn.at[1, 1 - half, :, core, :, :, cols], ry.at[i], to_y)

        def p3():
            st["x"].wait_recv()
            own = ffn.at[0, :, :, core, s, :, cols]
            own[...] = summed([own, rx.at[i]])
            st["y2"] = push(ffn.at[0, 1 - half, :, core, s, :, cols], ry2.at[i], to_y)
            st["y"].wait_recv()
            own = ffn.at[1, half, :, core, :, :, cols]
            own[...] = summed([own, ry.at[i]])
            st["x2"] = push(ffn.at[1, half, :, core, 1 - s, :, cols], rx2.at[i], to_x)

        def p4():
            st["y2"].wait_recv()
            own = ffn.at[0, half, :, core, s, :, cols]
            own[...] = summed([own, ry2.at[i]])
            st["x2"].wait_recv()
            own = ffn.at[1, half, :, core, s, :, cols]
            own[...] = summed([own, rx2.at[i]])
            st["z"] = [
                push(
                    ffn.at[:, half, (zv + j) % nz, core, s, :, cols],
                    rz.at[i, j - 1], to_z[j - 1],
                )
                for j in range(1, nz)
            ]

        def p5():
            for copy in st["z"]:
                copy.wait_recv()
            part = fin.at[:, s, :, cols]
            part[...] = summed(
                [ffn.at[:, half, zv, core, s, :, cols]] + [rz.at[i, j] for j in range(nz - 1)]
            )
            st["f"] = push(part, part, to_x)

        def p6():
            st["f"].wait_recv()

        return [("ffn", p) for p in (p1, p2, p3, p4, p5, p6)]

    cross_sum = reduce_small(CROSSED, 5, 3, 1)
    cross_sum.pop(0)[1]()
    work[...] = mm(dkvc, wa[rows.ckv, :], TN).astype(BF16).astype(F32)
    norm_back_into(top.at[ENC], 2, work, None, (top.at[ENC], workb.at[ENC]))
    cross_sum.pop(0)[1]()
    feed_back(ENC, workb.at[ENC], work)
    cross_sum.pop(0)[1]()

    waited_sends()
    waves = []
    for i in range(NC):
        for hh in (0, 1):
            at = hh * FFH + i * CW
            cols, to = slice(at, at + CW), slice(i * CW, (i + 1) * CW)
            shape = (nz, 2, 2, Dh, CW)
            up = mm(fa[ENC], gp[ENC, :, cols], TN) + mm(fa[DEC], gp[DEC, :, cols], TN)
            ffn[0, hh, :, :, :, :, to] = up.astype(BF16).reshape(shape)
            down = mm(workb[ENC], act[ENC, :, cols], TN) + mm(ct[...], act[DEC, :, cols], TN)
            ffn[1, hh, :, :, :, :, to] = down.astype(BF16).reshape(shape)
        wave = reduce_ffn(i)
        wave.pop(0)[1]()
        waves.append(wave)
    for step in range(NC + 5):
        for i in range(NC):
            if 0 <= step - i < 5:
                queue.append(waves[i][step - i])
        if cross_sum:
            queue.append(cross_sum.pop(0))
    norm_back_into(mid.at[ENC], 1, work, top.at[ENC], (top.at[ENC], workb.at[ENC]))

    def self_back(m, slot):
        go = attend_back(m, workb[m], rows.o, 2)
        kvs[slot % 3] = dkv[:, R:T].astype(BF16)
        return go, exchange(slot)

    def finish(m, slot, copy, x, out):
        copy.wait_recv()
        at = QR + 16
        dT[m, at : at + 2 * hs, :] = (dkv[:, 0:R] + kvr[slot].astype(F32)).astype(BF16)
        work[...] = sum(
            mm(dT[m, at : at + part.stop - part.start, :], wa[part, :], TN)
            for part, at in ((rows.q, 0), (rows.r, QR), (rows.kv, QR + 16))
        )
        norm_back_into(x, 0, work, top.at[m], (out,))

    go, copy = self_back(there, 4)
    mid[DEC, 0:QR, :] = go
    pump(1)
    finish(there, 4, copy, other, sent.at[1])
    grads_in = push(sent.at[1], came, to_x)
    go, copy = self_back(here, 5)
    go = go + mid[DEC, 0:QR, :]
    grad_block(1, go[0:128])
    grad_block(5, go[128:256])
    pump(1)
    finish(here, 5, copy, mine, out_grads.at[s])
    t = mm(dT[ENC, :, :], a1[ENC]) + mm(dT[DEC, :, :], a1[DEC])
    grad_block(0, t[0:128])
    grad_block(4, t[128:256])
    grad_block(KV, t[QR + 16 :])
    grad_block(
        MISC,
        jnp.concatenate(
            [t[QR : QR + 16], gaT[16:32, :], gacc[...], jnp.zeros((80, W), F32)], 0
        ),
    )
    queue += reduce_small(SELF, 6, 4, 0)
    pump(len(queue))
    grads_in.wait_recv()
    out_grads[1 - s] = came[...].astype(F32)
    rows_in.wait_recv()
    for to, k, b in (
        (0, 0, 2 * half), (1, 0, 2 * half + 1), (2, 0, 2 - 2 * half), (3, 0, 3 - 2 * half),
        (4, 1, half), (5, 1, half + 1), (6, 1, 2 - 2 * half),
    ):
        g_small[to] = sfin[k, b].reshape(2 * Dh, 128)
    waited_sends()


def run_layers(experts, hs, nz, zs, tok, msk, xmsk, lens, ct, wsh, fsh):
    _, R, W = tok.shape
    Dh, FFH = fsh.shape[2:]
    T, QR, NC = 2 * R, experts * hs, 4
    CW = FFH // NC
    vm = pltpu.VMEM
    dma = pltpu.SemaphoreType.DMA
    any_, whole = pl.BlockSpec(memory_space=pl.ANY), pl.BlockSpec(memory_space=vm)
    return pl.pallas_call(
        functools.partial(layer_kernel, experts, hs, zs),
        out_shape=(
            jax.ShapeDtypeStruct((2, R, W), BF16),
            jax.ShapeDtypeStruct((2, R, W), F32),
            jax.ShapeDtypeStruct((7, 2 * Dh, 128), BF16),
            jax.ShapeDtypeStruct((2, 2, Dh, FFH), BF16),
        ),
        in_specs=[any_] + [whole] * 3 + [any_] + [whole] * 2,
        out_specs=[whole] * 4,
        scratch_shapes=[
            vm((R, W), BF16),
            vm((R, W), BF16),
            vm((16, R), BF16),
            vm((R, W), BF16),
            vm((BLOCKS, nz, 2, 2, Dh, 128), BF16),
            vm((Rows(QR, hs).total, W), BF16),
            vm((2, 2, nz, 2, 2, Dh, FFH), BF16),
            vm((2, R, W), BF16),
            vm((3, experts, hs, R), BF16),
            vm((3, 128, T), BF16),
            vm((3, 128, T), BF16),
            vm((3, T, 128), BF16),
            vm((3, T, 128), BF16),
            vm((128, R), BF16),
            vm((128, R), BF16),
            vm((3, 2 * experts, R), F32),
            vm((3, experts, T, R), BF16),
            vm((3, experts, hs, R), F32),
            vm((3, 8, R), F32),
            vm((3, QR, R), BF16),
            vm((3, QR + 16 + 2 * hs, R), BF16),
            vm((2 * hs, T), F32),
            vm((2, R, W), F32),
            vm((2, R, W), F32),
            vm((2, R, W), BF16),
            vm((R, W), BF16),
            vm((R, W), BF16),
            vm((2, R, 2 * FFH), BF16),
            vm((2, R, 2 * FFH), BF16),
            vm((R, W), F32),
            vm((2, R, W), BF16),
            vm((16, W), F32),
            vm((32, W), F32),
            vm((BLOCKS, nz, 2, 2, Dh, 128), BF16),
            vm((3, 2 * hs, R), BF16),
            vm((6, 2 * hs, R), BF16),
            vm((2, R, W), BF16),
            vm((R, W), BF16),
            vm((NC, 2, 2, nz, 2, Dh, CW), BF16),
            vm((NC, 2, nz, Dh, CW), BF16),
            vm((NC, nz, 2, Dh, CW), BF16),
            vm((NC, nz, Dh, CW), BF16),
            vm((NC, nz, Dh, CW), BF16),
            vm((NC, max(nz - 1, 1), 2, Dh, CW), BF16),
            vm((2, 6, nz, 2, Dh, 128), BF16),
            vm((2, 6, nz, Dh, 128), BF16),
            vm((2, 4, nz, Dh, 128), BF16),
            vm((2, 4, nz, Dh, 128), BF16),
            vm((2, max(nz - 1, 1), 4, Dh, 128), BF16),
            vm((2, 4, 2, Dh, 128), BF16),
            dma((160,)),
            dma((160,)),
            dma((2,)),
        ],
        compiler_params=pltpu.CompilerParams(
            collective_id=0, has_side_effects=True, vmem_limit_bytes=63 * 2**20
        ),
    )(tok, msk, xmsk, lens, ct, wsh, fsh)


def on_device(
    tokens, self_routes, cross_routes, lengths, cotangent,
    norm_attn, norm_ffn, norm_final, norm_cross,
    router, query_weight, key_weight, value_weight, output_weight, up_weight, down_weight,
    cross_router, cross_query, cross_key, cross_value, cross_output,
):
    section, half = lax.axis_index("section"), lax.axis_index("head")
    dp = lax.axis_size("dp")
    R, W = tokens.shape[2:]
    el, D, hs = query_weight.shape
    experts = el * lax.axis_size("head")
    FFH = up_weight.shape[1]
    nz = min(4, dp // 2)
    zs = dp // nz
    Dv = W // (2 * nz)

    def named(routes):
        ids = jnp.arange(16, dtype=jnp.int32)[:, None]
        first, second = routes[..., None, :, 0], routes[..., None, :, 1]
        return ((first == ids) | (second == ids)).astype(BF16)

    def mine(a):
        return lax.dynamic_slice_in_dim(a, half * R, R, 1)

    msk = named(mine(self_routes[0]))
    xmsk = named(lax.dynamic_index_in_dim(mine(cross_routes), section, 0, keepdims=False))
    lens = jnp.broadcast_to(lengths[:, section].astype(F32)[:, :, None], (2, 8, 128))

    def by_rows(w):
        return jnp.swapaxes(w, 0, 1).reshape(D, el * hs)

    def out_rows(w):
        return w.reshape(el * hs, D).T

    def pad(w, n):
        return jnp.pad(w, ((0, 0), (0, n - w.shape[1])))

    gains = jnp.stack([norm_attn, norm_ffn, norm_final, norm_cross], 1)
    wsh = jnp.stack(
        [
            jnp.concatenate([key_weight, value_weight], 1),
            jnp.concatenate([pad(router, 16), pad(cross_router, 16), pad(gains, 96)], 1),
            by_rows(query_weight), out_rows(output_weight),
            jnp.concatenate([cross_key, cross_value], 1),
            by_rows(cross_query), out_rows(cross_output),
        ]
    )
    fsh = jnp.stack([up_weight, down_weight.T])
    blocks = [[z * zs + j for j in range(zs)] for z in range(nz)]
    core = lax.axis_index("dp") % 2
    if zs > 2:

        def widened(a):
            a = lax.all_gather(a, "dp", axis=1, tiled=True, axis_index_groups=blocks)
            return lax.dynamic_slice_in_dim(a, core * Dv, Dv, 1)

        wsh, fsh = widened(wsh), widened(fsh)

    out, grads, small, ffn = run_layers(
        experts, hs, nz, zs, tokens[0], msk, xmsk, lens, cotangent,
        wsh.reshape(7, 2, Dv // 2, 128), fsh.reshape(2, 2, Dv // 2, FFH),
    )
    ffn = ffn.reshape(2, Dv, FFH)
    if zs > 2:

        def narrowed(a):
            wide = jnp.zeros((a.shape[0], 2 * Dv, a.shape[2]), BF16)
            wide = lax.dynamic_update_slice_in_dim(wide, a, core * Dv, 1)
            return lax.psum_scatter(
                wide, "dp", scatter_dimension=1, axis_index_groups=blocks, tiled=True
            )

        small, ffn = narrowed(small), narrowed(ffn)
    small, ffn = small.astype(F32), ffn.astype(F32)

    def experts_first(a):
        return jnp.swapaxes(a.reshape(D, el, hs), 0, 1)

    def experts_out(a):
        return a.T.reshape(el, hs, D)

    q, o, kv, misc, cq, co, ckv = (small[k] for k in range(7))
    return (
        out[None], grads[None],
        misc[:, 32], misc[:, 33], misc[:, 34], misc[:, 35],
        misc[:, 0:experts], experts_first(q), kv[:, 0:hs], kv[:, hs:], experts_out(o),
        ffn[0], ffn[1].T,
        misc[:, 16 : 16 + experts], experts_first(cq), ckv[:, 0:hs], ckv[:, hs:], experts_out(co),
    )


def solution(mesh):
    rows = P("section", None, ("dp", "head"), None)
    vector, tall = P("dp"), P("dp", None)
    query, out = P("head", "dp", None), P("head", None, "dp")
    weights = (
        vector, vector, vector, vector,
        tall, query, tall, tall, out, P("dp", "head"), P("head", "dp"),
        tall, query, tall, tall, out,
    )
    return jax.shard_map(
        on_device,
        mesh=mesh,
        in_specs=(
            rows, P("section", None, "dp", None), P(None, "dp", None), P(None, None, "dp"),
            P(None, ("dp", "head"), None), *weights,
        ),
        out_specs=(rows, rows, *weights),
        check_vma=False,
    )
```

```python
import functools
import math

import jax
import jax.numpy as jnp
from jax import lax
from jax.experimental import pallas as pl
from jax.experimental.pallas import tpu as pltpu
from jax.sharding import PartitionSpec as P

EPSILON = 1e-05
FAR = -1e30
F32 = jnp.float32
BF16 = jnp.bfloat16
MESH = pl.DeviceIdType.MESH
NN = (((1,), (0,)), ((), ()))
NT = (((1,), (1,)), ((), ()))
TN = (((0,), (0,)), ((), ()))


def mm(a, b, dims=NN):
    return lax.dot_general(a, b, dims, preferred_element_type=F32)


def chunks(total, size, body):
    def step(i, carry):
        body(pl.ds(pl.multiple_of(i * size, size), size))
        return carry

    lax.fori_loop(0, total // size, step, 0)


def norm_parts(x):
    centred = x - jnp.mean(x, -1, keepdims=True)
    rstd = lax.rsqrt(jnp.mean(centred * centred, -1, keepdims=True) + EPSILON)
    return centred * rstd, rstd


def norm_back(x, gain, dz):
    xhat, rstd = norm_parts(x)
    dxh = dz * gain
    dx = (
        dxh
        - jnp.mean(dxh, -1, keepdims=True)
        - xhat * jnp.mean(dxh * xhat, -1, keepdims=True)
    ) * rstd
    return dx, jnp.sum(dz * xhat, 0, keepdims=True)


class Rows:
    def __init__(self, q, h):
        at = 0
        for name, size in (
            ("q", q), ("kv", 2 * h), ("r", 16), ("o", q),
            ("cq", q), ("cr", 16), ("ckv", 2 * h), ("co", q), ("gain", 16),
        ):
            setattr(self, name, slice(at, at + size))
            at += size
        self.total = at
        self.self_in = slice(self.q.start, self.r.stop)
        self.cross_in = slice(self.cq.start, self.cr.stop)


SELF, SHARED, CROSSED, BLOCKS = 0, 4, 6, 11
KV, MISC, CKV = 4, 5, 8


def layer_kernel(
    experts, hs, zs,
    tok, routes, xroutes, lens, ct_hbm,
    g0, g1, g2, g3, wr, wq, wk, wv, wo, wup, wdown, wcr, wcq, wck, wcv, wco,
    out_rows, out_grads, g_small, fin,
    mine, other, msk, omsk, ct, wd, wa, ffn, a1, qT, kT, vT, kA, vA, qA, dA, gate, prob, attT, rl,
    hT, dT, dkv, dkv_own, mid, top, fa, b2, mem, act, gp, work, workb, gacc, gaT, kvs, kvr, sent, came,
    rc, rx, ry, r2, rz, sc, sxy, sg, sz, ssem, rsem, csem,
):
    R, W = mine.shape
    T = 2 * R
    FFH = ffn.shape[-1]
    nz, Dh = ffn.shape[2], ffn.shape[5]
    Dv = 2 * Dh
    QR = experts * hs
    rows = Rows(QR, hs)
    LC, FC = 128, 512
    NC = rc.shape[0]
    CW = FFH // NC
    ENC, DEC, CROSS = 0, 1, 2
    scale = 1.0 / math.sqrt(hs)

    s, d, half = lax.axis_index("section"), lax.axis_index("dp"), lax.axis_index("head")
    zv, core = d // zs, d % 2
    to_x, to_y = {"section": 1 - s}, {"head": 1 - half}
    to_xy = {"section": 1 - s, "head": 1 - half}
    to_c = {"dp": d + 1 - 2 * core}
    dz = [(zv + k) % nz * zs + d % zs for k in range(1, nz)]
    to_z = [{"dp": k} for k in dz]
    to_xz = [{"section": 1 - s, "dp": k} for k in dz]

    barrier = pltpu.get_barrier_semaphore()
    everyone = [to_x, to_y, to_xy, to_c] + to_z + to_xz
    for peer in everyone:
        pl.semaphore_signal(barrier, inc=1, device_id=peer, device_id_type=MESH)

    mine_copy = pltpu.make_async_copy(tok.at[s], mine, csem.at[1])
    mine_copy.start()
    ct_copy = pltpu.make_async_copy(ct_hbm.at[s], ct, csem.at[0])
    ct_copy.start()

    def named(ref, m):
        two = ref[m, :, pl.ds(pl.multiple_of(half * R, R), R)]
        ids = lax.broadcasted_iota(jnp.int32, (16, R), 0)
        return jnp.where((two[0:1] == ids) | (two[1:2] == ids), 1.0, 0.0)

    for m in (0, 1):
        msk[m] = named(routes, m).astype(BF16)

    def beside(a, b):
        return jnp.concatenate([a.astype(F32), b.astype(F32)], 1).astype(BF16)

    def own_block(b, value):
        wd[b, zv, core] = value.reshape(2, Dh, 128)

    row = lax.broadcasted_iota(jnp.int32, (128, Dv), 0)
    misc = jnp.zeros((128, Dv), F32)
    for ref, at in ((wr, 0), (wcr, 16)):
        for e in range(experts):
            misc = jnp.where(row == at + e, ref[e : e + 1, :].astype(F32), misc)
    for k, ref in enumerate((g0, g1, g2, g3)):
        misc = jnp.where(row == 32 + k, ref[...].astype(F32), misc)
    q_own, q_far = SELF + 2 * half, SELF + 2 * (1 - half)
    c_own, c_far = CROSSED + 3 * half, CROSSED + 3 * (1 - half)
    own_block(KV, beside(wk[...], wv[...]))
    own_block(MISC, misc.T.astype(BF16))
    own_block(q_own, beside(wq[0], wq[1]))

    pl.semaphore_wait(barrier, len(everyone))

    started = []

    def push(src, dst, peer):
        k = len(started)
        copy = pltpu.make_async_remote_copy(
            src_ref=src, dst_ref=dst, send_sem=ssem.at[k], recv_sem=rsem.at[k],
            device_id=peer, device_id_type=MESH,
        )
        copy.start()
        started.append(copy)
        return copy

    def same(part, peer):
        return push(part, part, peer)

    left = []

    def waited_sends():
        for copy in started[len(left) :]:
            copy.wait_send()
            left.append(copy)

    queue = []

    def pump(n=1):
        for _ in range(n):
            if queue:
                queue.pop(0)[1]()

    def until(name):
        while any(k == name for k, _ in queue):
            queue.pop(0)[1]()

    def gather(group, own, far, shared):
        copies = [
            same(wd.at[pl.ds(b, n), zv, core], peer) for peer in to_z for b, n in own + shared
        ]
        over = {}

        def of_core(b, n):
            return wd.at[pl.ds(b, n), :, core]

        def one():
            for copy in copies:
                copy.wait_recv()
            over["y"] = [same(of_core(*b), to_y) for b in own]
            over["c"] = [same(of_core(*b), to_c) for b in own + shared]

        def two():
            for copy in over["y"]:
                copy.wait_recv()
            over["c"] += [same(of_core(*b), to_c) for b in far]

        def three():
            for copy in over["c"]:
                copy.wait_recv()

        return [(group, one), (group, two), (group, three)]

    early = gather("early", [(q_own, 1)], [(q_far, 1)], [(KV, 2)])
    tokens_in = [push(tok.at[1 - s], other, to_x), push(msk.at[1 - s], omsk, to_x)]

    def turned(ref):
        return ref[...].astype(F32).reshape(QR // 2, Dv).T.astype(BF16)

    own_block(q_own + 1, turned(wo))
    own_block(CKV, beside(wck[...], wcv[...]))
    own_block(c_own, beside(wcq[0], wcq[1]))
    own_block(c_own + 1, turned(wco))
    ffn[0, half, zv, core] = wup[...].reshape(2, Dh, FFH)
    ffn[1, half, zv, core] = wdown[...].reshape(2, Dh, FFH)
    xmask = named(xroutes, s)

    NA = 4
    AW = FFH // NA
    ffn_z, ffn_y, ffn_c = {}, {}, {}

    def ffn_part(h, z, j):
        return ffn.at[:, h, z, core, :, :, j * AW : (j + 1) * AW]

    def all_z(h, j):
        return ffn.at[:, h, :, core, :, :, j * AW : (j + 1) * AW]

    def ffn_send(j):
        ffn_z[j] = [same(ffn_part(half, zv, j), peer) for peer in to_z]

    def ffn_on(j):
        def run():
            for copy in ffn_z[j]:
                copy.wait_recv()
            ffn_y[j] = [same(ffn_part(half, k, j), to_y) for k in others]
            ffn_c[j] = [same(all_z(half, j), to_c)]

        return ("on%d" % j, run)

    def ffn_far(j):
        def run():
            if j == 0:
                ffn_own.wait_recv()
            for copy in ffn_y[j]:
                copy.wait_recv()
            ffn_c[j].append(same(all_z(1 - half, j), to_c))

        return ("far%d" % j, run)

    def ffn_end(j, far):
        def run():
            ffn_c[j][far].wait_recv()

        return ("end%d%d" % (j, far), run)

    others = [(zv + k) % nz for k in range(1, nz)]
    ffn_send(0)
    out_weights = gather("o", [(q_own + 1, 1)], [(q_far + 1, 1)], [])
    for j in range(1, NA):
        ffn_send(j)
    cross_weights = gather("cross", [(c_own, 2)], [(c_far, 2)], [(CKV, 1)])
    early[0][1]()
    ffn_own = same(ffn.at[:, half, zv, core], to_y)
    early[1][1]()
    early[2][1]()
    idle = ("idle", lambda: None)
    o1, o2, o3 = out_weights
    c1, c2, c3 = cross_weights
    on = [ffn_on(j) for j in range(NA)]
    far = [ffn_far(j) for j in range(NA)]
    end = [(ffn_end(j, 0), ffn_end(j, 1)) for j in range(NA)]
    queue += [on[0], o1, idle, on[1], idle, far[0], o2, on[2], idle, o3]
    queue += [end[0][0], end[1][0], far[1], end[0][1], end[1][1], on[3]]
    queue += [c1, end[2][0], end[3][0], far[2], far[3], end[2][1], end[3][1], c2, c3]

    def block(b):
        return wd[b].reshape(W, 128).astype(F32).T.astype(BF16)

    def head_rows(part, b0, b1):
        n = (part.stop - part.start) // 2
        wa[part.start : part.start + n, :] = block(b0)
        wa[part.start + n : part.stop, :] = block(b1)

    def exchange(slot):
        return push(kvs.at[slot % 3], kvr.at[slot], to_y)

    def gain(k):
        at = rows.gain.start
        return wa[at : at + 16, :].astype(F32)[k : k + 1, :]

    def norm_to(source, out, k):
        g = gain(k)

        def body(c):
            xhat, _ = norm_parts(source[c, :].astype(F32))
            out[c, :] = (xhat * g).astype(BF16)

        chunks(R, LC, body)

    def gates(m, named, logits):
        named = named[0:experts]
        l = jnp.where(named > 0, logits[0:experts], FAR)
        p = jnp.exp(l - jnp.max(l, 0, keepdims=True)) * named
        gate[m, 0:experts, :] = p / jnp.sum(p, 0, keepdims=True)

    def set_keys(m, slot, length):
        lane = lax.broadcasted_iota(jnp.int32, (1, T), 1)
        pos = jnp.where(lane < R, lane + half * R, lane - R + (1 - half) * R).astype(F32)
        outside = jnp.where(pos < length, 0.0, FAR)
        sub = lax.broadcasted_iota(jnp.int32, (128 - hs, T), 0)
        for to, wide, at, rest in (
            (kT, kA, 0, jnp.where(sub == 0, outside, 0.0)),
            (vT, vA, hs, jnp.where(sub < 2, 1.0, 0.0)),
        ):
            to[m, 0:hs, 0:R] = kvs[slot, at : at + hs, :]
            to[m, 0:hs, R:T] = kvr[slot, at : at + hs, :]
            wide[m] = jnp.concatenate([to[m, 0:hs, :].astype(F32), rest], 0).T.astype(BF16)
        vT[m, hs : hs + 16, :] = jnp.where(sub[0:16] < 2, 1.0, 0.0).astype(BF16)

    sub = lax.broadcasted_iota(jnp.int32, (128 - hs, R), 0)
    qA[hs:128, :] = jnp.where(sub == 0, 1.0, 0.0).astype(BF16)
    dA[hs:128, :] = jnp.zeros((128 - hs, R), BF16)
    gacc[...] = jnp.zeros_like(gacc)

    def over_experts(one, pumps):
        for e in range(experts):
            one(e, 0)
            pump(pumps[e] if isinstance(pumps, tuple) else pumps)

    def attend(m, reach, pumps=1):
        def one(e, carry):
            qA[0:hs, :] = qT[m, e]
            scores = mm(kA[m], qA[...])
            if reach is not None:
                k = lax.broadcasted_iota(jnp.int32, (T, 1), 0)
                k = jnp.where(k < R, k + half * R, k - R + (1 - half) * R)
                q = lax.broadcasted_iota(jnp.int32, (1, R), 1) + half * R + reach
                scores = jnp.where(k <= q, scores, FAR)
            p = jnp.exp(scores - jnp.max(scores, 0, keepdims=True)).astype(BF16)
            prob[m, e] = p
            out = mm(vT[m, 0 : hs + 16, :], p)
            inverse = 1.0 / out[hs : hs + 1, :]
            attended = out[0:hs, :] * inverse
            attT[m, e] = attended.astype(BF16)
            rl[m, e : e + 1, :] = inverse
            hT[m, e * hs : (e + 1) * hs, :] = (gate[m, e : e + 1, :] * attended).astype(BF16)
            return carry

        over_experts(one, pumps)

    def attend_back(m, dout, wo, pumps=1):
        dH = mm(wa[wo, :], dout, NT).astype(BF16)
        go = mm(hT[m], dout)
        work[0:QR, 0:R] = dH.astype(F32)

        def one(e, carry):
            span = slice(e * hs, (e + 1) * hs)
            dh = work[span, 0:R]
            dg = jnp.sum(dh * attT[m, e].astype(F32), 0, keepdims=True)
            g = gate[m, e : e + 1, :]
            inverse = rl[m, e : e + 1, :]
            gate[m, experts + e : experts + e + 1, :] = dg
            da = (dh * (g * inverse)).astype(BF16)
            delta = g * dg * inverse
            high = delta.astype(BF16).astype(F32)
            row = lax.broadcasted_iota(jnp.int32, (16, R), 0)
            dA[0:hs, :] = da
            dA[hs : hs + 16, :] = jnp.where(
                row == 0, -high, jnp.where(row == 1, high - delta, 0.0)
            ).astype(BF16)
            p = prob[m, e]
            ds = (p.astype(F32) * mm(vA[m], dA[...])).astype(BF16)
            dT[m, span, :] = (mm(kT[m, 0:hs, :], ds) * scale).astype(BF16)
            dk, dv = mm(qT[m, e], ds, NT), mm(da, p, NT)
            if e == 0:
                dkv[0:hs, :], dkv[hs : 2 * hs, :] = dk, dv
            else:
                dkv[0:hs, :] += dk
                dkv[hs : 2 * hs, :] += dv
            return carry

        over_experts(one, pumps)
        g = gate[m, 0:experts, :]
        dg = gate[m, experts : 2 * experts, :]
        dl = g * (dg - jnp.sum(g * dg, 0, keepdims=True))
        dT[m, QR : QR + 16, :] = jnp.concatenate(
            [dl, jnp.zeros((16 - experts, R), F32)], 0
        ).astype(BF16)
        return go

    def ffn_cols(mat, i):
        n = FFH // FC
        cols = pl.ds(pl.multiple_of(i % n * FC, FC), FC)
        return ffn[mat, i // n, :, :, :, :, cols].reshape(W, FC)

    def feed(m, out, i, start=None):
        c0 = math.sqrt(2.0 / math.pi)
        cols = pl.ds(pl.multiple_of(i * FC, FC), FC)
        u = mm(fa[m], ffn_cols(0, i))
        u2 = u * u
        t = jnp.tanh(c0 * u * (1.0 + 0.044715 * u2))
        half_up = 0.5 * (1.0 + t)
        a = (u * half_up).astype(BF16)
        act[m, :, cols] = a
        gp[m, :, cols] = (
            half_up + 0.5 * u * (1.0 - t * t) * (c0 * (1.0 + 3 * 0.044715 * u2))
        ).astype(BF16)
        part = mm(a, ffn_cols(1, i), NT)
        if start is None:
            out[...] += part
        else:
            out[...] = start[m] + part

    def feed_back(m, dout, out):
        def body(i, carry):
            cols = pl.ds(pl.multiple_of(i * FC, FC), FC)
            dh = mm(dout[...], ffn_cols(1, i))
            dh = (dh * gp[m, :, cols].astype(F32)).astype(BF16)
            gp[m, :, cols] = dh
            part = mm(dh, ffn_cols(0, i), NT)

            @pl.when(i == 0)
            def _():
                out[...] = part

            @pl.when(i > 0)
            def _():
                out[...] += part

            return carry

        lax.fori_loop(0, 2 * FFH // FC, body, 0)

    def norm_back_into(x, k, dz, add, outs):
        g = gain(k)

        def body(c):
            dx, dg = norm_back(x[c, :].astype(F32), g, dz[c, :])
            gacc[k : k + 1, :] += dg
            total = dx if add is None else add[c, :].astype(F32) + dx
            for out in outs:
                out[c, :] = total.astype(out.dtype)

        chunks(R, LC, body)

    def grad_block(b, t):
        gd[b] = t.T.astype(BF16).reshape(nz, 2, 2, Dh, 128)

    def summed(parts):
        total = parts[0][...].astype(F32)
        for part in parts[1:]:
            total = total + part[...].astype(F32)
        return total.astype(BF16)

    mt = block(MISC)
    wa[rows.r, :], wa[rows.cr, :], wa[rows.gain, :] = mt[0:16], mt[16:32], mt[32:48]
    wa[rows.kv, :] = block(KV)
    head_rows(rows.q, 0, 2)

    def project(m, slot, x, named):
        norm_to(x, a1.at[m], 0)
        kvs[slot] = mm(wa[rows.kv, :], a1[m], NT).astype(BF16)
        copy = exchange(slot)
        z = mm(wa[rows.self_in, :], a1[m], NT)
        qT[m] = (z[0:QR].astype(BF16).astype(F32) * scale).astype(BF16).reshape(experts, hs, R)
        gates(m, named[...].astype(F32), z[QR + 2 * hs :])
        return copy

    here, there = s, 1 - s
    mine_copy.wait()
    kv_here = project(here, 0, mine, msk.at[s])
    pump()
    for copy in tokens_in:
        copy.wait_recv()
    kv_there = project(there, 1, other, omsk)
    pump()
    for m, slot, copy in ((here, 0, kv_here), (there, 1, kv_there)):
        copy.wait_recv()
        set_keys(m, slot, lens[m, s].astype(F32))
        attend(m, (1 - m) * T)
    until("o")
    head_rows(rows.o, 1, 3)
    for m, x in ((here, mine), (there, other)):
        mid[m] = x[...].astype(F32) + mm(hT[m], wa[rows.o, :], TN)
    norm_to(mid.at[ENC], fa.at[ENC], 1)
    n = FFH // FC
    ready = ("end10", "end11", "end30", "end31")
    for k, name in enumerate(ready):
        until(name)
        feed(ENC, top.at[ENC], (half if k % 2 == 0 else 1 - half) * n + k // 2, mid if k == 0 else None)
    until("cross")
    head_rows(rows.cq, CROSSED, CROSSED + 3)
    head_rows(rows.co, CROSSED + 1, CROSSED + 4)
    wa[rows.ckv, :] = block(CKV)
    norm_to(top.at[ENC], mem, 2)
    kvs[2] = mm(wa[rows.ckv, :], mem[...], NT).astype(BF16)
    kv_cross = exchange(2)
    norm_to(mid.at[DEC], b2, 3)
    z = mm(wa[rows.cross_in, :], b2[...], NT)
    qT[CROSS] = (z[0:QR].astype(BF16).astype(F32) * scale).astype(BF16).reshape(experts, hs, R)
    gates(CROSS, xmask, z[QR:])
    kv_cross.wait_recv()
    set_keys(CROSS, 2, lens[0, s].astype(F32))
    attend(CROSS, None)
    top[DEC] = mid[DEC] + mm(hT[CROSS], wa[rows.co, :], TN)
    norm_to(top.at[DEC], fa.at[DEC], 1)
    work[...] = top[DEC]

    def feed_dec(i, carry):
        feed(DEC, work, i)
        return carry

    lax.fori_loop(0, 2 * n, feed_dec, 0)
    first = s == 0
    y = work[...].astype(BF16)
    sent[0] = jnp.where(first, mem[...], y)
    sent[1] = jnp.where(first, y, mem[...])
    rows_copy = pltpu.make_async_copy(sent.at[0], out_rows.at[s], csem.at[1])
    rows_copy.start()
    rows_in = push(sent.at[1], out_rows.at[s], to_x)

    gd = wd
    ct_copy.wait()
    feed_back(DEC, ct, work)
    norm_back_into(top.at[DEC], 1, work, ct, (top.at[DEC], workb.at[DEC]))
    go = attend_back(CROSS, workb[DEC], rows.co)
    waited_sends()
    kvs[0] = dkv[:, R:T].astype(BF16)
    back_cross = exchange(3)
    grad_block(CROSSED + 1, go[0:128])
    grad_block(CROSSED + 4, go[128:256])
    t = mm(dT[CROSS, 0 : QR + 16, :], b2[...])
    grad_block(CROSSED, t[0:128])
    grad_block(CROSSED + 3, t[128:256])
    gaT[16:32, :] = t[QR : QR + 16]
    work[...] = mm(dT[CROSS, 0 : QR + 16, :], wa[rows.cross_in, :], TN)
    norm_back_into(mid.at[DEC], 3, work, top.at[DEC], (top.at[DEC], workb.at[DEC]))
    back_cross.wait_recv()
    dkvc = (dkv[:, 0:R] + kvr[3].astype(F32)).astype(BF16)
    grad_block(CKV, mm(dkvc, mem[...]))

    def reduce_small(base, nb, st, n, at, place):
        mine_at, far_at = base + st * half, base + st * (1 - half)
        spare = slice(at, at + n)
        come = {}

        def p1():
            come["c"] = push(gd.at[base : base + nb, :, 1 - core], sc.at[base : base + nb], to_c)

        def p2():
            come["c"].wait_recv()
            own = gd.at[base : base + nb, :, core]
            own[...] = summed([own, sc.at[base : base + nb]])
            come["p"] = [
                push(gd.at[pl.ds(b, n), :, core, hs_], sxy.at[k, spare], peer)
                for k, (b, hs_, peer) in enumerate(
                    ((mine_at, 1 - s, to_x), (far_at, s, to_y), (far_at, 1 - s, to_xy))
                )
            ]

        def p3():
            for copy in come["p"]:
                copy.wait_recv()
            pair = gd[pl.ds(mine_at, n), :, core, s].astype(F32) + sxy[0, spare].astype(F32)
            far = sxy[1, spare].astype(F32) + sxy[2, spare].astype(F32)
            sg[spare] = (pair + far).astype(BF16)
            come["z"] = [
                push(sg.at[spare, (zv + j) % nz], sz.at[spare, s, j], peer)
                for j, peers in enumerate(zip([None] + to_z, [to_x] + to_xz))
                for peer in peers
                if peer is not None
            ]

        def p4():
            for copy in come["z"]:
                copy.wait_recv()
            sz[spare, s, 0] = sg[spare, zv]
            total = sz[spare, :, 0].astype(F32)
            for j in range(1, nz):
                total = total + sz[spare, :, j].astype(F32)
            for k in range(n):
                g_small[place(k)] = total[k].astype(BF16)

        return [("small", p) for p in (p1, p2, p3, p4)]

    slots = {"x": 0, "y": 0}

    def reduce_ffn(i):
        cols = slice(i * CW, (i + 1) * CW)
        come = {}
        order = ("yx" if i == NC - 2 else "xy", "yx")
        slot = []
        for ways in order:
            slot.append(slots[ways[0]])
            slots[ways[0]] += 1

        def part(mat, h, side):
            return ffn.at[mat, h, :, core, side, :, cols]

        def p1():
            come["c"] = push(ffn.at[:, :, :, 1 - core, :, :, cols], rc.at[i], to_c)

        def p2():
            come["c"].wait_recv()
            own = ffn.at[:, :, :, core, :, :, cols]
            own[...] = summed([own, rc.at[i]])
            for mat, ways in enumerate(order):
                if ways == "xy":
                    given = ffn.at[mat, :, :, core, 1 - s, :, cols]
                    come[mat] = push(given, rx.at[slot[mat]], to_x)
                else:
                    given = ffn.at[mat, 1 - half, :, core, :, :, cols]
                    come[mat] = push(given, ry.at[slot[mat]], to_y)

        def p3():
            for mat, ways in enumerate(order):
                come[mat].wait_recv()
                if ways == "xy":
                    own = ffn.at[mat, :, :, core, s, :, cols]
                    own[...] = summed([own, rx.at[slot[mat]]])
                    given, peer = part(mat, 1 - half, s), to_y
                else:
                    own = ffn.at[mat, half, :, core, :, :, cols]
                    own[...] = summed([own, ry.at[slot[mat]]])
                    given, peer = part(mat, half, 1 - s), to_x
                come[mat] = push(given, r2.at[i, mat], peer)

        def p4():
            for mat in (0, 1):
                come[mat].wait_recv()
                own = part(mat, half, s)
                own[...] = summed([own, r2.at[i, mat]])
            come["z"] = [
                push(
                    ffn.at[:, half, (zv + j) % nz, core, s, :, cols],
                    rz.at[i, j - 1], to_z[j - 1],
                )
                for j in range(1, nz)
            ]

        def p5():
            for copy in come["z"]:
                copy.wait_recv()
            own = fin.at[:, s, :, cols]
            own[...] = summed(
                [ffn.at[:, half, zv, core, s, :, cols]] + [rz.at[i, j] for j in range(nz - 1)]
            )
            come["f"] = same(own, to_x)

        def p6():
            come["f"].wait_recv()

        return [("p%d%d" % (k + 1, i), p) for k, p in enumerate((p1, p2, p3, p4, p5, p6))]

    cross_sum = reduce_small(CROSSED, 5, 2, 3, 4, lambda k: 4 + (k + 2 * half) % 3)
    cross_sum[0][1]()
    work[...] = mm(dkvc, wa[rows.ckv, :], TN).astype(BF16).astype(F32)
    norm_back_into(top.at[ENC], 2, work, None, (top.at[ENC], workb.at[ENC]))
    cross_sum[1][1]()
    feed_back(ENC, workb.at[ENC], work)

    waited_sends()
    waves = []
    for i in range(NC):
        for hh in (0, 1):
            at = hh * FFH + i * CW
            cols, to = slice(at, at + CW), slice(i * CW, (i + 1) * CW)
            shape = (nz, 2, 2, Dh, CW)
            up = mm(fa[ENC], gp[ENC, :, cols], TN) + mm(fa[DEC], gp[DEC, :, cols], TN)
            ffn[0, hh, :, :, :, :, to] = up.astype(BF16).reshape(shape)
            down = mm(workb[ENC], act[ENC, :, cols], TN) + mm(ct[...], act[DEC, :, cols], TN)
            ffn[1, hh, :, :, :, :, to] = down.astype(BF16).reshape(shape)
        waves.append(reduce_ffn(i))
        waves[i][0][1]()
        if i > 0 and i < NC - 1:
            waves[i - 1][1][1]()
    waves[NC - 2][1][1]()
    p2, p3, p4, p5, p6 = ([wave[k] for wave in waves] for k in range(1, 6))
    norm_back_into(mid.at[ENC], 1, work, top.at[ENC], (top.at[ENC], workb.at[ENC]))

    at_r, at_kv = QR, QR + 16
    kv_rows = slice(at_kv, at_kv + 2 * hs)

    def self_back(m, slot, pumps):
        go = attend_back(m, workb[m], rows.o, pumps)
        kvs[slot % 3] = dkv[:, R:T].astype(BF16)
        return go, exchange(slot)

    def inner(m, slot, copy, own):
        copy.wait_recv()
        dT[m, kv_rows, :] = (own + kvr[slot].astype(F32)).astype(BF16)
        work[...] = (
            mm(dT[m, 0:at_r, :], wa[rows.q, :], TN)
            + mm(dT[m, at_r:at_kv, :], wa[rows.r, :], TN)
            + mm(dT[m, kv_rows, :], wa[rows.kv, :], TN)
        )

    def run(*events):
        for _, event in events:
            event()

    queue += [cross_sum[2], p3[0]]
    go, copy_there = self_back(there, 4, (0, 1, 0, 1))
    mid[DEC, 0:QR, :] = go
    dkv_own[...] = dkv[:, 0:R]
    run(p2[NC - 1])
    queue += [p3[1], cross_sum[3], p3[2]]
    go, copy_here = self_back(here, 5, (1, 1, 0, 1))
    go = go + mid[DEC, 0:QR, :]
    grad_block(SELF + 1, go[0:128])
    grad_block(SELF + 3, go[128:256])
    t = mm(dT[ENC, 0:at_kv, :], a1[ENC]) + mm(dT[DEC, 0:at_kv, :], a1[DEC])
    grad_block(SELF, t[0:128])
    grad_block(SELF + 2, t[128:256])
    self_sum = reduce_small(SELF, 4, 2, 2, 0, lambda k: k)
    run(self_sum[0])
    inner(there, 4, copy_there, dkv_own[...])
    run(self_sum[1])
    norm_back_into(other, 0, work, top.at[there], (sent.at[1],))
    halves = [slice(0, R // 2), slice(R // 2, R)]
    grads_in = [push(sent.at[1, halves[0]], came.at[halves[0]], to_x)]
    run(p4[0])
    inner(here, 5, copy_here, dkv[:, 0:R])
    grad_block(KV, mm(dT[ENC, kv_rows, :], a1[ENC]) + mm(dT[DEC, kv_rows, :], a1[DEC]))
    run(p4[1])
    norm_back_into(mine, 0, work, top.at[here], (mid.at[here],))
    grads_copy = pltpu.make_async_copy(mid.at[here], out_grads.at[s], csem.at[0])
    grads_copy.start()
    grad_block(
        MISC, jnp.concatenate([t[at_r:], gaT[16:32, :], gacc[...], jnp.zeros((80, W), F32)], 0)
    )
    shared_sum = reduce_small(SHARED, 2, 0, 2, 2, lambda k: 2 + k)
    run(shared_sum[0], p3[3], shared_sum[1], p4[2], p5[0], p5[1])
    grads_in.append(push(sent.at[1, halves[1]], came.at[halves[1]], to_x))
    run(self_sum[2], p4[3], p5[2], shared_sum[2], p5[3], self_sum[3])
    far_copies = []
    for k, half_rows in enumerate(halves):
        grads_in[k].wait_recv()
        mid[there, half_rows] = came[half_rows].astype(F32)
        far_copies.append(
            pltpu.make_async_copy(
                mid.at[there, half_rows], out_grads.at[1 - s, half_rows], csem.at[2 + k]
            )
        )
        far_copies[k].start()
    run(shared_sum[3], *p6)
    rows_in.wait_recv()
    rows_copy.wait()
    grads_copy.wait()
    for copy in far_copies:
        copy.wait()
    waited_sends()


def outputs_kernel(
    el, hs, experts, small, ffn,
    n0, n1, n2, n3, gr, gq, gk, gv, go, gup, gdown, gcr, gcq, gck, gcv, gco,
):
    q, o, kv, misc, cq, co, ckv = (small[k].astype(F32) for k in range(7))
    for ref, value in ((gq, q), (gcq, cq)):
        for e in range(el):
            ref[e] = value[:, e * hs : (e + 1) * hs]
    for ref, value in ((go, o), (gco, co)):
        ref[...] = value.T.reshape(ref.shape)
    gk[...], gv[...], gck[...], gcv[...] = kv[:, 0:hs], kv[:, hs:], ckv[:, 0:hs], ckv[:, hs:]
    misc = misc.T
    gr[...], gcr[...] = misc[0:experts], misc[16 : 16 + experts]
    for k, ref in enumerate((n0, n1, n2, n3)):
        ref[...] = misc[32 + k : 33 + k, :]
    gup[...] = ffn[0].astype(F32)
    gdown[...] = ffn[1].astype(F32)


def run_layers(experts, hs, nz, zs, tok, routes, xroutes, lens, ct, weights):
    _, R, W = tok.shape
    FFH = weights[9].shape[1]
    Dh = W // (4 * nz)
    T, QR, NC = 2 * R, experts * hs, 4
    CW = FFH // NC
    vm = pltpu.VMEM
    dma = pltpu.SemaphoreType.DMA
    any_, whole = pl.BlockSpec(memory_space=pl.ANY), pl.BlockSpec(memory_space=vm)
    scalars = pl.BlockSpec(memory_space=pltpu.SMEM)
    return pl.pallas_call(
        functools.partial(layer_kernel, experts, hs, zs),
        out_shape=(
            jax.ShapeDtypeStruct((2, R, W), BF16),
            jax.ShapeDtypeStruct((2, R, W), F32),
            jax.ShapeDtypeStruct((7, 2, Dh, 128), BF16),
            jax.ShapeDtypeStruct((2, 2, Dh, FFH), BF16),
        ),
        in_specs=[any_, whole, whole, scalars, any_] + [whole] * len(weights),
        out_specs=[any_, any_, whole, whole],
        scratch_shapes=[
            vm((R, W), BF16),
            vm((R, W), BF16),
            vm((2, 16, R), BF16),
            vm((16, R), BF16),
            vm((R, W), BF16),
            vm((BLOCKS, nz, 2, 2, Dh, 128), BF16),
            vm((Rows(QR, hs).total, W), BF16),
            vm((2, 2, nz, 2, 2, Dh, FFH), BF16),
            vm((2, R, W), BF16),
            vm((3, experts, hs, R), BF16),
            vm((3, hs, T), BF16),
            vm((3, hs + 16, T), BF16),
            vm((3, T, 128), BF16),
            vm((3, T, 128), BF16),
            vm((128, R), BF16),
            vm((128, R), BF16),
            vm((3, 2 * experts, R), F32),
            vm((3, experts, T, R), BF16),
            vm((3, experts, hs, R), BF16),
            vm((3, 8, R), F32),
            vm((3, QR, R), BF16),
            vm((3, QR + 16 + 2 * hs, R), BF16),
            vm((2 * hs, T), F32),
            vm((2 * hs, R), F32),
            vm((2, R, W), F32),
            vm((2, R, W), F32),
            vm((2, R, W), BF16),
            vm((R, W), BF16),
            vm((R, W), BF16),
            vm((2, R, 2 * FFH), BF16),
            vm((2, R, 2 * FFH), BF16),
            vm((R, W), F32),
            vm((2, R, W), BF16),
            vm((16, W), F32),
            vm((32, W), F32),
            vm((3, 2 * hs, R), BF16),
            vm((6, 2 * hs, R), BF16),
            vm((2, R, W), BF16),
            vm((R, W), BF16),
            vm((NC, 2, 2, nz, 2, Dh, CW), BF16),
            vm((NC - 1, 2, nz, Dh, CW), BF16),
            vm((NC + 1, nz, 2, Dh, CW), BF16),
            vm((NC, 2, nz, Dh, CW), BF16),
            vm((NC, max(nz - 1, 1), 2, Dh, CW), BF16),
            vm((BLOCKS, nz, 2, Dh, 128), BF16),
            vm((3, 7, nz, Dh, 128), BF16),
            vm((7, nz, Dh, 128), BF16),
            vm((7, 2, nz, Dh, 128), BF16),
            dma((200,)),
            dma((200,)),
            dma((4,)),
        ],
        compiler_params=pltpu.CompilerParams(
            collective_id=0, has_side_effects=True, vmem_limit_bytes=63 * 2**20
        ),
    )(tok, routes, xroutes, lens, ct, *weights)


def on_device(
    tokens, self_routes, cross_routes, lengths, cotangent,
    norm_attn, norm_ffn, norm_final, norm_cross,
    router, query_weight, key_weight, value_weight, output_weight, up_weight, down_weight,
    cross_router, cross_query, cross_key, cross_value, cross_output,
):
    dp = lax.axis_size("dp")
    R, W = tokens.shape[2:]
    el, D, hs = query_weight.shape
    experts = el * lax.axis_size("head")
    FFH = up_weight.shape[1]
    nz = min(4, dp // 2)
    zs = dp // nz
    Dv = W // (2 * nz)
    blocks = [[z * zs + j for j in range(zs)] for z in range(nz)]
    core = lax.axis_index("dp") % 2

    def widened(a, axis):
        if zs == 2:
            return a
        a = lax.all_gather(a, "dp", axis=axis, tiled=True, axis_index_groups=blocks)
        return lax.dynamic_slice_in_dim(a, core * Dv, Dv, axis)

    def narrowed(a):
        if zs == 2:
            return a
        wide = jnp.zeros((a.shape[0], 2 * Dv, a.shape[2]), BF16)
        wide = lax.dynamic_update_slice_in_dim(wide, a, core * Dv, 1)
        return lax.psum_scatter(
            wide, "dp", scatter_dimension=1, axis_index_groups=blocks, tiled=True
        )

    gains = (norm_attn, norm_ffn, norm_final, norm_cross)
    weights = [widened(g, 0).reshape(1, Dv) for g in gains]
    weights += [
        widened(w, axis)
        for w, axis in (
            (router.T, 1), (query_weight, 1), (key_weight, 0), (value_weight, 0),
            (output_weight, 2), (up_weight, 0), (down_weight.T, 0),
            (cross_router.T, 1), (cross_query, 1), (cross_key, 0), (cross_value, 0),
            (cross_output, 2),
        )
    ]
    out, grads, small, ffn = run_layers(
        experts, hs, nz, zs, tokens[0],
        jnp.swapaxes(self_routes[0], 1, 2), jnp.swapaxes(cross_routes, 1, 2),
        lengths[:, :, 0], cotangent, weights,
    )
    small = narrowed(small.reshape(7, Dv, 128))
    ffn = narrowed(ffn.reshape(2, Dv, FFH))

    def f32(*shape):
        return jax.ShapeDtypeStruct(shape, F32)

    whole = pl.BlockSpec(memory_space=pltpu.VMEM)
    attention = (
        f32(experts, D), f32(el, D, hs), f32(D, hs), f32(D, hs), f32(el, hs, D),
    )
    done = pl.pallas_call(
        functools.partial(outputs_kernel, el, hs, experts),
        out_shape=(*(f32(1, D),) * 4, *attention, *(f32(D, FFH),) * 2, *attention),
        in_specs=[whole] * 2,
        out_specs=[whole] * 16,
    )(small, ffn)
    n0, n1, n2, n3, gr, gq, gk, gv, go, gup, gdown, gcr, gcq, gck, gcv, gco = done
    return (
        out[None], grads[None], *(g.reshape(D) for g in (n0, n1, n2, n3)),
        gr.T, gq, gk, gv, go, gup, gdown.T, gcr.T, gcq, gck, gcv, gco,
    )


def solution(mesh):
    rows = P("section", None, ("dp", "head"), None)
    vector, tall = P("dp"), P("dp", None)
    query, out = P("head", "dp", None), P("head", None, "dp")
    weights = (
        vector, vector, vector, vector,
        tall, query, tall, tall, out, P("dp", "head"), P("head", "dp"),
        tall, query, tall, tall, out,
    )
    return jax.shard_map(
        on_device,
        mesh=mesh,
        in_specs=(
            rows, P("section", None, "dp", None), P(None, "dp", None), P(None, None, "dp"),
            P(None, ("dp", "head"), None), *weights,
        ),
        out_specs=(rows, rows, *weights),
        check_vma=False,
    )
```

```python
import functools
import math

import jax
import jax.numpy as jnp
from jax import lax
from jax.experimental import pallas as pl
from jax.experimental.pallas import tpu as pltpu
from jax.sharding import PartitionSpec as P

EPSILON = 1e-05
FAR = -1e30
F32 = jnp.float32
BF16 = jnp.bfloat16
MESH = pl.DeviceIdType.MESH
NN = (((1,), (0,)), ((), ()))
NT = (((1,), (1,)), ((), ()))
TN = (((0,), (0,)), ((), ()))


def mm(a, b, dims=NN):
    return lax.dot_general(a, b, dims, preferred_element_type=F32)


def chunks(total, size, body):
    def step(i, carry):
        body(pl.ds(pl.multiple_of(i * size, size), size))
        return carry

    lax.fori_loop(0, total // size, step, 0)


def norm_parts(x):
    centred = x - jnp.mean(x, -1, keepdims=True)
    rstd = lax.rsqrt(jnp.mean(centred * centred, -1, keepdims=True) + EPSILON)
    return centred * rstd, rstd


def norm_back(x, gain, dz):
    xhat, rstd = norm_parts(x)
    dxh = dz * gain
    dx = (
        dxh
        - jnp.mean(dxh, -1, keepdims=True)
        - xhat * jnp.mean(dxh * xhat, -1, keepdims=True)
    ) * rstd
    return dx, jnp.sum(dz * xhat, 0, keepdims=True)


class Rows:
    def __init__(self, q, h):
        at = 0
        for name, size in (
            ("q", q), ("kv", 2 * h), ("r", 16), ("o", q),
            ("cq", q), ("cr", 16), ("ckv", 2 * h), ("co", q), ("gain", 16),
        ):
            setattr(self, name, slice(at, at + size))
            at += size
        self.total = at
        self.self_in = slice(self.q.start, self.r.stop)
        self.cross_in = slice(self.cq.start, self.cr.stop)


SELF, SHARED, CROSSED, BLOCKS = 0, 4, 6, 11
KV, MISC, CKV = 4, 5, 8


def layer_kernel(
    experts, hs, zs,
    tok, routes, xroutes, lens, ct_hbm,
    g0, g1, g2, g3, wr, wq, wk, wv, wo, wup, wdown, wcr, wcq, wck, wcv, wco,
    out_rows, out_grads, g_small, g_misc, fin,
    mine, other, msk, omsk, ct, wd, wa, ffn, a1, qT, kT, vT, kA, vA, qA, dA, gate, prob, attT, rl,
    hT, dT, dkv, dkv_own, mid, top, fa, b2, mem, act, gp, work, workb, gacc, gaT, kvs, kvr, sent, came,
    rc, rx, ry, r2, rz, zx, ms, mz, sc, sxy, sg, sz, ssem, rsem, csem,
):
    R, W = mine.shape
    T = 2 * R
    FFH = ffn.shape[-1]
    nz, Dh = ffn.shape[2], ffn.shape[5]
    Dv = 2 * Dh
    QR = experts * hs
    rows = Rows(QR, hs)
    LC, FC = 256, 512
    NC = rc.shape[0]
    CW = FFH // NC
    ENC, DEC, CROSS = 0, 1, 2
    scale = 1.0 / math.sqrt(hs)

    s, d, half = lax.axis_index("section"), lax.axis_index("dp"), lax.axis_index("head")
    zv, core = d // zs, d % 2
    to_x, to_y = {"section": 1 - s}, {"head": 1 - half}
    to_xy = {"section": 1 - s, "head": 1 - half}
    to_c = {"dp": d + 1 - 2 * core}
    dz = [(zv + k) % nz * zs + d % zs for k in range(1, nz)]
    to_z = [{"dp": k} for k in dz]
    to_xz = [{"section": 1 - s, "dp": k} for k in dz]

    barrier = pltpu.get_barrier_semaphore()
    everyone = [to_x, to_y, to_xy, to_c] + to_z + to_xz
    for peer in everyone:
        pl.semaphore_signal(barrier, inc=1, device_id=peer, device_id_type=MESH)

    mine_copy = pltpu.make_async_copy(tok.at[s], mine, csem.at[1])
    mine_copy.start()
    ct_copy = pltpu.make_async_copy(ct_hbm.at[s], ct, csem.at[0])
    ct_copy.start()

    def named(ref, m):
        two = ref[m, :, pl.ds(pl.multiple_of(half * R, R), R)]
        ids = lax.broadcasted_iota(jnp.int32, (16, R), 0)
        return jnp.where((two[0:1] == ids) | (two[1:2] == ids), 1.0, 0.0)

    for m in (0, 1):
        msk[m] = named(routes, m).astype(BF16)

    def beside(a, b):
        return jnp.concatenate([a.astype(F32), b.astype(F32)], 1).astype(BF16)

    def own_block(b, value):
        wd[b, zv, core] = value.reshape(2, Dh, 128)

    row = lax.broadcasted_iota(jnp.int32, (128, Dv), 0)
    misc = jnp.zeros((128, Dv), F32)
    for ref, at in ((wr, 0), (wcr, 16)):
        for e in range(experts):
            misc = jnp.where(row == at + e, ref[e : e + 1, :].astype(F32), misc)
    for k, ref in enumerate((g0, g1, g2, g3)):
        misc = jnp.where(row == 32 + k, ref[...].astype(F32), misc)
    q_own, q_far = SELF + 2 * half, SELF + 2 * (1 - half)
    c_own, c_far = CROSSED + 3 * half, CROSSED + 3 * (1 - half)
    own_block(KV, beside(wk[...], wv[...]))
    own_block(MISC, misc.T.astype(BF16))
    own_block(q_own, beside(wq[0], wq[1]))

    pl.semaphore_wait(barrier, len(everyone))

    started = []

    def push(src, dst, peer):
        k = len(started)
        copy = pltpu.make_async_remote_copy(
            src_ref=src, dst_ref=dst, send_sem=ssem.at[k], recv_sem=rsem.at[k],
            device_id=peer, device_id_type=MESH,
        )
        copy.start()
        started.append(copy)
        return copy

    def same(part, peer):
        return push(part, part, peer)

    left = []

    def sent_off(copies):
        for copy in copies:
            if not any(copy is c for c in left):
                copy.wait_send()
                left.append(copy)

    queue = []

    def pump(n=1):
        for _ in range(n):
            if queue:
                queue.pop(0)[1]()

    def until(name):
        while any(k == name for k, _ in queue):
            queue.pop(0)[1]()

    def gather(group, own, far, shared):
        copies = [
            same(wd.at[pl.ds(b, n), zv, core], peer) for peer in to_z for b, n in own + shared
        ]
        over = {}

        def of_core(b, n):
            return wd.at[pl.ds(b, n), :, core]

        def one():
            for copy in copies:
                copy.wait_recv()
            over["y"] = [same(of_core(*b), to_y) for b in own]
            over["c"] = [same(of_core(*b), to_c) for b in own + shared]

        def two():
            for copy in over["y"]:
                copy.wait_recv()
            over["c"] += [same(of_core(*b), to_c) for b in far]

        def three():
            for copy in over["c"]:
                copy.wait_recv()

        return [(group, one), (group, two), (group, three)]

    early = gather("early", [(q_own, 1)], [(q_far, 1)], [(KV, 2)])
    tokens_in = [push(tok.at[1 - s], other, to_x), push(msk.at[1 - s], omsk, to_x)]

    def turned(ref):
        return ref[...].astype(F32).reshape(QR // 2, Dv).T.astype(BF16)

    own_block(q_own + 1, turned(wo))
    own_block(CKV, beside(wck[...], wcv[...]))
    own_block(c_own, beside(wcq[0], wcq[1]))
    own_block(c_own + 1, turned(wco))
    ffn[0, half, zv, core] = wup[...].reshape(2, Dh, FFH)
    ffn[1, half, zv, core] = wdown[...].reshape(2, Dh, FFH)
    xmask = named(xroutes, s)

    NA = 4
    AW = FFH // NA
    others = [(zv + k) % nz for k in range(1, nz)]
    go_z, go_y, go_x, go_xf = {}, {}, {}, {}
    go_c = {(j, far): [] for j in range(NA) for far in (0, 1)}

    def part(mat, h, z, j):
        return ffn.at[mat, h, z, core, :, :, j * AW : (j + 1) * AW]

    def all_z(mat, h, j):
        return ffn.at[mat, h, :, core, :, :, j * AW : (j + 1) * AW]

    def wait_all(copies):
        for copy in copies:
            copy.wait_recv()

    def ffn_send(j):
        go_z[j] = [same(part(s, half, zv, j), peer) for peer in to_z]

    def ffn_on(j):
        def run():
            wait_all(go_z[j])
            go_y[j] = [same(part(s, half, k, j), to_y) for k in others]
            go_x[j] = [same(part(s, half, k, j), to_x) for k in others]
            go_c[j, 0].append(same(all_z(s, half, j), to_c))

        return ("on%d" % j, run)

    def ffn_swap(j):
        def run():
            wait_all(go_x[j])
            go_c[j, 0].append(same(all_z(1 - s, half, j), to_c))

        return ("swap%d" % j, run)

    def ffn_far(j):
        def run():
            if j == 0:
                ffn_own.wait_recv()
            wait_all(go_y[j])
            go_xf[j] = [same(all_z(s, 1 - half, j), to_x)]
            go_c[j, 1].append(same(all_z(s, 1 - half, j), to_c))

        return ("far%d" % j, run)

    def ffn_far_swap(j):
        def run():
            wait_all(go_xf[j])
            go_c[j, 1].append(same(all_z(1 - s, 1 - half, j), to_c))

        return ("farswap%d" % j, run)

    def ffn_end(j, far):
        return ("end%d%d" % (j, far), lambda: wait_all(go_c[j, far]))

    ffn_send(0)
    out_weights = gather("o", [(q_own + 1, 1)], [(q_far + 1, 1)], [])
    for j in range(1, NA):
        ffn_send(j)
    cross_weights = gather("cross", [(c_own, 2)], [(c_far, 2)], [(CKV, 1)])
    early[0][1]()
    ffn_own = same(ffn.at[s, half, zv, core], to_y)
    early[1][1]()
    early[2][1]()
    o1, o2, o3 = out_weights
    c1, c2, c3 = cross_weights
    on, swap, far, far_swap = (
        [make(j) for j in range(NA)] for make in (ffn_on, ffn_swap, ffn_far, ffn_far_swap)
    )
    end = [(ffn_end(j, 0), ffn_end(j, 1)) for j in range(NA)]
    queue += [on[0], o1, on[1], on[2], swap[0], o2, far[0], on[3], swap[1], o3, far[1]]
    queue += [c1, end[0][0], end[1][0]]
    queue += [swap[2], swap[3], far[2], end[2][0], end[3][0]]
    queue += [far_swap[0], far_swap[1], far[3], end[0][1], end[1][1]]
    queue += [c2, far_swap[2], far_swap[3], end[2][1], end[3][1], c3]

    def block(b):
        return wd[b].reshape(W, 128).astype(F32).T.astype(BF16)

    def head_rows(part, b0, b1):
        n = (part.stop - part.start) // 2
        wa[part.start : part.start + n, :] = block(b0)
        wa[part.start + n : part.stop, :] = block(b1)

    def exchange(slot):
        return push(kvs.at[slot % 3], kvr.at[slot], to_y)

    def gain(k):
        at = rows.gain.start
        return wa[at : at + 16, :].astype(F32)[k : k + 1, :]

    def norm_to(source, out, k):
        g = gain(k)

        def body(c):
            xhat, _ = norm_parts(source[c, :].astype(F32))
            out[c, :] = (xhat * g).astype(BF16)

        chunks(R, LC, body)

    def gates(m, named, logits):
        named = named[0:experts]
        l = jnp.where(named > 0, logits[0:experts], FAR)
        p = jnp.exp(l - jnp.max(l, 0, keepdims=True)) * named
        gate[m, 0:experts, :] = p / jnp.sum(p, 0, keepdims=True)

    def set_keys(m, slot, length):
        lane = lax.broadcasted_iota(jnp.int32, (1, T), 1)
        pos = jnp.where(lane < R, lane + half * R, lane - R + (1 - half) * R).astype(F32)
        outside = jnp.where(pos < length, 0.0, FAR)
        sub = lax.broadcasted_iota(jnp.int32, (128 - hs, T), 0)
        for to, wide, at, rest in (
            (kT, kA, 0, jnp.where(sub == 0, outside, 0.0)),
            (vT, vA, hs, jnp.where(sub < 2, 1.0, 0.0)),
        ):
            to[m, 0:hs, 0:R] = kvs[slot, at : at + hs, :]
            to[m, 0:hs, R:T] = kvr[slot, at : at + hs, :]
            wide[m] = jnp.concatenate([to[m, 0:hs, :].astype(F32), rest], 0).T.astype(BF16)
        vT[m, hs : hs + 16, :] = jnp.where(sub[0:16] < 2, 1.0, 0.0).astype(BF16)

    sub = lax.broadcasted_iota(jnp.int32, (128 - hs, R), 0)
    qA[hs:128, :] = jnp.where(sub == 0, 1.0, 0.0).astype(BF16)
    dA[hs:128, :] = jnp.zeros((128 - hs, R), BF16)
    gacc[...] = jnp.zeros_like(gacc)

    def over_experts(one, pumps):
        for e in range(experts):
            one(e, 0)
            pump(pumps[e] if isinstance(pumps, tuple) else pumps)

    def attend(m, reach, pumps=1):
        def one(e, carry):
            qA[0:hs, :] = qT[m, e]
            scores = mm(kA[m], qA[...])
            if reach is not None:
                k = lax.broadcasted_iota(jnp.int32, (T, 1), 0)
                k = jnp.where(k < R, k + half * R, k - R + (1 - half) * R)
                q = lax.broadcasted_iota(jnp.int32, (1, R), 1) + half * R + reach
                scores = jnp.where(k <= q, scores, FAR)
            p = jnp.exp(scores - jnp.max(scores, 0, keepdims=True)).astype(BF16)
            prob[m, e] = p
            out = mm(vT[m, 0 : hs + 16, :], p)
            inverse = 1.0 / out[hs : hs + 1, :]
            attended = out[0:hs, :] * inverse
            attT[m, e] = attended.astype(BF16)
            rl[m, e : e + 1, :] = inverse
            hT[m, e * hs : (e + 1) * hs, :] = (gate[m, e : e + 1, :] * attended).astype(BF16)
            return carry

        over_experts(one, pumps)

    def attend_back(m, dout, wo, pumps=1):
        dH = mm(wa[wo, :], dout, NT).astype(BF16)
        go = mm(hT[m], dout)
        work[0:QR, 0:R] = dH.astype(F32)

        def one(e, carry):
            span = slice(e * hs, (e + 1) * hs)
            dh = work[span, 0:R]
            dg = jnp.sum(dh * attT[m, e].astype(F32), 0, keepdims=True)
            g = gate[m, e : e + 1, :]
            inverse = rl[m, e : e + 1, :]
            gate[m, experts + e : experts + e + 1, :] = dg
            da = (dh * (g * inverse)).astype(BF16)
            delta = g * dg * inverse
            high = delta.astype(BF16).astype(F32)
            row = lax.broadcasted_iota(jnp.int32, (16, R), 0)
            dA[0:hs, :] = da
            dA[hs : hs + 16, :] = jnp.where(
                row == 0, -high, jnp.where(row == 1, high - delta, 0.0)
            ).astype(BF16)
            p = prob[m, e]
            ds = (p.astype(F32) * mm(vA[m], dA[...])).astype(BF16)
            dT[m, span, :] = (mm(kT[m, 0:hs, :], ds) * scale).astype(BF16)
            dk, dv = mm(qT[m, e], ds, NT), mm(da, p, NT)
            if e == 0:
                dkv[0:hs, :], dkv[hs : 2 * hs, :] = dk, dv
            else:
                dkv[0:hs, :] += dk
                dkv[hs : 2 * hs, :] += dv
            return carry

        over_experts(one, pumps)
        g = gate[m, 0:experts, :]
        dg = gate[m, experts : 2 * experts, :]
        dl = g * (dg - jnp.sum(g * dg, 0, keepdims=True))
        dT[m, QR : QR + 16, :] = jnp.concatenate(
            [dl, jnp.zeros((16 - experts, R), F32)], 0
        ).astype(BF16)
        return go

    def ffn_cols(mat, i):
        n = FFH // FC
        cols = pl.ds(pl.multiple_of(i % n * FC, FC), FC)
        return ffn[mat, i // n, :, :, :, :, cols].reshape(W, FC)

    def feed(m, out, i, start=None):
        c0 = math.sqrt(2.0 / math.pi)
        cols = pl.ds(pl.multiple_of(i * FC, FC), FC)
        u = mm(fa[m], ffn_cols(0, i))
        u2 = u * u
        t = jnp.tanh(c0 * u * (1.0 + 0.044715 * u2))
        half_up = 0.5 * (1.0 + t)
        a = (u * half_up).astype(BF16)
        act[m, :, cols] = a
        gp[m, :, cols] = (
            half_up + 0.5 * u * (1.0 - t * t) * (c0 * (1.0 + 3 * 0.044715 * u2))
        ).astype(BF16)
        part = mm(a, ffn_cols(1, i), NT)
        if start is None:
            out[...] += part
        else:
            out[...] = start[m] + part

    def feed_back(m, dout, out):
        def body(i, carry):
            cols = pl.ds(pl.multiple_of(i * FC, FC), FC)
            dh = mm(dout[...], ffn_cols(1, i))
            dh = (dh * gp[m, :, cols].astype(F32)).astype(BF16)
            gp[m, :, cols] = dh
            part = mm(dh, ffn_cols(0, i), NT)

            @pl.when(i == 0)
            def _():
                out[...] = part

            @pl.when(i > 0)
            def _():
                out[...] += part

            return carry

        lax.fori_loop(0, 2 * FFH // FC, body, 0)

    def norm_back_into(x, k, dz, add, outs):
        g = gain(k)

        def body(c):
            dx, dg = norm_back(x[c, :].astype(F32), g, dz[c, :])
            gacc[k : k + 1, :] += dg
            total = dx if add is None else add[c, :].astype(F32) + dx
            for out in outs:
                out[c, :] = total.astype(out.dtype)

        chunks(R, LC, body)

    def grad_block(b, t):
        gd[b] = t.T.astype(BF16).reshape(nz, 2, 2, Dh, 128)

    def summed(parts):
        total = parts[0][...].astype(F32)
        for part in parts[1:]:
            total = total + part[...].astype(F32)
        return total.astype(BF16)

    mt = block(MISC)
    wa[rows.r, :], wa[rows.cr, :], wa[rows.gain, :] = mt[0:16], mt[16:32], mt[32:48]
    wa[rows.kv, :] = block(KV)
    head_rows(rows.q, 0, 2)

    def project(m, slot, x, named):
        norm_to(x, a1.at[m], 0)
        kvs[slot] = mm(wa[rows.kv, :], a1[m], NT).astype(BF16)
        copy = exchange(slot)
        z = mm(wa[rows.self_in, :], a1[m], NT)
        qT[m] = (z[0:QR].astype(BF16).astype(F32) * scale).astype(BF16).reshape(experts, hs, R)
        gates(m, named[...].astype(F32), z[QR + 2 * hs :])
        return copy

    here, there = s, 1 - s
    mine_copy.wait()
    kv_here = project(here, 0, mine, msk.at[s])
    for copy in tokens_in:
        copy.wait_recv()
    kv_there = project(there, 1, other, omsk)
    pump(3)
    for m, slot, copy in ((here, 0, kv_here), (there, 1, kv_there)):
        copy.wait_recv()
        set_keys(m, slot, lens[m, s].astype(F32))
        attend(m, (1 - m) * T)
    until("o")
    head_rows(rows.o, 1, 3)
    for m, x in ((here, mine), (there, other)):
        mid[m] = x[...].astype(F32) + mm(hT[m], wa[rows.o, :], TN)
    norm_to(mid.at[ENC], fa.at[ENC], 1)
    n = FFH // FC
    for k, name in enumerate(("end10", "end30", "end11", "end31")):
        until(name)
        h = half if k < 2 else 1 - half
        feed(ENC, top.at[ENC], h * n + k % 2, mid if k == 0 else None)
    until("cross")
    head_rows(rows.cq, CROSSED, CROSSED + 3)
    head_rows(rows.co, CROSSED + 1, CROSSED + 4)
    wa[rows.ckv, :] = block(CKV)
    weight_copies = list(started)
    norm_to(top.at[ENC], mem, 2)
    kvs[2] = mm(wa[rows.ckv, :], mem[...], NT).astype(BF16)
    kv_cross = exchange(2)
    norm_to(mid.at[DEC], b2, 3)
    z = mm(wa[rows.cross_in, :], b2[...], NT)
    qT[CROSS] = (z[0:QR].astype(BF16).astype(F32) * scale).astype(BF16).reshape(experts, hs, R)
    gates(CROSS, xmask, z[QR:])
    kv_cross.wait_recv()
    set_keys(CROSS, 2, lens[0, s].astype(F32))
    attend(CROSS, None)
    top[DEC] = mid[DEC] + mm(hT[CROSS], wa[rows.co, :], TN)
    norm_to(top.at[DEC], fa.at[DEC], 1)
    work[...] = top[DEC]

    def feed_dec(i, carry):
        feed(DEC, work, i)
        return carry

    lax.fori_loop(0, 2 * n, feed_dec, 0)
    first = s == 0
    y = work[...].astype(BF16)
    sent[0] = jnp.where(first, mem[...], y)
    sent[1] = jnp.where(first, y, mem[...])
    rows_copy = pltpu.make_async_copy(sent.at[0], out_rows.at[s], csem.at[1])
    rows_copy.start()
    rows_in = push(sent.at[1], out_rows.at[s], to_x)

    sent_off(weight_copies)
    gd = wd
    ct_copy.wait()
    feed_back(DEC, ct, work)
    norm_back_into(top.at[DEC], 1, work, ct, (top.at[DEC], workb.at[DEC]))
    go = attend_back(CROSS, workb[DEC], rows.co)
    sent_off((kv_here, kv_there, kv_cross))
    kvs[0] = dkv[:, R:T].astype(BF16)
    back_cross = exchange(3)
    grad_block(CROSSED + 1, go[0:128])
    grad_block(CROSSED + 4, go[128:256])
    t = mm(dT[CROSS, 0 : QR + 16, :], b2[...])
    grad_block(CROSSED, t[0:128])
    grad_block(CROSSED + 3, t[128:256])
    gaT[16:32, :] = t[QR : QR + 16]
    work[...] = mm(dT[CROSS, 0 : QR + 16, :], wa[rows.cross_in, :], TN)
    norm_back_into(mid.at[DEC], 3, work, top.at[DEC], (top.at[DEC], workb.at[DEC]))
    back_cross.wait_recv()
    dkvc = (dkv[:, 0:R] + kvr[3].astype(F32)).astype(BF16)
    grad_block(CKV, mm(dkvc, mem[...]))

    def reduce_small(base, nb, st, n, at, place):
        mine_at, far_at = base + st * half, base + st * (1 - half)
        spare = slice(at, at + n)
        come = {}

        def p1():
            come["c"] = push(gd.at[base : base + nb, :, 1 - core], sc.at[base : base + nb], to_c)

        def p2():
            come["c"].wait_recv()
            own = gd.at[base : base + nb, :, core]
            own[...] = summed([own, sc.at[base : base + nb]])
            come["p"] = [
                push(gd.at[pl.ds(b, n), :, core, hs_], sxy.at[k, spare], peer)
                for k, (b, hs_, peer) in enumerate(
                    ((mine_at, 1 - s, to_x), (far_at, s, to_y), (far_at, 1 - s, to_xy))
                )
            ]

        def p3():
            for copy in come["p"]:
                copy.wait_recv()
            pair = gd[pl.ds(mine_at, n), :, core, s].astype(F32) + sxy[0, spare].astype(F32)
            far = sxy[1, spare].astype(F32) + sxy[2, spare].astype(F32)
            sg[spare] = (pair + far).astype(BF16)
            come["z"] = [
                push(sg.at[spare, (zv + j) % nz], sz.at[spare, s, j], peer)
                for j, peers in enumerate(zip([None] + to_z, [to_x] + to_xz))
                for peer in peers
                if peer is not None
            ]

        def p4():
            for copy in come["z"]:
                copy.wait_recv()
            sz[spare, s, 0] = sg[spare, zv]
            total = sz[spare, :, 0].astype(F32)
            for j in range(1, nz):
                total = total + sz[spare, :, j].astype(F32)
            for k in range(n):
                g_small[place(k)] = total[k].astype(BF16)

        return [("small", p) for p in (p1, p2, p3, p4)]

    def reduce_ffn(i):
        cols = slice(i * CW, (i + 1) * CW)
        come = {}
        ways = ("yzx" if i == NC - 2 else "xyz", "yzx")

        def p1():
            come["c"] = push(ffn.at[:, :, :, 1 - core, :, :, cols], rc.at[i], to_c)

        def p2():
            come["c"].wait_recv()
            own = ffn.at[:, :, :, core, :, :, cols]
            own[...] = summed([own, rc.at[i]])
            for mat in (0, 1):
                if ways[mat] == "xyz":
                    given = ffn.at[mat, :, :, core, 1 - s, :, cols]
                    come[mat] = push(given, rx.at[min(i, NC - 2)], to_x)
                else:
                    given = ffn.at[mat, 1 - half, :, core, :, :, cols]
                    come[mat] = push(given, ry.at[i if mat else NC], to_y)

        def z_push(mat, side, to):
            return [
                push(ffn.at[mat, half, (zv + j) % nz, core, side, :, cols], to.at[j - 1], to_z[j - 1])
                for j in range(1, nz)
            ]

        def p3():
            for mat in (0, 1):
                come[mat].wait_recv()
                if ways[mat] == "xyz":
                    own = ffn.at[mat, :, :, core, s, :, cols]
                    own[...] = summed([own, rx.at[min(i, NC - 2)]])
                    given = ffn.at[mat, 1 - half, :, core, s, :, cols]
                    come[mat] = [push(given, r2.at[i], to_y)]
                else:
                    own = ffn.at[mat, half, :, core, :, :, cols]
                    own[...] = summed([own, ry.at[i if mat else NC]])
                    come[mat] = z_push(mat, slice(None), rz.at[i, mat])

        def z_sum(mat, side, out):
            out[...] = summed(
                [ffn.at[mat, half, zv, core, side, :, cols]]
                + [rz.at[i, mat, j, side] for j in range(nz - 1)]
            )

        def p4():
            for mat in (0, 1):
                wait_all(come[mat])
                if ways[mat] == "xyz":
                    own = ffn.at[mat, half, :, core, s, :, cols]
                    own[...] = summed([own, r2.at[i]])
                    come[mat] = z_push(mat, s, rz.at[i, mat, :, s])
                else:
                    z_sum(mat, slice(None), zx.at[i, mat, 0])
                    come[mat] = [push(zx.at[i, mat, 0], zx.at[i, mat, 1], to_x)]

        def p5():
            for mat in (0, 1):
                wait_all(come[mat])
                if ways[mat] == "xyz":
                    z_sum(mat, s, fin.at[mat, s, :, cols])
                    come[mat] = [same(fin.at[mat, s, :, cols], to_x)]
                else:
                    fin[mat, :, :, cols] = summed([zx.at[i, mat, 0], zx.at[i, mat, 1]])
                    come[mat] = []

        def p6():
            for mat in (0, 1):
                wait_all(come[mat])

        return [("p%d%d" % (k + 1, i), p) for k, p in enumerate((p1, p2, p3, p4, p5, p6))]

    def reduce_misc():
        come = {}

        def p1():
            come["c"] = push(ms.at[0], ms.at[1], to_c)

        def p2():
            come["c"].wait_recv()
            ms[2] = summed([ms.at[0], ms.at[1]])
            come["p"] = [
                push(ms.at[2], ms.at[3 + k], peer) for k, peer in enumerate((to_x, to_y, to_xy))
            ]

        def p3():
            wait_all(come["p"])
            pair = ms[2].astype(F32) + ms[3].astype(F32)
            far = ms[4].astype(F32) + ms[5].astype(F32)
            mz[zv] = (pair + far).astype(BF16)
            come["z"] = [same(mz.at[zv], peer) for peer in to_z]

        def p4():
            wait_all(come["z"])
            g_misc[...] = summed([mz.at[j] for j in range(nz)])

        return [("misc", p) for p in (p1, p2, p3, p4)]

    cross_sum = reduce_small(CROSSED, 5, 2, 3, 3, lambda k: 3 + (k + 2 * half) % 3)
    cross_sum[0][1]()
    work[...] = mm(dkvc, wa[rows.ckv, :], TN).astype(BF16).astype(F32)
    norm_back_into(top.at[ENC], 2, work, None, (top.at[ENC], workb.at[ENC]))
    cross_sum[1][1]()
    feed_back(ENC, workb.at[ENC], work)

    waves = []
    for i in range(NC):
        for hh in (0, 1):
            at = hh * FFH + i * CW
            cols, to = slice(at, at + CW), slice(i * CW, (i + 1) * CW)
            shape = (nz, 2, 2, Dh, CW)
            up = mm(fa[ENC], gp[ENC, :, cols], TN) + mm(fa[DEC], gp[DEC, :, cols], TN)
            ffn[0, hh, :, :, :, :, to] = up.astype(BF16).reshape(shape)
            down = mm(workb[ENC], act[ENC, :, cols], TN) + mm(ct[...], act[DEC, :, cols], TN)
            ffn[1, hh, :, :, :, :, to] = down.astype(BF16).reshape(shape)
        waves.append(reduce_ffn(i))
        waves[i][0][1]()
        if i > 0 and i < NC - 1:
            waves[i - 1][1][1]()
    waves[NC - 2][1][1]()
    p2, p3, p4, p5, p6 = ([wave[k] for wave in waves] for k in range(1, 6))
    norm_back_into(mid.at[ENC], 1, work, top.at[ENC], (top.at[ENC], workb.at[ENC]))

    at_r, at_kv = QR, QR + 16
    kv_rows = slice(at_kv, at_kv + 2 * hs)

    def self_back(m, slot, pumps):
        go = attend_back(m, workb[m], rows.o, pumps)
        kvs[slot % 3] = dkv[:, R:T].astype(BF16)
        return go, exchange(slot)

    def inner(m, slot, copy, own):
        copy.wait_recv()
        dT[m, kv_rows, :] = (own + kvr[slot].astype(F32)).astype(BF16)
        work[...] = (
            mm(dT[m, 0:at_r, :], wa[rows.q, :], TN)
            + mm(dT[m, at_r:at_kv, :], wa[rows.r, :], TN)
            + mm(dT[m, kv_rows, :], wa[rows.kv, :], TN)
        )

    def run(*events):
        for _, event in events:
            event()

    queue += [cross_sum[2], p3[0]]
    go, copy_there = self_back(there, 4, (0, 1, 0, 1))
    mid[DEC, 0:QR, :] = go
    dkv_own[...] = dkv[:, 0:R]
    run(p2[NC - 1])
    queue += [p3[1], cross_sum[3], p3[2]]
    go, copy_here = self_back(here, 5, (1, 1, 0, 1))
    go = go + mid[DEC, 0:QR, :]
    grad_block(SELF + 1, go[0:128])
    grad_block(SELF + 3, go[128:256])
    t = mm(dT[ENC, 0:at_kv, :], a1[ENC]) + mm(dT[DEC, 0:at_kv, :], a1[DEC])
    grad_block(SELF, t[0:128])
    grad_block(SELF + 2, t[128:256])
    self_sum = reduce_small(SELF, 4, 2, 2, 0, lambda k: k)
    run(self_sum[0])
    inner(there, 4, copy_there, dkv_own[...])
    run(self_sum[1])
    sent_off([rows_in])
    norm_back_into(other, 0, work, top.at[there], (sent.at[1],))
    halves = [slice(0, R // 2), slice(R // 2, R)]
    grads_in = [push(sent.at[1, halves[0]], came.at[halves[0]], to_x)]
    run(p4[0])
    inner(here, 5, copy_here, dkv[:, 0:R])
    grad_block(KV, mm(dT[ENC, kv_rows, :], a1[ENC]) + mm(dT[DEC, kv_rows, :], a1[DEC]))
    kv_sum = reduce_small(KV, 1, 0, 1, 2, lambda k: 2 + k)
    run(kv_sum[0])
    run(p4[1])
    norm_back_into(mine, 0, work, top.at[here], (mid.at[here],))
    grads_copy = pltpu.make_async_copy(mid.at[here], out_grads.at[s], csem.at[0])
    grads_copy.start()
    ms[0] = jnp.concatenate(
        [t[at_r : at_r + 4], gaT[16:20, :], gacc[0:4, :], jnp.zeros((4, W), F32)], 0
    ).astype(BF16)
    misc_sum = reduce_misc()
    run(misc_sum[0], kv_sum[1], misc_sum[1], p3[3], p4[2], p5[0], p5[1])
    grads_in.append(push(sent.at[1, halves[1]], came.at[halves[1]], to_x))
    run(self_sum[2], kv_sum[2], misc_sum[2], p4[3], p5[2], self_sum[3], kv_sum[3], misc_sum[3], p5[3])
    far_copies = []
    for k, half_rows in enumerate(halves):
        grads_in[k].wait_recv()
        mid[there, half_rows] = came[half_rows].astype(F32)
        far_copies.append(
            pltpu.make_async_copy(
                mid.at[there, half_rows], out_grads.at[1 - s, half_rows], csem.at[2 + k]
            )
        )
        far_copies[k].start()
    run(*p6)
    rows_in.wait_recv()
    rows_copy.wait()
    grads_copy.wait()
    for copy in far_copies:
        copy.wait()
    sent_off(started)


def outputs_kernel(
    el, hs, experts, rows_in, grads_in, small_in, misc, ffn_in,
    rows, grads, n0, n1, n2, n3, gr, gq, gk, gv, go, gup, gdown, gcr, gcq, gck, gcv, gco, small, ffn, sem,
):
    copies = [
        pltpu.make_async_copy(rows_in, rows.at[0], sem.at[0]),
        pltpu.make_async_copy(grads_in, grads.at[0], sem.at[1]),
        pltpu.make_async_copy(ffn_in, ffn, sem.at[2]),
        pltpu.make_async_copy(small_in, small, sem.at[3]),
    ]
    for copy in reversed(copies):
        copy.start()
    copies.pop().wait()
    q, o, kv, cq, co, ckv = (small[k].astype(F32) for k in range(6))
    for ref, value in ((gq, q), (gcq, cq)):
        for e in range(el):
            ref[e] = value[:, e * hs : (e + 1) * hs]
    for ref, value in ((go, o), (gco, co)):
        ref[...] = value.T.reshape(ref.shape)
    gk[...], gv[...], gck[...], gcv[...] = kv[:, 0:hs], kv[:, hs:], ckv[:, 0:hs], ckv[:, hs:]
    D, W = n0.shape[1], misc.shape[1]
    feature = lax.broadcasted_iota(jnp.int32, (W, D), 0) - lax.axis_index("dp") * D
    chosen = jnp.where(feature == lax.broadcasted_iota(jnp.int32, (W, D), 1), 1.0, 0.0)
    own = mm(misc[...], chosen.astype(BF16))
    gr[...], gcr[...] = own[0:experts], own[4 : 4 + experts]
    for k, ref in enumerate((n0, n1, n2, n3)):
        ref[...] = own[8 + k : 9 + k, :]
    copies.pop().wait()
    gup[...] = ffn[0].astype(F32)
    gdown[...] = ffn[1].astype(F32)
    for copy in copies:
        copy.wait()


def run_layers(experts, hs, nz, zs, tok, routes, xroutes, lens, ct, weights):
    _, R, W = tok.shape
    FFH = weights[9].shape[1]
    Dh = W // (4 * nz)
    T, QR, NC = 2 * R, experts * hs, 4
    CW = FFH // NC
    vm = pltpu.VMEM
    dma = pltpu.SemaphoreType.DMA
    any_, whole = pl.BlockSpec(memory_space=pl.ANY), pl.BlockSpec(memory_space=vm)
    scalars = pl.BlockSpec(memory_space=pltpu.SMEM)
    return pl.pallas_call(
        functools.partial(layer_kernel, experts, hs, zs),
        out_shape=(
            jax.ShapeDtypeStruct((2, R, W), BF16),
            jax.ShapeDtypeStruct((2, R, W), F32),
            jax.ShapeDtypeStruct((6, 2, Dh, 128), BF16),
            jax.ShapeDtypeStruct((16, W), BF16),
            jax.ShapeDtypeStruct((2, 2, Dh, FFH), BF16),
        ),
        in_specs=[any_, whole, whole, scalars, any_] + [whole] * len(weights),
        out_specs=[any_, any_, whole, whole, whole],
        scratch_shapes=[
            vm((R, W), BF16),
            vm((R, W), BF16),
            vm((2, 16, R), BF16),
            vm((16, R), BF16),
            vm((R, W), BF16),
            vm((BLOCKS, nz, 2, 2, Dh, 128), BF16),
            vm((Rows(QR, hs).total, W), BF16),
            vm((2, 2, nz, 2, 2, Dh, FFH), BF16),
            vm((2, R, W), BF16),
            vm((3, experts, hs, R), BF16),
            vm((3, hs, T), BF16),
            vm((3, hs + 16, T), BF16),
            vm((3, T, 128), BF16),
            vm((3, T, 128), BF16),
            vm((128, R), BF16),
            vm((128, R), BF16),
            vm((3, 2 * experts, R), F32),
            vm((3, experts, T, R), BF16),
            vm((3, experts, hs, R), BF16),
            vm((3, 8, R), F32),
            vm((3, QR, R), BF16),
            vm((3, QR + 16 + 2 * hs, R), BF16),
            vm((2 * hs, T), F32),
            vm((2 * hs, R), F32),
            vm((2, R, W), F32),
            vm((2, R, W), F32),
            vm((2, R, W), BF16),
            vm((R, W), BF16),
            vm((R, W), BF16),
            vm((2, R, 2 * FFH), BF16),
            vm((2, R, 2 * FFH), BF16),
            vm((R, W), F32),
            vm((2, R, W), BF16),
            vm((16, W), F32),
            vm((32, W), F32),
            vm((3, 2 * hs, R), BF16),
            vm((6, 2 * hs, R), BF16),
            vm((2, R, W), BF16),
            vm((R, W), BF16),
            vm((NC, 2, 2, nz, 2, Dh, CW), BF16),
            vm((NC - 1, 2, nz, Dh, CW), BF16),
            vm((NC + 1, nz, 2, Dh, CW), BF16),
            vm((NC, nz, Dh, CW), BF16),
            vm((NC, 2, max(nz - 1, 1), 2, Dh, CW), BF16),
            vm((NC, 2, 2, 2, Dh, CW), BF16),
            vm((6, 16, W), BF16),
            vm((nz, 16, W), BF16),
            vm((BLOCKS, nz, 2, Dh, 128), BF16),
            vm((3, 6, nz, Dh, 128), BF16),
            vm((6, nz, Dh, 128), BF16),
            vm((6, 2, nz, Dh, 128), BF16),
            dma((200,)),
            dma((200,)),
            dma((4,)),
        ],
        compiler_params=pltpu.CompilerParams(
            collective_id=0, has_side_effects=True, vmem_limit_bytes=63 * 2**20
        ),
    )(tok, routes, xroutes, lens, ct, *weights)


def on_device(
    tokens, self_routes, cross_routes, lengths, cotangent,
    norm_attn, norm_ffn, norm_final, norm_cross,
    router, query_weight, key_weight, value_weight, output_weight, up_weight, down_weight,
    cross_router, cross_query, cross_key, cross_value, cross_output,
):
    dp = lax.axis_size("dp")
    R, W = tokens.shape[2:]
    el, D, hs = query_weight.shape
    experts = el * lax.axis_size("head")
    FFH = up_weight.shape[1]
    nz = min(4, dp // 2)
    zs = dp // nz
    Dv = W // (2 * nz)
    blocks = [[z * zs + j for j in range(zs)] for z in range(nz)]
    core = lax.axis_index("dp") % 2

    def widened(a, axis):
        if zs == 2:
            return a
        a = lax.all_gather(a, "dp", axis=axis, tiled=True, axis_index_groups=blocks)
        return lax.dynamic_slice_in_dim(a, core * Dv, Dv, axis)

    def narrowed(a):
        if zs == 2:
            return a
        wide = jnp.zeros((a.shape[0], 2 * Dv, a.shape[2]), BF16)
        wide = lax.dynamic_update_slice_in_dim(wide, a, core * Dv, 1)
        return lax.psum_scatter(
            wide, "dp", scatter_dimension=1, axis_index_groups=blocks, tiled=True
        )

    gains = (norm_attn, norm_ffn, norm_final, norm_cross)
    weights = [widened(g, 0).reshape(1, Dv) for g in gains]
    weights += [
        widened(w, axis)
        for w, axis in (
            (router.T, 1), (query_weight, 1), (key_weight, 0), (value_weight, 0),
            (output_weight, 2), (up_weight, 0), (down_weight.T, 0),
            (cross_router.T, 1), (cross_query, 1), (cross_key, 0), (cross_value, 0),
            (cross_output, 2),
        )
    ]
    out, grads, small, misc, ffn = run_layers(
        experts, hs, nz, zs, tokens[0],
        jnp.swapaxes(self_routes[0], 1, 2), jnp.swapaxes(cross_routes, 1, 2),
        lengths[:, :, 0], cotangent, weights,
    )
    small = narrowed(small.reshape(6, Dv, 128))
    ffn = narrowed(ffn.reshape(2, Dv, FFH))

    def f32(*shape):
        return jax.ShapeDtypeStruct(shape, F32)

    whole = pl.BlockSpec(memory_space=pltpu.VMEM)
    attention = (
        f32(experts, D), f32(el, D, hs), f32(D, hs), f32(D, hs), f32(el, hs, D),
    )
    done = pl.pallas_call(
        functools.partial(outputs_kernel, el, hs, experts),
        out_shape=(
            jax.ShapeDtypeStruct((1, 2, R, W), BF16), f32(1, 2, R, W),
            *(f32(1, D),) * 4, *attention, *(f32(D, FFH),) * 2, *attention,
        ),
        in_specs=[pl.BlockSpec(memory_space=pltpu.HBM)] * 3 + [whole, pl.BlockSpec(memory_space=pltpu.HBM)],
        out_specs=[whole] * 18,
        scratch_shapes=[
            pltpu.VMEM(small.shape, BF16), pltpu.VMEM(ffn.shape, BF16), pltpu.SemaphoreType.DMA((4,)),
        ],
        compiler_params=pltpu.CompilerParams(vmem_limit_bytes=60 * 2**20),
    )(out, grads, small, misc, ffn)
    rows, grads, n0, n1, n2, n3, gr, gq, gk, gv, go, gup, gdown, gcr, gcq, gck, gcv, gco = done
    return (
        rows, grads, *(g.reshape(D) for g in (n0, n1, n2, n3)),
        gr.T, gq, gk, gv, go, gup, gdown.T, gcr.T, gcq, gck, gcv, gco,
    )


def solution(mesh):
    rows = P("section", None, ("dp", "head"), None)
    vector, tall = P("dp"), P("dp", None)
    query, out = P("head", "dp", None), P("head", None, "dp")
    weights = (
        vector, vector, vector, vector,
        tall, query, tall, tall, out, P("dp", "head"), P("head", "dp"),
        tall, query, tall, tall, out,
    )
    return jax.shard_map(
        on_device,
        mesh=mesh,
        in_specs=(
            rows, P("section", None, "dp", None), P(None, "dp", None), P(None, None, "dp"),
            P(None, ("dp", "head"), None), *weights,
        ),
        out_specs=(rows, rows, *weights),
        check_vma=False,
    )
```

```python
import functools
import math

import jax
import jax.numpy as jnp
from jax import lax
from jax.experimental import pallas as pl
from jax.experimental.pallas import tpu as pltpu
from jax.sharding import PartitionSpec as P

EPSILON = 1e-05
FAR = -1e30
F32 = jnp.float32
BF16 = jnp.bfloat16
MESH = pl.DeviceIdType.MESH
NN = (((1,), (0,)), ((), ()))
NT = (((1,), (1,)), ((), ()))
TN = (((0,), (0,)), ((), ()))


def mm(a, b, dims=NN):
    return lax.dot_general(a, b, dims, preferred_element_type=F32)


def chunks(total, size, body):
    def step(i, carry):
        body(pl.ds(pl.multiple_of(i * size, size), size))
        return carry

    lax.fori_loop(0, total // size, step, 0)


def norm_parts(x):
    centred = x - jnp.mean(x, -1, keepdims=True)
    rstd = lax.rsqrt(jnp.mean(centred * centred, -1, keepdims=True) + EPSILON)
    return centred * rstd, rstd


def norm_back(x, gain, dz):
    xhat, rstd = norm_parts(x)
    dxh = dz * gain
    dx = (
        dxh
        - jnp.mean(dxh, -1, keepdims=True)
        - xhat * jnp.mean(dxh * xhat, -1, keepdims=True)
    ) * rstd
    return dx, jnp.sum(dz * xhat, 0, keepdims=True)


class Rows:
    def __init__(self, q, h):
        at = 0
        for name, size in (
            ("q", q), ("kv", 2 * h), ("r", 16), ("o", q),
            ("cq", q), ("cr", 16), ("ckv", 2 * h), ("co", q), ("gain", 16),
        ):
            setattr(self, name, slice(at, at + size))
            at += size
        self.total = at
        self.self_in = slice(self.q.start, self.r.stop)
        self.cross_in = slice(self.cq.start, self.cr.stop)


SELF, SHARED, CROSSED, BLOCKS = 0, 4, 6, 11
KV, MISC, CKV = 4, 5, 8


def layer_kernel(
    experts, hs, zs,
    tok, routes, xroutes, lens, ct_hbm,
    g0, g1, g2, g3, wr, wq, wk, wv, wo, wup, wdown, wcr, wcq, wck, wcv, wco,
    out_rows, out_grads, g_small, g_misc, fin,
    mine, other, msk, omsk, ct, wd, wa, ffn, a1, qT, kT, vT, kA, vA, qA, dA, gate, prob, attT, rl,
    hT, dT, dkv, mid, top, fa, b2, mem, act, gp, work, workb, gacc, gaT, kvs, kvr, sent, came,
    rx, ry, r2, rz, zx, ms, mz, sc, sxy, sg, sz, ssem, rsem, csem,
):
    R, W = mine.shape
    T = 2 * R
    FFH = ffn.shape[-1]
    nz, Dh = ffn.shape[2], ffn.shape[5]
    Dv = 2 * Dh
    QR = experts * hs
    rows = Rows(QR, hs)
    LC, FC = 256, 512
    NC = r2.shape[0]
    CW = FFH // NC
    ENC, DEC, CROSS = 0, 1, 2
    scale = 1.0 / math.sqrt(hs)

    s, d, half = lax.axis_index("section"), lax.axis_index("dp"), lax.axis_index("head")
    zv, core = d // zs, d % 2
    to_x, to_y = {"section": 1 - s}, {"head": 1 - half}
    to_xy = {"section": 1 - s, "head": 1 - half}
    to_c = {"dp": d + 1 - 2 * core}
    dz = [(zv + k) % nz * zs + d % zs for k in range(1, nz)]
    to_z = [{"dp": k} for k in dz]
    to_xz = [{"section": 1 - s, "dp": k} for k in dz]

    barrier = pltpu.get_barrier_semaphore()
    everyone = [to_x, to_y, to_xy, to_c] + to_z + to_xz
    for peer in everyone:
        pl.semaphore_signal(barrier, inc=1, device_id=peer, device_id_type=MESH)

    mine_copy = pltpu.make_async_copy(tok.at[s], mine, csem.at[1])
    mine_copy.start()
    ct_copy = pltpu.make_async_copy(ct_hbm.at[s], ct, csem.at[0])
    ct_copy.start()

    def named(ref, m):
        two = ref[m, :, pl.ds(pl.multiple_of(half * R, R), R)]
        ids = lax.broadcasted_iota(jnp.int32, (16, R), 0)
        return jnp.where((two[0:1] == ids) | (two[1:2] == ids), 1.0, 0.0)

    for m in (0, 1):
        msk[m] = named(routes, m).astype(BF16)

    def beside(a, b):
        return jnp.concatenate([a.astype(F32), b.astype(F32)], 1).astype(BF16)

    def own_block(b, value):
        wd[b, zv, core] = value.reshape(2, Dh, 128)

    row = lax.broadcasted_iota(jnp.int32, (128, Dv), 0)
    misc = jnp.zeros((128, Dv), F32)
    for ref, at in ((wr, 0), (wcr, 16)):
        for e in range(experts):
            misc = jnp.where(row == at + e, ref[e : e + 1, :].astype(F32), misc)
    for k, ref in enumerate((g0, g1, g2, g3)):
        misc = jnp.where(row == 32 + k, ref[...].astype(F32), misc)
    q_own, q_far = SELF + 2 * half, SELF + 2 * (1 - half)
    c_own, c_far = CROSSED + 3 * half, CROSSED + 3 * (1 - half)
    own_block(KV, beside(wk[...], wv[...]))
    own_block(MISC, misc.T.astype(BF16))
    own_block(q_own, beside(wq[0], wq[1]))

    pl.semaphore_wait(barrier, len(everyone))

    started = []

    def push(src, dst, peer):
        k = len(started)
        copy = pltpu.make_async_remote_copy(
            src_ref=src, dst_ref=dst, send_sem=ssem.at[k], recv_sem=rsem.at[k],
            device_id=peer, device_id_type=MESH,
        )
        copy.start()
        started.append(copy)
        return copy

    def same(part, peer):
        return push(part, part, peer)

    left = []

    def sent_off(copies):
        for copy in copies:
            if not any(copy is c for c in left):
                copy.wait_send()
                left.append(copy)

    queue = []

    def pump(n=1):
        for _ in range(n):
            if queue:
                queue.pop(0)[1]()

    def until(name):
        while any(k == name for k, _ in queue):
            queue.pop(0)[1]()

    def gather(group, own, far, shared):
        copies = [
            same(wd.at[pl.ds(b, n), zv, core], peer) for peer in to_z for b, n in own + shared
        ]
        over = {}

        def of_core(b, n):
            return wd.at[pl.ds(b, n), :, core]

        def one():
            for copy in copies:
                copy.wait_recv()
            over["y"] = [same(of_core(*b), to_y) for b in own]
            over["c"] = [same(of_core(*b), to_c) for b in own + shared]

        def two():
            for copy in over["y"]:
                copy.wait_recv()
            over["c"] += [same(of_core(*b), to_c) for b in far]

        def three():
            for copy in over["c"]:
                copy.wait_recv()

        return [(group, one), (group, two), (group, three)]

    early = gather("early", [(q_own, 1)], [(q_far, 1)], [(KV, 2)])
    tokens_in = [push(tok.at[1 - s], other, to_x), push(msk.at[1 - s], omsk, to_x)]

    def turned(ref):
        return ref[...].astype(F32).reshape(QR // 2, Dv).T.astype(BF16)

    own_block(q_own + 1, turned(wo))
    own_block(CKV, beside(wck[...], wcv[...]))
    own_block(c_own, beside(wcq[0], wcq[1]))
    own_block(c_own + 1, turned(wco))
    ffn[0, half, zv, core] = wup[...].reshape(2, Dh, FFH)
    ffn[1, half, zv, core] = wdown[...].reshape(2, Dh, FFH)
    xmask = named(xroutes, s)

    NA = 4
    AW = FFH // NA
    others = [(zv + k) % nz for k in range(1, nz)]
    go_z, go_y, go_x, go_xf = {}, {}, {}, {}
    go_c = {(j, far): [] for j in range(NA) for far in (0, 1)}

    def part(mat, h, z, j):
        return ffn.at[mat, h, z, core, :, :, j * AW : (j + 1) * AW]

    def all_z(mat, h, j):
        return ffn.at[mat, h, :, core, :, :, j * AW : (j + 1) * AW]

    def wait_all(copies):
        for copy in copies:
            copy.wait_recv()

    def ffn_send(j):
        go_z[j] = [same(part(s, half, zv, j), peer) for peer in to_z]

    def ffn_on(j):
        def run():
            wait_all(go_z[j])
            go_y[j] = [same(part(s, half, k, j), to_y) for k in others]
            go_x[j] = [same(part(s, half, k, j), to_x) for k in others]
            go_c[j, 0].append(same(all_z(s, half, j), to_c))

        return ("on%d" % j, run)

    def ffn_swap(j):
        def run():
            wait_all(go_x[j])
            go_c[j, 0].append(same(all_z(1 - s, half, j), to_c))
            if j == NA - 1:
                go_xf[j] = [same(all_z(1 - s, half, j), to_y)]

        return ("swap%d" % j, run)

    def ffn_far(j):
        def run():
            if j == 0:
                ffn_own.wait_recv()
            wait_all(go_y[j])
            if j < NA - 1:
                go_xf[j] = [same(all_z(s, 1 - half, j), to_x)]
            go_c[j, 1].append(same(all_z(s, 1 - half, j), to_c))

        return ("far%d" % j, run)

    def ffn_far_swap(j):
        def run():
            wait_all(go_xf[j])
            go_c[j, 1].append(same(all_z(1 - s, 1 - half, j), to_c))

        return ("farswap%d" % j, run)

    def ffn_end(j, far):
        return ("end%d%d" % (j, far), lambda: wait_all(go_c[j, far]))

    ffn_send(0)
    out_weights = gather("o", [(q_own + 1, 1)], [(q_far + 1, 1)], [])
    for j in range(1, NA):
        ffn_send(j)
    cross_weights = gather("cross", [(c_own, 2)], [(c_far, 2)], [(CKV, 1)])
    early[0][1]()
    ffn_own = same(ffn.at[s, half, zv, core], to_y)
    early[1][1]()
    early[2][1]()
    o1, o2, o3 = out_weights
    c1, c2, c3 = cross_weights
    on, swap, far, far_swap = (
        [make(j) for j in range(NA)] for make in (ffn_on, ffn_swap, ffn_far, ffn_far_swap)
    )
    end = [(ffn_end(j, 0), ffn_end(j, 1)) for j in range(NA)]
    queue += [on[0], o1, on[1], on[2], swap[0], o2, far[0], on[3], swap[1], o3, far[1]]
    queue += [c1, end[0][0], end[1][0]]
    queue += [swap[2], swap[3], far[2], end[2][0], end[3][0]]
    queue += [far_swap[0], far_swap[1], far[3], end[0][1], end[1][1]]
    queue += [c2, far_swap[2], far_swap[3], end[2][1], end[3][1], c3]

    def block(b):
        return wd[b].reshape(W, 128).astype(F32).T.astype(BF16)

    def head_rows(part, b0, b1):
        n = (part.stop - part.start) // 2
        wa[part.start : part.start + n, :] = block(b0)
        wa[part.start + n : part.stop, :] = block(b1)

    def exchange(slot):
        return push(kvs.at[slot % 3], kvr.at[slot], to_y)

    def gain(k):
        at = rows.gain.start
        return wa[at : at + 16, :].astype(F32)[k : k + 1, :]

    def norm_to(source, out, k):
        g = gain(k)

        def body(c):
            xhat, _ = norm_parts(source[c, :].astype(F32))
            out[c, :] = (xhat * g).astype(BF16)

        chunks(R, LC, body)

    def gates(m, named, logits):
        named = named[0:experts]
        l = jnp.where(named > 0, logits[0:experts], FAR)
        p = jnp.exp(l - jnp.max(l, 0, keepdims=True)) * named
        gate[m, 0:experts, :] = p / jnp.sum(p, 0, keepdims=True)

    def set_keys(m, slot, length):
        lane = lax.broadcasted_iota(jnp.int32, (1, T), 1)
        pos = jnp.where(lane < R, lane + half * R, lane - R + (1 - half) * R).astype(F32)
        outside = jnp.where(pos < length, 0.0, FAR)
        sub = lax.broadcasted_iota(jnp.int32, (128 - hs, T), 0)
        for to, wide, at, rest in (
            (kT, kA, 0, jnp.where(sub == 0, outside, 0.0)),
            (vT, vA, hs, jnp.where(sub < 2, 1.0, 0.0)),
        ):
            to[m, 0:hs, 0:R] = kvs[slot, at : at + hs, :]
            to[m, 0:hs, R:T] = kvr[slot, at : at + hs, :]
            wide[m] = jnp.concatenate([to[m, 0:hs, :].astype(F32), rest], 0).T.astype(BF16)
        vT[m, hs : hs + 16, :] = jnp.where(sub[0:16] < 2, 1.0, 0.0).astype(BF16)

    sub = lax.broadcasted_iota(jnp.int32, (128 - hs, R), 0)
    for k in (0, 1):
        qA[k, hs:128, :] = jnp.where(sub == 0, 1.0, 0.0).astype(BF16)
        dA[k, hs:128, :] = jnp.zeros((128 - hs, R), BF16)
    gacc[...] = jnp.zeros_like(gacc)

    def over_experts(one, pumps):
        for e in range(experts):
            one(e, 0)
            pump(pumps[e] if isinstance(pumps, tuple) else pumps)

    def attend(m, reach, pumps=1):
        C = R // 2
        items = [(e, c) for e in range(experts) for c in range(2)]

        def scores_of(e, c):
            cols = slice(c * C, (c + 1) * C)
            qA[e % 2, 0:hs, cols] = qT[m, e, :, cols]
            return mm(kA[m], qA[e % 2, :, cols])

        scores = scores_of(*items[0])
        for i, (e, c) in enumerate(items):
            cols = slice(c * C, (c + 1) * C)
            ahead = scores_of(*items[i + 1]) if i + 1 < len(items) else None
            if reach is not None:
                k = lax.broadcasted_iota(jnp.int32, (T, 1), 0)
                k = jnp.where(k < R, k + half * R, k - R + (1 - half) * R)
                q = lax.broadcasted_iota(jnp.int32, (1, C), 1) + half * R + reach + c * C
                scores = jnp.where(k <= q, scores, FAR)
            p = jnp.exp(scores - jnp.max(scores, 0, keepdims=True)).astype(BF16)
            prob[m, e, :, :, :, :, :, cols] = p.reshape(prob.shape[2:-1] + (C,))
            out = mm(vT[m, 0 : hs + 16, :], p)
            inverse = 1.0 / out[hs : hs + 1, :]
            attended = out[0:hs, :] * inverse
            attT[m, e, :, cols] = attended.astype(BF16)
            rl[m, e : e + 1, cols] = inverse
            hT[m, e * hs : (e + 1) * hs, cols] = (gate[m, e : e + 1, cols] * attended).astype(BF16)
            scores = ahead
            if c == 1:
                pump(pumps)

    def attend_back(m, dout, wo, pumps=1):
        dH = mm(wa[wo, :], dout, NT).astype(BF16)
        go = mm(hT[m], dout)
        work[0:QR, 0:R] = dH.astype(F32)

        def one(e, carry):
            span = slice(e * hs, (e + 1) * hs)
            dh = work[span, 0:R]
            dg = jnp.sum(dh * attT[m, e].astype(F32), 0, keepdims=True)
            g = gate[m, e : e + 1, :]
            inverse = rl[m, e : e + 1, :]
            gate[m, experts + e : experts + e + 1, :] = dg
            da = (dh * (g * inverse)).astype(BF16)
            delta = g * dg * inverse
            high = delta.astype(BF16).astype(F32)
            row = lax.broadcasted_iota(jnp.int32, (16, R), 0)
            dA[e % 2, 0:hs, :] = da
            dA[e % 2, hs : hs + 16, :] = jnp.where(
                row == 0, -high, jnp.where(row == 1, high - delta, 0.0)
            ).astype(BF16)
            p = prob[m, e].reshape(T, R)
            ds = (p.astype(F32) * mm(vA[m], dA[e % 2])).astype(BF16)
            dT[m, span, :] = (mm(kT[m, 0:hs, :], ds) * scale).astype(BF16)
            dk, dv = mm(qT[m, e], ds, NT), mm(da, p, NT)
            if e == 0:
                dkv[0:hs, :], dkv[hs : 2 * hs, :] = dk, dv
            else:
                dkv[0:hs, :] += dk
                dkv[hs : 2 * hs, :] += dv
            return carry

        over_experts(one, pumps)
        g = gate[m, 0:experts, :]
        dg = gate[m, experts : 2 * experts, :]
        dl = g * (dg - jnp.sum(g * dg, 0, keepdims=True))
        dT[m, QR : QR + 16, :] = jnp.concatenate(
            [dl, jnp.zeros((16 - experts, R), F32)], 0
        ).astype(BF16)
        return go

    def ffn_cols(mat, i):
        n = FFH // FC
        cols = pl.ds(pl.multiple_of(i % n * FC, FC), FC)
        return ffn[mat, i // n, :, :, :, :, cols].reshape(W, FC)

    def feed(m, out, i, start=None):
        c0 = math.sqrt(2.0 / math.pi)
        cols = pl.ds(pl.multiple_of(i * FC, FC), FC)
        u = mm(fa[m], ffn_cols(0, i))
        u2 = u * u
        t = jnp.tanh(c0 * u * (1.0 + 0.044715 * u2))
        half_up = 0.5 * (1.0 + t)
        a = (u * half_up).astype(BF16)
        act[m, :, cols] = a
        gp[m, :, cols] = (
            half_up + 0.5 * u * (1.0 - t * t) * (c0 * (1.0 + 3 * 0.044715 * u2))
        ).astype(BF16)
        part = mm(a, ffn_cols(1, i), NT)
        if start is None:
            out[...] += part
        else:
            out[...] = start[m] + part

    def feed_back(m, dout, out):
        def body(i, carry):
            cols = pl.ds(pl.multiple_of(i * FC, FC), FC)
            dh = mm(dout[...], ffn_cols(1, i))
            dh = (dh * gp[m, :, cols].astype(F32)).astype(BF16)
            gp[m, :, cols] = dh
            part = mm(dh, ffn_cols(0, i), NT)

            @pl.when(i == 0)
            def _():
                out[...] = part

            @pl.when(i > 0)
            def _():
                out[...] += part

            return carry

        lax.fori_loop(0, 2 * FFH // FC, body, 0)

    def norm_back_into(x, k, dz, add, outs):
        g = gain(k)

        def body(c):
            dx, dg = norm_back(x[c, :].astype(F32), g, dz[c, :])
            gacc[k : k + 1, :] += dg
            total = dx if add is None else add[c, :].astype(F32) + dx
            for out in outs:
                out[c, :] = total.astype(out.dtype)

        chunks(R, LC, body)

    def grad_block(b, t):
        gd[b] = t.T.astype(BF16).reshape(nz, 2, 2, Dh, 128)

    def summed(parts):
        total = parts[0][...].astype(F32)
        for part in parts[1:]:
            total = total + part[...].astype(F32)
        return total.astype(BF16)

    mt = block(MISC)
    wa[rows.r, :], wa[rows.cr, :], wa[rows.gain, :] = mt[0:16], mt[16:32], mt[32:48]
    wa[rows.kv, :] = block(KV)
    head_rows(rows.q, 0, 2)

    def project(m, slot, x, named):
        norm_to(x, a1.at[m], 0)
        kvs[slot] = mm(wa[rows.kv, :], a1[m], NT).astype(BF16)
        copy = exchange(slot)
        z = mm(wa[rows.self_in, :], a1[m], NT)
        qT[m] = (z[0:QR].astype(BF16).astype(F32) * scale).astype(BF16).reshape(experts, hs, R)
        gates(m, named[...].astype(F32), z[QR + 2 * hs :])
        return copy

    here, there = s, 1 - s
    mine_copy.wait()
    kv_here = project(here, 0, mine, msk.at[s])
    pump()
    for copy in tokens_in:
        copy.wait_recv()
    kv_there = project(there, 1, other, omsk)
    pump(2)
    for m, slot, copy in ((here, 0, kv_here), (there, 1, kv_there)):
        copy.wait_recv()
        set_keys(m, slot, lens[m, s].astype(F32))
        attend(m, (1 - m) * T)
    until("o")
    head_rows(rows.o, 1, 3)
    for m, x in ((here, mine), (there, other)):
        mid[m] = x[...].astype(F32) + mm(hT[m], wa[rows.o, :], TN)
    norm_to(mid.at[ENC], fa.at[ENC], 1)
    n = FFH // FC
    for k, name in enumerate(("end10", "end30", "end11", "end31")):
        until(name)
        h = half if k < 2 else 1 - half
        feed(ENC, top.at[ENC], h * n + k % 2, mid if k == 0 else None)
    until("cross")
    head_rows(rows.cq, CROSSED, CROSSED + 3)
    head_rows(rows.co, CROSSED + 1, CROSSED + 4)
    wa[rows.ckv, :] = block(CKV)
    weight_copies = list(started)
    norm_to(top.at[ENC], mem, 2)
    kvs[2] = mm(wa[rows.ckv, :], mem[...], NT).astype(BF16)
    kv_cross = exchange(2)
    norm_to(mid.at[DEC], b2, 3)
    z = mm(wa[rows.cross_in, :], b2[...], NT)
    qT[CROSS] = (z[0:QR].astype(BF16).astype(F32) * scale).astype(BF16).reshape(experts, hs, R)
    gates(CROSS, xmask, z[QR:])
    kv_cross.wait_recv()
    set_keys(CROSS, 2, lens[0, s].astype(F32))
    attend(CROSS, None)
    top[DEC] = mid[DEC] + mm(hT[CROSS], wa[rows.co, :], TN)
    norm_to(top.at[DEC], fa.at[DEC], 1)
    work[...] = top[DEC]

    for i in range(2 * n):
        feed(DEC, work, i)
    first = s == 0
    y = work[...].astype(BF16)
    sent[0] = jnp.where(first, mem[...], y)
    sent[1] = jnp.where(first, y, mem[...])
    rows_copy = pltpu.make_async_copy(sent.at[0], out_rows.at[s], csem.at[1])
    rows_copy.start()
    rows_in = push(sent.at[1], out_rows.at[s], to_x)

    sent_off(weight_copies)
    gd = wd
    ct_copy.wait()
    feed_back(DEC, ct, work)
    norm_back_into(top.at[DEC], 1, work, ct, (top.at[DEC], workb.at[DEC]))
    go = attend_back(CROSS, workb[DEC], rows.co)
    sent_off((kv_here, kv_there, kv_cross))
    kvs[0] = dkv[:, R:T].astype(BF16)
    back_cross = exchange(3)
    grad_block(CROSSED + 1, go[0:128])
    grad_block(CROSSED + 4, go[128:256])
    t = mm(dT[CROSS, 0 : QR + 16, :], b2[...])
    grad_block(CROSSED, t[0:128])
    grad_block(CROSSED + 3, t[128:256])
    gaT[16:32, :] = t[QR : QR + 16]
    work[...] = mm(dT[CROSS, 0 : QR + 16, :], wa[rows.cross_in, :], TN)
    norm_back_into(mid.at[DEC], 3, work, top.at[DEC], (top.at[DEC], workb.at[DEC]))
    back_cross.wait_recv()
    dkvc = (dkv[:, 0:R] + kvr[3].astype(F32)).astype(BF16)
    grad_block(CKV, mm(dkvc, mem[...]))

    def reduce_small(base, nb, st, n, at, place):
        mine_at, far_at = base + st * half, base + st * (1 - half)
        spare = slice(at, at + n)
        come = {}

        def p1():
            come["c"] = push(gd.at[base : base + nb, :, 1 - core], sc.at[base : base + nb], to_c)

        def p2():
            come["c"].wait_recv()
            own = gd.at[base : base + nb, :, core]
            own[...] = summed([own, sc.at[base : base + nb]])
            come["p"] = [
                push(gd.at[pl.ds(b, n), :, core, hs_], sxy.at[k, spare], peer)
                for k, (b, hs_, peer) in enumerate(
                    ((mine_at, 1 - s, to_x), (far_at, s, to_y), (far_at, 1 - s, to_xy))
                )
            ]

        def p3():
            for copy in come["p"]:
                copy.wait_recv()
            pair = gd[pl.ds(mine_at, n), :, core, s].astype(F32) + sxy[0, spare].astype(F32)
            far = sxy[1, spare].astype(F32) + sxy[2, spare].astype(F32)
            sg[spare] = (pair + far).astype(BF16)
            come["z"] = [
                push(sg.at[spare, (zv + j) % nz], sz.at[spare, s, j], peer)
                for j, peers in enumerate(zip([None] + to_z, [to_x] + to_xz))
                for peer in peers
                if peer is not None
            ]

        def p4():
            for copy in come["z"]:
                copy.wait_recv()
            sz[spare, s, 0] = sg[spare, zv]
            total = sz[spare, :, 0].astype(F32)
            for j in range(1, nz):
                total = total + sz[spare, :, j].astype(F32)
            for k in range(n):
                g_small[place(k)] = total[k].astype(BF16)

        return [("small", p) for p in (p1, p2, p3, p4)]

    def reduce_ffn(i):
        cols = slice(i * CW, (i + 1) * CW)
        come = {}

        def rc(i):
            return prob.at[CROSS, i, :, :, :, :, 0:Dh, 0:CW]

        ways = ("yzx" if i == NC - 2 else "xyz", "yzx")

        def p1():
            come["c"] = push(ffn.at[:, :, :, 1 - core, :, :, cols], rc(i), to_c)

        def p2():
            come["c"].wait_recv()
            own = ffn.at[:, :, :, core, :, :, cols]
            own[...] = summed([own, rc(i)])
            for mat in (0, 1):
                if ways[mat] == "xyz":
                    given = ffn.at[mat, :, :, core, 1 - s, :, cols]
                    come[mat] = push(given, rx.at[min(i, NC - 2)], to_x)
                else:
                    given = ffn.at[mat, 1 - half, :, core, :, :, cols]
                    come[mat] = push(given, ry.at[i if mat else NC], to_y)

        def z_push(mat, side, to):
            return [
                push(ffn.at[mat, half, (zv + j) % nz, core, side, :, cols], to.at[j - 1], to_z[j - 1])
                for j in range(1, nz)
            ]

        def p3():
            for mat in (0, 1):
                come[mat].wait_recv()
                if ways[mat] == "xyz":
                    own = ffn.at[mat, :, :, core, s, :, cols]
                    own[...] = summed([own, rx.at[min(i, NC - 2)]])
                    given = ffn.at[mat, 1 - half, :, core, s, :, cols]
                    come[mat] = [push(given, r2.at[i], to_y)]
                else:
                    own = ffn.at[mat, half, :, core, :, :, cols]
                    own[...] = summed([own, ry.at[i if mat else NC]])
                    come[mat] = z_push(mat, slice(None), rz.at[i, mat])

        def z_sum(mat, side, out):
            out[...] = summed(
                [ffn.at[mat, half, zv, core, side, :, cols]]
                + [rz.at[i, mat, j, side] for j in range(nz - 1)]
            )

        def p4():
            for mat in (0, 1):
                wait_all(come[mat])
                if ways[mat] == "xyz":
                    own = ffn.at[mat, half, :, core, s, :, cols]
                    own[...] = summed([own, r2.at[i]])
                    come[mat] = z_push(mat, s, rz.at[i, mat, :, s])
                else:
                    z_sum(mat, slice(None), zx.at[i, mat, 0])
                    come[mat] = [push(zx.at[i, mat, 0], zx.at[i, mat, 1], to_x)]

        def p5():
            for mat in (0, 1):
                wait_all(come[mat])
                if ways[mat] == "xyz":
                    z_sum(mat, s, fin.at[mat, s, :, cols])
                    come[mat] = [same(fin.at[mat, s, :, cols], to_x)]
                else:
                    fin[mat, :, :, cols] = summed([zx.at[i, mat, 0], zx.at[i, mat, 1]])
                    come[mat] = []

        def p6():
            for mat in (0, 1):
                wait_all(come[mat])

        return [("p%d%d" % (k + 1, i), p) for k, p in enumerate((p1, p2, p3, p4, p5, p6))]

    def reduce_misc():
        come = {}

        def p1():
            come["c"] = push(ms.at[0], ms.at[1], to_c)

        def p2():
            come["c"].wait_recv()
            ms[2] = summed([ms.at[0], ms.at[1]])
            come["p"] = [
                push(ms.at[2], ms.at[3 + k], peer) for k, peer in enumerate((to_x, to_y, to_xy))
            ]

        def p3():
            wait_all(come["p"])
            pair = ms[2].astype(F32) + ms[3].astype(F32)
            far = ms[4].astype(F32) + ms[5].astype(F32)
            mz[zv] = (pair + far).astype(BF16)
            come["z"] = [same(mz.at[zv], peer) for peer in to_z]

        def p4():
            wait_all(come["z"])
            g_misc[...] = summed([mz.at[j] for j in range(nz)])

        return [("misc", p) for p in (p1, p2, p3, p4)]

    cross_sum = reduce_small(CROSSED, 5, 2, 3, 3, lambda k: 3 + (k + 2 * half) % 3)
    cross_sum[0][1]()
    work[...] = mm(dkvc, wa[rows.ckv, :], TN).astype(BF16).astype(F32)
    norm_back_into(top.at[ENC], 2, work, None, (top.at[ENC], workb.at[ENC]))
    cross_sum[1][1]()
    feed_back(ENC, workb.at[ENC], work)

    waves = [reduce_ffn(i) for i in range(NC)]
    p1, p2, p3, p4, p5, p6 = ([wave[k] for wave in waves] for k in range(6))

    def weight_grads(i):
        for hh in (0, 1):
            at = hh * FFH + i * CW
            cols, to = slice(at, at + CW), slice(i * CW, (i + 1) * CW)
            shape = (nz, 2, 2, Dh, CW)
            up = mm(fa[ENC], gp[ENC, :, cols], TN) + mm(fa[DEC], gp[DEC, :, cols], TN)
            ffn[0, hh, :, :, :, :, to] = up.astype(BF16).reshape(shape)
            down = mm(dout_enc[...], act[ENC, :, cols], TN) + mm(ct[...], act[DEC, :, cols], TN)
            ffn[1, hh, :, :, :, :, to] = down.astype(BF16).reshape(shape)
        run(p1[i])

    def run(*events):
        for _, event in events:
            event()

    dout_enc = b2
    dout_enc[...] = workb[ENC]
    for i in range(NC // 2):
        weight_grads(i)
        if i > 0:
            run(p2[i - 1])
    norm_back_into(mid.at[ENC], 1, work, top.at[ENC], (top.at[ENC], workb.at[ENC]))
    run(p2[NC // 2 - 1])

    at_r, at_kv = QR, QR + 16
    kv_rows = slice(at_kv, at_kv + 2 * hs)

    def self_back(m, slot, pumps):
        go = attend_back(m, workb[m], rows.o, pumps)
        kvs[slot % 3] = dkv[:, R:T].astype(BF16)
        return go, exchange(slot)

    def inner(m, slot, copy):
        copy.wait_recv()
        dT[m, kv_rows, :] = (dkv[:, 0:R] + kvr[slot].astype(F32)).astype(BF16)
        work[...] = (
            mm(dT[m, 0:at_r, :], wa[rows.q, :], TN)
            + mm(dT[m, at_r:at_kv, :], wa[rows.r, :], TN)
            + mm(dT[m, kv_rows, :], wa[rows.kv, :], TN)
        )

    queue += [cross_sum[2], p3[0]]
    go, copy_there = self_back(there, 4, (0, 1, 0, 1))
    mid[DEC, 0:QR, :] = go
    for i in range(NC // 2, NC):
        weight_grads(i)
        if i > NC // 2:
            run(p2[i - 1])
    run(p3[1], p2[NC - 1])
    inner(there, 4, copy_there)
    sent_off([rows_in])
    norm_back_into(other, 0, work, top.at[there], (sent.at[1],))
    grads_in = push(sent.at[1], came, to_x)
    queue += [cross_sum[3], p3[2], p4[0], p3[3]]
    go, copy_here = self_back(here, 5, (0, 1, 1, 2))
    go = go + mid[DEC, 0:QR, :]
    grad_block(SELF + 1, go[0:128])
    grad_block(SELF + 3, go[128:256])
    t = mm(dT[ENC, 0:at_kv, :], a1[ENC]) + mm(dT[DEC, 0:at_kv, :], a1[DEC])
    grad_block(SELF, t[0:128])
    grad_block(SELF + 2, t[128:256])
    self_sum = reduce_small(SELF, 4, 2, 2, 0, lambda k: k)
    run(self_sum[0], p4[1], self_sum[1])
    inner(here, 5, copy_here)
    grad_block(KV, mm(dT[ENC, kv_rows, :], a1[ENC]) + mm(dT[DEC, kv_rows, :], a1[DEC]))
    kv_sum = reduce_small(KV, 1, 0, 1, 2, lambda k: 2 + k)
    run(kv_sum[0])
    norm_back_into(mine, 0, work, top.at[here], (mid.at[here],))
    grads_copy = pltpu.make_async_copy(mid.at[here], out_grads.at[s], csem.at[0])
    grads_copy.start()
    ms[0] = jnp.concatenate(
        [t[at_r : at_r + 4], gaT[16:20, :], gacc[0:4, :], jnp.zeros((4, W), F32)], 0
    ).astype(BF16)
    misc_sum = reduce_misc()
    run(misc_sum[0], kv_sum[1], misc_sum[1], p4[2], p5[0], p4[3], p5[1], self_sum[2])
    grads_in.wait_recv()
    mid[there] = came[...].astype(F32)
    far_copy = pltpu.make_async_copy(mid.at[there], out_grads.at[1 - s], csem.at[2])
    far_copy.start()
    run(kv_sum[2], misc_sum[2], p5[2], p5[3], self_sum[3], kv_sum[3], misc_sum[3], *p6)
    rows_in.wait_recv()
    rows_copy.wait()
    grads_copy.wait()
    far_copy.wait()
    sent_off(started)


def outputs_kernel(
    el, hs, experts, rows_in, grads_in, small_in, misc, ffn_in,
    rows, grads, n0, n1, n2, n3, gr, gq, gk, gv, go, gup, gdown, gcr, gcq, gck, gcv, gco, small, ffn, sem,
):
    copies = [
        pltpu.make_async_copy(rows_in, rows.at[0], sem.at[0]),
        pltpu.make_async_copy(grads_in, grads.at[0], sem.at[1]),
        pltpu.make_async_copy(ffn_in, ffn, sem.at[2]),
        pltpu.make_async_copy(small_in, small, sem.at[3]),
    ]
    for copy in reversed(copies):
        copy.start()
    copies.pop().wait()
    q, o, kv, cq, co, ckv = (small[k].astype(F32) for k in range(6))
    for ref, value in ((gq, q), (gcq, cq)):
        for e in range(el):
            ref[e] = value[:, e * hs : (e + 1) * hs]
    for ref, value in ((go, o), (gco, co)):
        ref[...] = value.T.reshape(ref.shape)
    gk[...], gv[...], gck[...], gcv[...] = kv[:, 0:hs], kv[:, hs:], ckv[:, 0:hs], ckv[:, hs:]
    D, W = n0.shape[1], misc.shape[1]
    feature = lax.broadcasted_iota(jnp.int32, (W, D), 0) - lax.axis_index("dp") * D
    chosen = jnp.where(feature == lax.broadcasted_iota(jnp.int32, (W, D), 1), 1.0, 0.0)
    own = mm(misc[...], chosen.astype(BF16))
    gr[...], gcr[...] = own[0:experts], own[4 : 4 + experts]
    for k, ref in enumerate((n0, n1, n2, n3)):
        ref[...] = own[8 + k : 9 + k, :]
    copies.pop().wait()
    gup[...] = ffn[0].astype(F32)
    gdown[...] = ffn[1].astype(F32)
    for copy in copies:
        copy.wait()


def run_layers(experts, hs, nz, zs, tok, routes, xroutes, lens, ct, weights):
    _, R, W = tok.shape
    FFH = weights[9].shape[1]
    Dh = W // (4 * nz)
    T, QR, NC = 2 * R, experts * hs, 4
    CW = FFH // NC
    vm = pltpu.VMEM
    dma = pltpu.SemaphoreType.DMA
    any_, whole = pl.BlockSpec(memory_space=pl.ANY), pl.BlockSpec(memory_space=vm)
    scalars = pl.BlockSpec(memory_space=pltpu.SMEM)
    return pl.pallas_call(
        functools.partial(layer_kernel, experts, hs, zs),
        out_shape=(
            jax.ShapeDtypeStruct((2, R, W), BF16),
            jax.ShapeDtypeStruct((2, R, W), F32),
            jax.ShapeDtypeStruct((6, 2, Dh, 128), BF16),
            jax.ShapeDtypeStruct((16, W), BF16),
            jax.ShapeDtypeStruct((2, 2, Dh, FFH), BF16),
        ),
        in_specs=[any_, whole, whole, scalars, any_] + [whole] * len(weights),
        out_specs=[any_, any_, whole, whole, whole],
        scratch_shapes=[
            vm((R, W), BF16),
            vm((R, W), BF16),
            vm((2, 16, R), BF16),
            vm((16, R), BF16),
            vm((R, W), BF16),
            vm((BLOCKS, nz, 2, 2, Dh, 128), BF16),
            vm((Rows(QR, hs).total, W), BF16),
            vm((2, 2, nz, 2, 2, Dh, FFH), BF16),
            vm((2, R, W), BF16),
            vm((3, experts, hs, R), BF16),
            vm((3, hs, T), BF16),
            vm((3, hs + 16, T), BF16),
            vm((3, T, 128), BF16),
            vm((3, T, 128), BF16),
            vm((2, 128, R), BF16),
            vm((2, 128, R), BF16),
            vm((3, 2 * experts, R), F32),
            vm((3, experts, 2, 2, nz, 2, T // (8 * nz), R), BF16),
            vm((3, experts, hs, R), BF16),
            vm((3, 8, R), F32),
            vm((3, QR, R), BF16),
            vm((3, QR + 16 + 2 * hs, R), BF16),
            vm((2 * hs, T), F32),
            vm((2, R, W), F32),
            vm((2, R, W), F32),
            vm((2, R, W), BF16),
            vm((R, W), BF16),
            vm((R, W), BF16),
            vm((2, R, 2 * FFH), BF16),
            vm((2, R, 2 * FFH), BF16),
            vm((R, W), F32),
            vm((2, R, W), BF16),
            vm((16, W), F32),
            vm((32, W), F32),
            vm((3, 2 * hs, R), BF16),
            vm((6, 2 * hs, R), BF16),
            vm((2, R, W), BF16),
            vm((R, W), BF16),
            vm((NC - 1, 2, nz, Dh, CW), BF16),
            vm((NC + 1, nz, 2, Dh, CW), BF16),
            vm((NC, nz, Dh, CW), BF16),
            vm((NC, 2, max(nz - 1, 1), 2, Dh, CW), BF16),
            vm((NC, 2, 2, 2, Dh, CW), BF16),
            vm((6, 16, W), BF16),
            vm((nz, 16, W), BF16),
            vm((BLOCKS, nz, 2, Dh, 128), BF16),
            vm((3, 6, nz, Dh, 128), BF16),
            vm((6, nz, Dh, 128), BF16),
            vm((6, 2, nz, Dh, 128), BF16),
            dma((200,)),
            dma((200,)),
            dma((3,)),
        ],
        compiler_params=pltpu.CompilerParams(
            collective_id=0, has_side_effects=True, vmem_limit_bytes=63 * 2**20
        ),
    )(tok, routes, xroutes, lens, ct, *weights)


def on_device(
    tokens, self_routes, cross_routes, lengths, cotangent,
    norm_attn, norm_ffn, norm_final, norm_cross,
    router, query_weight, key_weight, value_weight, output_weight, up_weight, down_weight,
    cross_router, cross_query, cross_key, cross_value, cross_output,
):
    dp = lax.axis_size("dp")
    R, W = tokens.shape[2:]
    el, D, hs = query_weight.shape
    experts = el * lax.axis_size("head")
    FFH = up_weight.shape[1]
    nz = min(4, dp // 2)
    zs = dp // nz
    Dv = W // (2 * nz)
    blocks = [[z * zs + j for j in range(zs)] for z in range(nz)]
    core = lax.axis_index("dp") % 2

    def widened(a, axis):
        if zs == 2:
            return a
        a = lax.all_gather(a, "dp", axis=axis, tiled=True, axis_index_groups=blocks)
        return lax.dynamic_slice_in_dim(a, core * Dv, Dv, axis)

    def narrowed(a):
        if zs == 2:
            return a
        wide = jnp.zeros((a.shape[0], 2 * Dv, a.shape[2]), BF16)
        wide = lax.dynamic_update_slice_in_dim(wide, a, core * Dv, 1)
        return lax.psum_scatter(
            wide, "dp", scatter_dimension=1, axis_index_groups=blocks, tiled=True
        )

    gains = (norm_attn, norm_ffn, norm_final, norm_cross)
    weights = [widened(g, 0).reshape(1, Dv) for g in gains]
    weights += [
        widened(w, axis)
        for w, axis in (
            (router.T, 1), (query_weight, 1), (key_weight, 0), (value_weight, 0),
            (output_weight, 2), (up_weight, 0), (down_weight.T, 0),
            (cross_router.T, 1), (cross_query, 1), (cross_key, 0), (cross_value, 0),
            (cross_output, 2),
        )
    ]
    out, grads, small, misc, ffn = run_layers(
        experts, hs, nz, zs, tokens[0],
        jnp.swapaxes(self_routes[0], 1, 2), jnp.swapaxes(cross_routes, 1, 2),
        lengths[:, :, 0], cotangent, weights,
    )
    small = narrowed(small.reshape(6, Dv, 128))
    ffn = narrowed(ffn.reshape(2, Dv, FFH))

    def f32(*shape):
        return jax.ShapeDtypeStruct(shape, F32)

    whole = pl.BlockSpec(memory_space=pltpu.VMEM)
    attention = (
        f32(experts, D), f32(el, D, hs), f32(D, hs), f32(D, hs), f32(el, hs, D),
    )
    done = pl.pallas_call(
        functools.partial(outputs_kernel, el, hs, experts),
        out_shape=(
            jax.ShapeDtypeStruct((1, 2, R, W), BF16), f32(1, 2, R, W),
            *(f32(1, D),) * 4, *attention, *(f32(D, FFH),) * 2, *attention,
        ),
        in_specs=[pl.BlockSpec(memory_space=pltpu.HBM)] * 3 + [whole, pl.BlockSpec(memory_space=pltpu.HBM)],
        out_specs=[whole] * 18,
        scratch_shapes=[
            pltpu.VMEM(small.shape, BF16), pltpu.VMEM(ffn.shape, BF16), pltpu.SemaphoreType.DMA((4,)),
        ],
        compiler_params=pltpu.CompilerParams(vmem_limit_bytes=60 * 2**20),
    )(out, grads, small, misc, ffn)
    rows, grads, n0, n1, n2, n3, gr, gq, gk, gv, go, gup, gdown, gcr, gcq, gck, gcv, gco = done
    return (
        rows, grads, *(g.reshape(D) for g in (n0, n1, n2, n3)),
        gr.T, gq, gk, gv, go, gup, gdown.T, gcr.T, gcq, gck, gcv, gco,
    )


def solution(mesh):
    rows = P("section", None, ("dp", "head"), None)
    vector, tall = P("dp"), P("dp", None)
    query, out = P("head", "dp", None), P("head", None, "dp")
    weights = (
        vector, vector, vector, vector,
        tall, query, tall, tall, out, P("dp", "head"), P("head", "dp"),
        tall, query, tall, tall, out,
    )
    return jax.shard_map(
        on_device,
        mesh=mesh,
        in_specs=(
            rows, P("section", None, "dp", None), P(None, "dp", None), P(None, None, "dp"),
            P(None, ("dp", "head"), None), *weights,
        ),
        out_specs=(rows, rows, *weights),
        check_vma=False,
    )
```

```python
import functools
import math

import jax
import jax.numpy as jnp
from jax import lax
from jax.experimental import pallas as pl
from jax.experimental.pallas import tpu as pltpu
from jax.sharding import PartitionSpec as P

EPSILON = 1e-05
FAR = -1e30
F32 = jnp.float32
BF16 = jnp.bfloat16
MESH = pl.DeviceIdType.MESH
NN = (((1,), (0,)), ((), ()))
NT = (((1,), (1,)), ((), ()))
TN = (((0,), (0,)), ((), ()))


def mm(a, b, dims=NN):
    return lax.dot_general(a, b, dims, preferred_element_type=F32)


def chunks(total, size, body):
    def step(i, carry):
        body(pl.ds(pl.multiple_of(i * size, size), size))
        return carry

    lax.fori_loop(0, total // size, step, 0)


def norm_parts(x):
    centred = x - jnp.mean(x, -1, keepdims=True)
    rstd = lax.rsqrt(jnp.mean(centred * centred, -1, keepdims=True) + EPSILON)
    return centred * rstd, rstd


def norm_back(x, gain, dz):
    xhat, rstd = norm_parts(x)
    dxh = dz * gain
    dx = (
        dxh
        - jnp.mean(dxh, -1, keepdims=True)
        - xhat * jnp.mean(dxh * xhat, -1, keepdims=True)
    ) * rstd
    return dx, jnp.sum(dz * xhat, 0, keepdims=True)


class Rows:
    def __init__(self, q, h):
        at = 0
        for name, size in (
            ("q", q), ("kv", 2 * h), ("r", 16), ("o", q),
            ("cq", q), ("cr", 16), ("ckv", 2 * h), ("co", q), ("gain", 16),
        ):
            setattr(self, name, slice(at, at + size))
            at += size
        self.total = at
        self.self_in = slice(self.q.start, self.r.stop)
        self.cross_in = slice(self.cq.start, self.cr.stop)


SELF, SHARED, CROSSED, BLOCKS = 0, 4, 6, 11
KV, MISC, CKV = 4, 5, 8


def layer_kernel(
    experts, hs, zs,
    tok, routes, xroutes, lens, ct_hbm,
    g0, g1, g2, g3, wr, wq, wk, wv, wo, wup, wdown, wcr, wcq, wck, wcv, wco,
    out_rows, out_grads, g_small, g_misc, fin,
    mine, other, msk, omsk, ct, wd, wa, ffn, a1, qT, kT, vT, kA, vA, qA, dA, gate, prob, attT, rl,
    hT, dT, dkv, mid, top, fa, b2, mem, act, gp, work, workb, gacc, gaT, kvs, kvr, sent, came,
    rx, ry, r2, rz, zx, ms, mz, sc, sxy, sg, sy, xs, sz, ssem, rsem, csem,
):
    R, W = mine.shape
    T = 2 * R
    FFH = ffn.shape[-1]
    nz, Dh = ffn.shape[2], ffn.shape[5]
    Dv = 2 * Dh
    QR = experts * hs
    rows = Rows(QR, hs)
    LC, FC = 256, 512
    NC = r2.shape[0]
    CW = FFH // NC
    ENC, DEC, CROSS = 0, 1, 2
    scale = 1.0 / math.sqrt(hs)
    base2 = scale * math.log2(math.e)

    s, d, half = lax.axis_index("section"), lax.axis_index("dp"), lax.axis_index("head")
    zv, core = d // zs, d % 2
    to_x, to_y = {"section": 1 - s}, {"head": 1 - half}
    to_xy = {"section": 1 - s, "head": 1 - half}
    to_c = {"dp": d + 1 - 2 * core}
    dz = [(zv + k) % nz * zs + d % zs for k in range(1, nz)]
    to_z = [{"dp": k} for k in dz]
    to_xz = [{"section": 1 - s, "dp": k} for k in dz]

    barrier = pltpu.get_barrier_semaphore()
    everyone = [to_x, to_y, to_xy, to_c] + to_z + to_xz
    for peer in everyone:
        pl.semaphore_signal(barrier, inc=1, device_id=peer, device_id_type=MESH)

    mine_copy = pltpu.make_async_copy(tok.at[s], mine, csem.at[1])
    mine_copy.start()
    ct_copy = pltpu.make_async_copy(ct_hbm.at[s], ct, csem.at[0])
    ct_copy.start()

    def named(ref, m):
        two = ref[m, :, pl.ds(pl.multiple_of(half * R, R), R)]
        ids = lax.broadcasted_iota(jnp.int32, (16, R), 0)
        return jnp.where((two[0:1] == ids) | (two[1:2] == ids), 1.0, 0.0)

    for m in (0, 1):
        msk[m] = named(routes, m).astype(BF16)

    def beside(a, b):
        return jnp.concatenate([a.astype(F32), b.astype(F32)], 1).astype(BF16)

    def own_block(b, value):
        wd[b, zv, core] = value.reshape(2, Dh, 128)

    row = lax.broadcasted_iota(jnp.int32, (128, Dv), 0)
    misc = jnp.zeros((128, Dv), F32)
    for ref, at in ((wr, 0), (wcr, 16)):
        for e in range(experts):
            misc = jnp.where(row == at + e, ref[e : e + 1, :].astype(F32), misc)
    for k, ref in enumerate((g0, g1, g2, g3)):
        misc = jnp.where(row == 32 + k, ref[...].astype(F32), misc)
    q_own, q_far = SELF + 2 * half, SELF + 2 * (1 - half)
    c_own, c_far = CROSSED + 3 * half, CROSSED + 3 * (1 - half)
    own_block(KV, beside(wk[...], wv[...]))
    own_block(MISC, misc.T.astype(BF16))
    own_block(q_own, beside(wq[0], wq[1]))

    pl.semaphore_wait(barrier, len(everyone))

    started = []

    def push(src, dst, peer):
        k = len(started)
        copy = pltpu.make_async_remote_copy(
            src_ref=src, dst_ref=dst, send_sem=ssem.at[k], recv_sem=rsem.at[k],
            device_id=peer, device_id_type=MESH,
        )
        copy.start()
        started.append(copy)
        return copy

    def same(part, peer):
        return push(part, part, peer)

    left = []

    def sent_off(copies):
        for copy in copies:
            if not any(copy is c for c in left):
                copy.wait_send()
                left.append(copy)

    queue = []

    def pump(n=1):
        for _ in range(n):
            if queue:
                queue.pop(0)[1]()

    def until(name):
        while any(k == name for k, _ in queue):
            queue.pop(0)[1]()

    def gather(group, own, far, shared):
        copies = [
            same(wd.at[pl.ds(b, n), zv, core], peer) for peer in to_z for b, n in own + shared
        ]
        over = {}

        def of_core(b, n):
            return wd.at[pl.ds(b, n), :, core]

        def one():
            for copy in copies:
                copy.wait_recv()
            over["y"] = [same(of_core(*b), to_y) for b in own]
            over["c"] = [same(of_core(*b), to_c) for b in own + shared]

        def two():
            for copy in over["y"]:
                copy.wait_recv()
            over["c"] += [same(of_core(*b), to_c) for b in far]

        def three():
            for copy in over["c"]:
                copy.wait_recv()

        return [(group, one), (group, two), (group, three)]

    early = gather("early", [(q_own, 1)], [(q_far, 1)], [(KV, 2)])
    tokens_in = [push(tok.at[1 - s], other, to_x), push(msk.at[1 - s], omsk, to_x)]

    def turned(ref):
        return ref[...].astype(F32).reshape(QR // 2, Dv).T.astype(BF16)

    own_block(q_own + 1, turned(wo))
    own_block(CKV, beside(wck[...], wcv[...]))
    own_block(c_own, beside(wcq[0], wcq[1]))
    own_block(c_own + 1, turned(wco))
    ffn[0, half, zv, core] = wup[...].reshape(2, Dh, FFH)
    ffn[1, half, zv, core] = wdown[...].reshape(2, Dh, FFH)
    xmask = named(xroutes, s)

    NA = 4
    AW = FFH // NA
    others = [(zv + k) % nz for k in range(1, nz)]
    go_z, go_y, go_x, go_xf = {}, {}, {}, {}
    go_c = {(j, far): [] for j in range(NA) for far in (0, 1)}

    def part(mat, h, z, j):
        return ffn.at[mat, h, z, core, :, :, j * AW : (j + 1) * AW]

    def all_z(mat, h, j):
        return ffn.at[mat, h, :, core, :, :, j * AW : (j + 1) * AW]

    def wait_all(copies):
        for copy in copies:
            copy.wait_recv()

    def ffn_send(j):
        go_z[j] = [same(part(s, half, zv, j), peer) for peer in to_z]

    def ffn_on(j):
        def run():
            wait_all(go_z[j])
            go_y[j] = [same(part(s, half, k, j), to_y) for k in others]
            go_x[j] = [same(part(s, half, k, j), to_x) for k in others]
            go_c[j, 0].append(same(all_z(s, half, j), to_c))

        return ("on%d" % j, run)

    def ffn_swap(j):
        def run():
            wait_all(go_x[j])
            go_c[j, 0].append(same(all_z(1 - s, half, j), to_c))
            if j == NA - 1:
                go_xf[j] = [same(all_z(1 - s, half, j), to_y)]

        return ("swap%d" % j, run)

    def ffn_far(j):
        def run():
            if j == 0:
                ffn_own.wait_recv()
            wait_all(go_y[j])
            if j < NA - 1:
                go_xf[j] = [same(all_z(s, 1 - half, j), to_x)]
            go_c[j, 1].append(same(all_z(s, 1 - half, j), to_c))

        return ("far%d" % j, run)

    def ffn_far_swap(j):
        def run():
            wait_all(go_xf[j])
            go_c[j, 1].append(same(all_z(1 - s, 1 - half, j), to_c))

        return ("farswap%d" % j, run)

    def ffn_end(j, far):
        return ("end%d%d" % (j, far), lambda: wait_all(go_c[j, far]))

    ffn_send(0)
    out_weights = gather("o", [(q_own + 1, 1)], [(q_far + 1, 1)], [])
    for j in range(1, NA):
        ffn_send(j)
    cross_weights = gather("cross", [(c_own, 2)], [(c_far, 2)], [(CKV, 1)])
    early[0][1]()
    ffn_own = same(ffn.at[s, half, zv, core], to_y)
    early[1][1]()
    early[2][1]()
    o1, o2, o3 = out_weights
    c1, c2, c3 = cross_weights
    on, swap, far, far_swap = (
        [make(j) for j in range(NA)] for make in (ffn_on, ffn_swap, ffn_far, ffn_far_swap)
    )
    end = [(ffn_end(j, 0), ffn_end(j, 1)) for j in range(NA)]
    queue += [on[0], o1, on[1], on[2], swap[0], o2, far[0], on[3], swap[1], o3, far[1]]
    queue += [c1, end[0][0], end[1][0]]
    queue += [swap[2], swap[3], far[2], end[2][0], end[3][0]]
    queue += [far_swap[0], far_swap[1], far[3], end[0][1], end[1][1]]
    queue += [c2, far_swap[2], far_swap[3], end[2][1], end[3][1], c3]

    def block(b):
        return wd[b].reshape(W, 128).astype(F32).T.astype(BF16)

    def head_rows(part, b0, b1):
        n = (part.stop - part.start) // 2
        wa[part.start : part.start + n, :] = block(b0)
        wa[part.start + n : part.stop, :] = block(b1)

    def exchange(slot):
        return push(kvs.at[slot % 3], kvr.at[slot], to_y)

    def gain(k):
        at = rows.gain.start
        return wa[at : at + 16, :].astype(F32)[k : k + 1, :]

    def norm_to(source, out, k):
        g = gain(k)

        def body(c):
            xhat, _ = norm_parts(source[c, :].astype(F32))
            out[c, :] = (xhat * g).astype(BF16)

        chunks(R, R, body)

    def gates(m, named, logits):
        named = named[0:experts]
        l = jnp.where(named > 0, logits[0:experts], FAR)
        p = jnp.exp(l - jnp.max(l, 0, keepdims=True)) * named
        gate[m, 0:experts, :] = p / jnp.sum(p, 0, keepdims=True)

    def set_keys(m, pairs, length, far):
        keys = slice(far * R, (far + 1) * R)
        pos = lax.broadcasted_iota(jnp.int32, (1, R), 1) + (1 - half if far else half) * R
        outside = jnp.where(pos.astype(F32) < length, 0.0, FAR)
        sub = lax.broadcasted_iota(jnp.int32, (128 - hs, R), 0)
        for to, wide, at, rest in (
            (kT, kA, 0, jnp.where(sub == 0, outside, 0.0)),
            (vT, vA, hs, jnp.where(sub < 2, 1.0, 0.0)),
        ):
            part = pairs[at : at + hs, :]
            to[m, 0:hs, keys] = part
            wide[m, keys, :] = jnp.concatenate([part.astype(F32), rest], 0).T.astype(BF16)
        vT[m, hs : hs + 16, keys] = jnp.where(sub[0:16] < 2, 1.0, 0.0).astype(BF16)

    sub = lax.broadcasted_iota(jnp.int32, (128 - hs, R), 0)
    for k in (0, 1):
        qA[k, hs:128, :] = jnp.where(sub == 0, 1.0, 0.0).astype(BF16)
        dA[k, hs:128, :] = jnp.zeros((128 - hs, R), BF16)
    gacc[...] = jnp.zeros_like(gacc)

    def over_experts(one, pumps):
        for e in range(experts):
            one(e, 0)
            pump(pumps[e] if isinstance(pumps, tuple) else pumps)

    def attend(m, reach, pumps=1):
        C = R // 2
        items = [(e, c) for e in range(experts) for c in range(2)]

        def scores_of(e, c):
            cols = slice(c * C, (c + 1) * C)
            qA[e % 2, 0:hs, cols] = qT[m, e, :, cols]
            return mm(kA[m], qA[e % 2, :, cols])

        scores = scores_of(*items[0])
        for i, (e, c) in enumerate(items):
            cols = slice(c * C, (c + 1) * C)
            ahead = scores_of(*items[i + 1]) if i + 1 < len(items) else None
            if reach is not None:
                k = lax.broadcasted_iota(jnp.int32, (T, 1), 0)
                k = jnp.where(k < R, k + half * R, k - R + (1 - half) * R)
                q = lax.broadcasted_iota(jnp.int32, (1, C), 1) + half * R + reach + c * C
                scores = jnp.where(k <= q, scores, FAR)
            p = jnp.exp2(scores - jnp.max(scores, 0, keepdims=True)).astype(BF16)
            prob[m, e, :, :, :, :, :, cols] = p.reshape(prob.shape[2:-1] + (C,))
            out = mm(vT[m, 0 : hs + 16, :], p)
            inverse = 1.0 / out[hs : hs + 1, :]
            attended = out[0:hs, :] * inverse
            attT[m, e, :, cols] = attended.astype(BF16)
            rl[m, e : e + 1, cols] = inverse
            hT[m, e * hs : (e + 1) * hs, cols] = (gate[m, e : e + 1, cols] * attended).astype(BF16)
            scores = ahead
            if c == 1:
                pump(pumps)

    def attend_back(m, dout, wo, pumps=1):
        dH = mm(wa[wo, :], dout, NT).astype(BF16)
        go = mm(hT[m], dout)
        work[0:QR, 0:R] = dH.astype(F32)

        C = R // 2

        def start(e):
            span = slice(e * hs, (e + 1) * hs)
            dh = work[span, 0:R]
            dg = jnp.sum(dh * attT[m, e].astype(F32), 0, keepdims=True)
            g = gate[m, e : e + 1, :]
            inverse = rl[m, e : e + 1, :]
            gate[m, experts + e : experts + e + 1, :] = dg
            da = (dh * (g * inverse)).astype(BF16)
            delta = g * dg * inverse
            high = delta.astype(BF16).astype(F32)
            row = lax.broadcasted_iota(jnp.int32, (16, R), 0)
            dA[e % 2, 0:hs, :] = da
            dA[e % 2, hs : hs + 16, :] = jnp.where(
                row == 0, -high, jnp.where(row == 1, high - delta, 0.0)
            ).astype(BF16)

        def slopes(e, c):
            if c == 0:
                start(e)
            return mm(vA[m], dA[e % 2, :, c * C : (c + 1) * C])

        items = [(e, c) for e in range(experts) for c in range(2)]
        x = slopes(*items[0])
        for i, (e, c) in enumerate(items):
            cols = slice(c * C, (c + 1) * C)
            ahead = slopes(*items[i + 1]) if i + 1 < len(items) else None
            p = prob[m, e, :, :, :, :, :, cols].reshape(T, C)
            ds = (p.astype(F32) * x).astype(BF16)
            dT[m, e * hs : (e + 1) * hs, cols] = (mm(kT[m, 0:hs, :], ds) * scale).astype(BF16)
            dk, dv = mm(qT[m, e, :, cols], ds, NT) * math.log(2.0), mm(dA[e % 2, 0:hs, cols], p, NT)
            if i == 0:
                dkv[0:hs, :], dkv[hs : 2 * hs, :] = dk, dv
            else:
                dkv[0:hs, :] += dk
                dkv[hs : 2 * hs, :] += dv
            x = ahead
            if c == 1:
                pump(pumps[e] if isinstance(pumps, tuple) else pumps)

        g = gate[m, 0:experts, :]
        dg = gate[m, experts : 2 * experts, :]
        dl = g * (dg - jnp.sum(g * dg, 0, keepdims=True))
        dT[m, QR : QR + 16, :] = jnp.concatenate(
            [dl, jnp.zeros((16 - experts, R), F32)], 0
        ).astype(BF16)
        return go

    def ffn_cols(mat, i):
        n = FFH // FC
        cols = pl.ds(pl.multiple_of(i % n * FC, FC), FC)
        return ffn[mat, i // n, :, :, :, :, cols].reshape(W, FC)

    def feed(m, out, i, start=None):
        c0 = math.sqrt(2.0 / math.pi)
        cols = pl.ds(pl.multiple_of(i * FC, FC), FC)
        u = mm(fa[m], ffn_cols(0, i))
        u2 = u * u
        t = jnp.tanh(c0 * u * (1.0 + 0.044715 * u2))
        half_up = 0.5 * (1.0 + t)
        a = (u * half_up).astype(BF16)
        act[m, :, cols] = a
        gp[m, :, cols] = (
            half_up + 0.5 * u * (1.0 - t * t) * (c0 * (1.0 + 3 * 0.044715 * u2))
        ).astype(BF16)
        part = mm(a, ffn_cols(1, i), NT)
        if start is None:
            out[...] += part
        else:
            out[...] = start[m] + part

    def feed_back(m, dout, out):
        def body(i, carry):
            cols = pl.ds(pl.multiple_of(i * FC, FC), FC)
            dh = mm(dout[...], ffn_cols(1, i))
            dh = (dh * gp[m, :, cols].astype(F32)).astype(BF16)
            gp[m, :, cols] = dh
            part = mm(dh, ffn_cols(0, i), NT)

            @pl.when(i == 0)
            def _():
                out[...] = part

            @pl.when(i > 0)
            def _():
                out[...] += part

            return carry

        lax.fori_loop(0, 2 * FFH // FC, body, 0)

    def norm_back_into(x, k, dz, add, outs):
        g = gain(k)

        def body(c):
            dx, dg = norm_back(x[c, :].astype(F32), g, dz[c, :])
            gacc[k : k + 1, :] += dg
            total = dx if add is None else add[c, :].astype(F32) + dx
            for out in outs:
                out[c, :] = total.astype(out.dtype)

        chunks(R, LC, body)

    def grad_block(b, t):
        gd[b] = t.T.astype(BF16).reshape(nz, 2, 2, Dh, 128)

    def summed(parts):
        total = parts[0][...].astype(F32)
        for part in parts[1:]:
            total = total + part[...].astype(F32)
        return total.astype(BF16)

    mt = block(MISC)
    wa[rows.r, :], wa[rows.cr, :], wa[rows.gain, :] = mt[0:16], mt[16:32], mt[32:48]
    wa[rows.kv, :] = block(KV)
    head_rows(rows.q, 0, 2)

    def project(m, slot, x, named):
        norm_to(x, a1.at[m], 0)
        kvs[slot] = mm(wa[rows.kv, :], a1[m], NT).astype(BF16)
        copy = exchange(slot)
        z = mm(wa[rows.self_in, :], a1[m], NT)
        qT[m] = (z[0:QR].astype(BF16).astype(F32) * base2).astype(BF16).reshape(experts, hs, R)
        gates(m, named[...].astype(F32), z[QR + 2 * hs :])
        set_keys(m, kvs.at[slot], lens[m, s].astype(F32), 0)
        return copy

    here, there = s, 1 - s
    mine_copy.wait()
    kv_here = project(here, 0, mine, msk.at[s])
    pump()
    for copy in tokens_in:
        copy.wait_recv()
    kv_there = project(there, 1, other, omsk)
    pump(2)
    for m, slot, copy in ((here, 0, kv_here), (there, 1, kv_there)):
        copy.wait_recv()
        set_keys(m, kvr.at[slot], lens[m, s].astype(F32), 1)
        attend(m, (1 - m) * T)
    until("o")
    head_rows(rows.o, 1, 3)
    for m, x in ((here, mine), (there, other)):
        mid[m] = x[...].astype(F32) + mm(hT[m], wa[rows.o, :], TN)
    norm_to(mid.at[ENC], fa.at[ENC], 1)
    n = FFH // FC
    for k, name in enumerate(("end10", "end30", "end11", "end31")):
        until(name)
        h = half if k < 2 else 1 - half
        feed(ENC, top.at[ENC], h * n + k % 2, mid if k == 0 else None)
    until("cross")
    head_rows(rows.cq, CROSSED, CROSSED + 3)
    head_rows(rows.co, CROSSED + 1, CROSSED + 4)
    wa[rows.ckv, :] = block(CKV)
    weight_copies = list(started)
    norm_to(top.at[ENC], mem, 2)
    kvs[2] = mm(wa[rows.ckv, :], mem[...], NT).astype(BF16)
    kv_cross = exchange(2)
    norm_to(mid.at[DEC], b2, 3)
    z = mm(wa[rows.cross_in, :], b2[...], NT)
    qT[CROSS] = (z[0:QR].astype(BF16).astype(F32) * base2).astype(BF16).reshape(experts, hs, R)
    gates(CROSS, xmask, z[QR:])
    set_keys(CROSS, kvs.at[2], lens[0, s].astype(F32), 0)
    kv_cross.wait_recv()
    set_keys(CROSS, kvr.at[2], lens[0, s].astype(F32), 1)
    attend(CROSS, None)
    top[DEC] = mid[DEC] + mm(hT[CROSS], wa[rows.co, :], TN)
    norm_to(top.at[DEC], fa.at[DEC], 1)
    work[...] = top[DEC]

    for i in range(2 * n):
        feed(DEC, work, i)
    first = s == 0
    y = work[...].astype(BF16)
    sent[0] = jnp.where(first, mem[...], y)
    sent[1] = jnp.where(first, y, mem[...])
    rows_copy = pltpu.make_async_copy(sent.at[0], out_rows.at[s], csem.at[1])
    rows_copy.start()
    rows_in = push(sent.at[1], out_rows.at[s], to_x)

    sent_off(weight_copies)
    gd = wd
    ct_copy.wait()
    feed_back(DEC, ct, work)
    norm_back_into(top.at[DEC], 1, work, ct, (top.at[DEC], workb.at[DEC]))
    go = attend_back(CROSS, workb[DEC], rows.co)
    sent_off((kv_here, kv_there, kv_cross))
    kvs[0] = dkv[:, R:T].astype(BF16)
    back_cross = exchange(3)
    grad_block(CROSSED + 1, go[0:128])
    grad_block(CROSSED + 4, go[128:256])
    t = mm(dT[CROSS, 0 : QR + 16, :], b2[...])
    grad_block(CROSSED, t[0:128])
    grad_block(CROSSED + 3, t[128:256])
    gaT[16:32, :] = t[QR : QR + 16]
    work[...] = mm(dT[CROSS, 0 : QR + 16, :], wa[rows.cross_in, :], TN)
    norm_back_into(mid.at[DEC], 3, work, top.at[DEC], (top.at[DEC], workb.at[DEC]))
    back_cross.wait_recv()
    dkvc = (dkv[:, 0:R] + kvr[3].astype(F32)).astype(BF16)
    grad_block(CKV, mm(dkvc, mem[...]))

    def reduce_small(base, nb, st, n, at, place):
        mine_at, far_at = base + st * half, base + st * (1 - half)
        spare = slice(at, at + n)
        come = {}

        def p1():
            come["c"] = push(gd.at[base : base + nb, :, 1 - core], sc.at[base : base + nb], to_c)

        def p2():
            come["c"].wait_recv()
            own = gd.at[base : base + nb, :, core]
            own[...] = summed([own, sc.at[base : base + nb]])
            come["p"] = [
                push(gd.at[pl.ds(b, n), :, core, hs_], sxy.at[k, spare], peer)
                for k, (b, hs_, peer) in enumerate(
                    ((mine_at, 1 - s, to_x), (far_at, s, to_y), (far_at, 1 - s, to_xy))
                )
            ]

        def p3():
            for copy in come["p"]:
                copy.wait_recv()
            pair = gd[pl.ds(mine_at, n), :, core, s].astype(F32) + sxy[0, spare].astype(F32)
            far = sxy[1, spare].astype(F32) + sxy[2, spare].astype(F32)
            sg[spare] = (pair + far).astype(BF16)
            come["z"] = [
                push(sg.at[spare, (zv + j) % nz], sz.at[spare, s, j], peer)
                for j, peers in enumerate(zip([None] + to_z, [to_x] + to_xz))
                for peer in peers
                if peer is not None
            ]

        def p4():
            for copy in come["z"]:
                copy.wait_recv()
            sz[spare, s, 0] = sg[spare, zv]
            total = sz[spare, :, 0].astype(F32)
            for j in range(1, nz):
                total = total + sz[spare, :, j].astype(F32)
            for k in range(n):
                g_small[place(k)] = total[k].astype(BF16)

        return [("small", p) for p in (p1, p2, p3, p4)]

    def reduce_split(base, nb, n, at, place):
        mine_at, far_at = base + 2 * half, base + 2 * (1 - half)
        spare = slice(at, at + n)
        come = {}

        def p1():
            come["c"] = push(gd.at[base : base + nb, :, 1 - core], sc.at[base : base + nb], to_c)

        def p2():
            come["c"].wait_recv()
            own = gd.at[base : base + nb, :, core]
            own[...] = summed([own, sc.at[base : base + nb]])
            come["y"] = push(gd.at[pl.ds(far_at, n), :, core], sy.at[spare], to_y)

        def p3():
            come["y"].wait_recv()
            sy[spare] = summed([gd.at[pl.ds(mine_at, n), :, core], sy.at[spare]])
            come["z"] = [
                push(sy.at[spare, (zv + j) % nz], sz.at[at : at + n, :, j], to_z[j - 1])
                for j in range(1, nz)
            ]

        def p4():
            wait_all(come["z"])
            sz[spare, :, 0] = sy[spare, zv]
            xs[0, spare] = summed([sz.at[spare, :, j] for j in range(nz)])
            come["x"] = push(xs.at[0, spare], xs.at[1, spare], to_x)

        def p5():
            come["x"].wait_recv()
            total = summed([xs.at[0, spare], xs.at[1, spare]])
            for k in range(n):
                g_small[place(k)] = total[k]

        return [("small", p) for p in (p1, p2, p3, p4, p5)]

    def reduce_ffn(i):
        cols = slice(i * CW, (i + 1) * CW)
        come = {}

        def rc(i):
            return prob.at[CROSS, i, :, :, :, :, 0:Dh, 0:CW]

        ways = ("yzx" if i == NC - 2 else "xyz", "yzx")

        def p1():
            come["c"] = push(ffn.at[:, :, :, 1 - core, :, :, cols], rc(i), to_c)

        def p2():
            come["c"].wait_recv()
            own = ffn.at[:, :, :, core, :, :, cols]
            own[...] = summed([own, rc(i)])
            for mat in (0, 1):
                if ways[mat] == "xyz":
                    given = ffn.at[mat, :, :, core, 1 - s, :, cols]
                    come[mat] = push(given, rx.at[min(i, NC - 2)], to_x)
                else:
                    given = ffn.at[mat, 1 - half, :, core, :, :, cols]
                    come[mat] = push(given, ry.at[i if mat else NC], to_y)

        def z_push(mat, side, to):
            return [
                push(ffn.at[mat, half, (zv + j) % nz, core, side, :, cols], to.at[j - 1], to_z[j - 1])
                for j in range(1, nz)
            ]

        def p3():
            for mat in (0, 1):
                come[mat].wait_recv()
                if ways[mat] == "xyz":
                    own = ffn.at[mat, :, :, core, s, :, cols]
                    own[...] = summed([own, rx.at[min(i, NC - 2)]])
                    given = ffn.at[mat, 1 - half, :, core, s, :, cols]
                    come[mat] = [push(given, r2.at[i], to_y)]
                else:
                    own = ffn.at[mat, half, :, core, :, :, cols]
                    own[...] = summed([own, ry.at[i if mat else NC]])
                    come[mat] = z_push(mat, slice(None), rz.at[i, mat])

        def z_sum(mat, side, out):
            out[...] = summed(
                [ffn.at[mat, half, zv, core, side, :, cols]]
                + [rz.at[i, mat, j, side] for j in range(nz - 1)]
            )

        def p4():
            for mat in (0, 1):
                wait_all(come[mat])
                if ways[mat] == "xyz":
                    own = ffn.at[mat, half, :, core, s, :, cols]
                    own[...] = summed([own, r2.at[i]])
                    come[mat] = z_push(mat, s, rz.at[i, mat, :, s])
                else:
                    z_sum(mat, slice(None), zx.at[i, mat, 0])
                    come[mat] = [push(zx.at[i, mat, 0], zx.at[i, mat, 1], to_x)]

        def p5():
            for mat in (0, 1):
                wait_all(come[mat])
                if ways[mat] == "xyz":
                    z_sum(mat, s, fin.at[mat, s, :, cols])
                    come[mat] = [same(fin.at[mat, s, :, cols], to_x)]
                else:
                    fin[mat, :, :, cols] = summed([zx.at[i, mat, 0], zx.at[i, mat, 1]])
                    come[mat] = []

        def p6():
            for mat in (0, 1):
                wait_all(come[mat])

        return [("p%d%d" % (k + 1, i), p) for k, p in enumerate((p1, p2, p3, p4, p5, p6))]

    def reduce_misc():
        come = {}

        def p1():
            come["c"] = push(ms.at[0], ms.at[1], to_c)

        def p2():
            come["c"].wait_recv()
            ms[2] = summed([ms.at[0], ms.at[1]])
            come["p"] = [
                push(ms.at[2], ms.at[3 + k], peer) for k, peer in enumerate((to_x, to_y, to_xy))
            ]

        def p3():
            wait_all(come["p"])
            pair = ms[2].astype(F32) + ms[3].astype(F32)
            far = ms[4].astype(F32) + ms[5].astype(F32)
            mz[zv] = (pair + far).astype(BF16)
            come["z"] = [same(mz.at[zv], peer) for peer in to_z]

        def p4():
            wait_all(come["z"])
            g_misc[...] = summed([mz.at[j] for j in range(nz)])

        return [("misc", p) for p in (p1, p2, p3, p4)]

    cross_sum = reduce_split(CROSSED, 5, 3, 3, lambda k: 3 + (k + 2 * half) % 3)
    cross_sum[0][1]()
    work[...] = mm(dkvc, wa[rows.ckv, :], TN).astype(BF16).astype(F32)
    norm_back_into(top.at[ENC], 2, work, None, (top.at[ENC], workb.at[ENC]))
    cross_sum[1][1]()
    feed_back(ENC, workb.at[ENC], work)

    waves = [reduce_ffn(i) for i in range(NC)]
    p1, p2, p3, p4, p5, p6 = ([wave[k] for wave in waves] for k in range(6))

    def weight_grads(i):
        for hh in (0, 1):
            at = hh * FFH + i * CW
            cols, to = slice(at, at + CW), slice(i * CW, (i + 1) * CW)
            shape = (nz, 2, 2, Dh, CW)
            up = mm(fa[ENC], gp[ENC, :, cols], TN) + mm(fa[DEC], gp[DEC, :, cols], TN)
            ffn[0, hh, :, :, :, :, to] = up.astype(BF16).reshape(shape)
            down = mm(dout_enc[...], act[ENC, :, cols], TN) + mm(ct[...], act[DEC, :, cols], TN)
            ffn[1, hh, :, :, :, :, to] = down.astype(BF16).reshape(shape)
        run(p1[i])

    def run(*events):
        for _, event in events:
            event()

    dout_enc = b2
    dout_enc[...] = workb[ENC]
    for i in range(NC // 2):
        weight_grads(i)
        if i > 0:
            run(p2[i - 1])
    norm_back_into(mid.at[ENC], 1, work, top.at[ENC], (top.at[ENC], workb.at[ENC]))
    run(p2[NC // 2 - 1])

    at_r, at_kv = QR, QR + 16
    kv_rows = slice(at_kv, at_kv + 2 * hs)

    def self_back(m, slot, pumps):
        go = attend_back(m, workb[m], rows.o, pumps)
        kvs[slot % 3] = dkv[:, R:T].astype(BF16)
        return go, exchange(slot)

    def inner(m, slot, copy):
        copy.wait_recv()
        dT[m, kv_rows, :] = (dkv[:, 0:R] + kvr[slot].astype(F32)).astype(BF16)
        work[...] = (
            mm(dT[m, 0:at_r, :], wa[rows.q, :], TN)
            + mm(dT[m, at_r:at_kv, :], wa[rows.r, :], TN)
            + mm(dT[m, kv_rows, :], wa[rows.kv, :], TN)
        )

    queue += [cross_sum[2], p3[0]]
    go, copy_there = self_back(there, 4, (0, 1, 0, 1))
    mid[DEC, 0:QR, :] = go
    for i in range(NC // 2, NC):
        weight_grads(i)
        if i > NC // 2:
            run(p2[i - 1])
    run(p3[1], p2[NC - 1])
    inner(there, 4, copy_there)
    sent_off([rows_in])
    norm_back_into(other, 0, work, top.at[there], (sent.at[1],))
    grads_in = push(sent.at[1], came, to_x)
    queue += [cross_sum[3], p3[2], p4[0], p3[3]]
    go, copy_here = self_back(here, 5, (0, 1, 1, 2))
    go = go + mid[DEC, 0:QR, :]
    grad_block(SELF + 1, go[0:128])
    grad_block(SELF + 3, go[128:256])
    t = mm(dT[ENC, 0:at_kv, :], a1[ENC]) + mm(dT[DEC, 0:at_kv, :], a1[DEC])
    grad_block(SELF, t[0:128])
    grad_block(SELF + 2, t[128:256])
    self_sum = reduce_split(SELF, 4, 2, 0, lambda k: k)
    run(self_sum[0], p4[1], self_sum[1])
    inner(here, 5, copy_here)
    grad_block(KV, mm(dT[ENC, kv_rows, :], a1[ENC]) + mm(dT[DEC, kv_rows, :], a1[DEC]))
    kv_sum = reduce_small(KV, 1, 0, 1, 2, lambda k: 2 + k)
    run(kv_sum[0])
    norm_back_into(mine, 0, work, top.at[here], (mid.at[here],))
    grads_copy = pltpu.make_async_copy(mid.at[here], out_grads.at[s], csem.at[0])
    grads_copy.start()
    ms[0] = jnp.concatenate(
        [t[at_r : at_r + 4], gaT[16:20, :], gacc[0:4, :], jnp.zeros((4, W), F32)], 0
    ).astype(BF16)
    misc_sum = reduce_misc()
    run(misc_sum[0], kv_sum[1], misc_sum[1], p4[2], p5[0], p4[3], p5[1], self_sum[2])
    run(kv_sum[2], misc_sum[2], p5[2], p5[3], self_sum[3], cross_sum[4])
    grads_in.wait_recv()
    mid[there] = came[...].astype(F32)
    far_copy = pltpu.make_async_copy(mid.at[there], out_grads.at[1 - s], csem.at[2])
    far_copy.start()
    run(kv_sum[3], misc_sum[3], self_sum[4], *p6)
    rows_in.wait_recv()
    rows_copy.wait()
    grads_copy.wait()
    far_copy.wait()
    sent_off(started)


def outputs_kernel(
    el, hs, experts, rows_in, grads_in, small_in, misc, ffn_in,
    rows, grads, n0, n1, n2, n3, gr, gq, gk, gv, go, gup, gdown, gcr, gcq, gck, gcv, gco, small, ffn, sem,
):
    copies = [
        pltpu.make_async_copy(rows_in, rows.at[0], sem.at[0]),
        pltpu.make_async_copy(grads_in, grads.at[0], sem.at[1]),
        pltpu.make_async_copy(ffn_in, ffn, sem.at[2]),
        pltpu.make_async_copy(small_in, small, sem.at[3]),
    ]
    for copy in reversed(copies):
        copy.start()
    copies.pop().wait()
    q, o, kv, cq, co, ckv = (small[k].astype(F32) for k in range(6))
    for ref, value in ((gq, q), (gcq, cq)):
        for e in range(el):
            ref[e] = value[:, e * hs : (e + 1) * hs]
    for ref, value in ((go, o), (gco, co)):
        ref[...] = value.T.reshape(ref.shape)
    gk[...], gv[...], gck[...], gcv[...] = kv[:, 0:hs], kv[:, hs:], ckv[:, 0:hs], ckv[:, hs:]
    D, W = n0.shape[1], misc.shape[1]
    feature = lax.broadcasted_iota(jnp.int32, (W, D), 0) - lax.axis_index("dp") * D
    chosen = jnp.where(feature == lax.broadcasted_iota(jnp.int32, (W, D), 1), 1.0, 0.0)
    own = mm(misc[...], chosen.astype(BF16))
    gr[...], gcr[...] = own[0:experts], own[4 : 4 + experts]
    for k, ref in enumerate((n0, n1, n2, n3)):
        ref[...] = own[8 + k : 9 + k, :]
    copies.pop().wait()
    gup[...] = ffn[0].astype(F32)
    gdown[...] = ffn[1].astype(F32)
    for copy in copies:
        copy.wait()


def run_layers(experts, hs, nz, zs, tok, routes, xroutes, lens, ct, weights):
    _, R, W = tok.shape
    FFH = weights[9].shape[1]
    Dh = W // (4 * nz)
    T, QR, NC = 2 * R, experts * hs, 4
    CW = FFH // NC
    vm = pltpu.VMEM
    dma = pltpu.SemaphoreType.DMA
    any_, whole = pl.BlockSpec(memory_space=pl.ANY), pl.BlockSpec(memory_space=vm)
    scalars = pl.BlockSpec(memory_space=pltpu.SMEM)
    return pl.pallas_call(
        functools.partial(layer_kernel, experts, hs, zs),
        out_shape=(
            jax.ShapeDtypeStruct((2, R, W), BF16),
            jax.ShapeDtypeStruct((2, R, W), F32),
            jax.ShapeDtypeStruct((6, 2, Dh, 128), BF16),
            jax.ShapeDtypeStruct((16, W), BF16),
            jax.ShapeDtypeStruct((2, 2, Dh, FFH), BF16),
        ),
        in_specs=[any_, whole, whole, scalars, any_] + [whole] * len(weights),
        out_specs=[any_, any_, whole, whole, whole],
        scratch_shapes=[
            vm((R, W), BF16),
            vm((R, W), BF16),
            vm((2, 16, R), BF16),
            vm((16, R), BF16),
            vm((R, W), BF16),
            vm((BLOCKS, nz, 2, 2, Dh, 128), BF16),
            vm((Rows(QR, hs).total, W), BF16),
            vm((2, 2, nz, 2, 2, Dh, FFH), BF16),
            vm((2, R, W), BF16),
            vm((3, experts, hs, R), BF16),
            vm((3, hs, T), BF16),
            vm((3, hs + 16, T), BF16),
            vm((3, T, 128), BF16),
            vm((3, T, 128), BF16),
            vm((2, 128, R), BF16),
            vm((2, 128, R), BF16),
            vm((3, 2 * experts, R), F32),
            vm((3, experts, 2, 2, nz, 2, T // (8 * nz), R), BF16),
            vm((3, experts, hs, R), BF16),
            vm((3, 8, R), F32),
            vm((3, QR, R), BF16),
            vm((3, QR + 16 + 2 * hs, R), BF16),
            vm((2 * hs, T), F32),
            vm((2, R, W), F32),
            vm((2, R, W), F32),
            vm((2, R, W), BF16),
            vm((R, W), BF16),
            vm((R, W), BF16),
            vm((2, R, 2 * FFH), BF16),
            vm((2, R, 2 * FFH), BF16),
            vm((R, W), F32),
            vm((2, R, W), BF16),
            vm((16, W), F32),
            vm((32, W), F32),
            vm((3, 2 * hs, R), BF16),
            vm((6, 2 * hs, R), BF16),
            vm((2, R, W), BF16),
            vm((R, W), BF16),
            vm((NC - 1, 2, nz, Dh, CW), BF16),
            vm((NC + 1, nz, 2, Dh, CW), BF16),
            vm((NC, nz, Dh, CW), BF16),
            vm((NC, 2, max(nz - 1, 1), 2, Dh, CW), BF16),
            vm((NC, 2, 2, 2, Dh, CW), BF16),
            vm((6, 16, W), BF16),
            vm((nz, 16, W), BF16),
            vm((BLOCKS, nz, 2, Dh, 128), BF16),
            vm((3, 3, nz, Dh, 128), BF16),
            vm((3, nz, Dh, 128), BF16),
            vm((6, nz, 2, Dh, 128), BF16),
            vm((2, 6, 2, Dh, 128), BF16),
            vm((6, 2, nz, Dh, 128), BF16),
            dma((200,)),
            dma((200,)),
            dma((3,)),
        ],
        compiler_params=pltpu.CompilerParams(
            collective_id=0, has_side_effects=True, vmem_limit_bytes=63 * 2**20
        ),
    )(tok, routes, xroutes, lens, ct, *weights)


def on_device(
    tokens, self_routes, cross_routes, lengths, cotangent,
    norm_attn, norm_ffn, norm_final, norm_cross,
    router, query_weight, key_weight, value_weight, output_weight, up_weight, down_weight,
    cross_router, cross_query, cross_key, cross_value, cross_output,
):
    dp = lax.axis_size("dp")
    R, W = tokens.shape[2:]
    el, D, hs = query_weight.shape
    experts = el * lax.axis_size("head")
    FFH = up_weight.shape[1]
    nz = min(4, dp // 2)
    zs = dp // nz
    Dv = W // (2 * nz)
    blocks = [[z * zs + j for j in range(zs)] for z in range(nz)]
    core = lax.axis_index("dp") % 2

    def widened(a, axis):
        if zs == 2:
            return a
        a = lax.all_gather(a, "dp", axis=axis, tiled=True, axis_index_groups=blocks)
        return lax.dynamic_slice_in_dim(a, core * Dv, Dv, axis)

    def narrowed(a):
        if zs == 2:
            return a
        wide = jnp.zeros((a.shape[0], 2 * Dv, a.shape[2]), BF16)
        wide = lax.dynamic_update_slice_in_dim(wide, a, core * Dv, 1)
        return lax.psum_scatter(
            wide, "dp", scatter_dimension=1, axis_index_groups=blocks, tiled=True
        )

    gains = (norm_attn, norm_ffn, norm_final, norm_cross)
    weights = [widened(g, 0).reshape(1, Dv) for g in gains]
    weights += [
        widened(w, axis)
        for w, axis in (
            (router.T, 1), (query_weight, 1), (key_weight, 0), (value_weight, 0),
            (output_weight, 2), (up_weight, 0), (down_weight.T, 0),
            (cross_router.T, 1), (cross_query, 1), (cross_key, 0), (cross_value, 0),
            (cross_output, 2),
        )
    ]
    out, grads, small, misc, ffn = run_layers(
        experts, hs, nz, zs, tokens[0],
        jnp.swapaxes(self_routes[0], 1, 2), jnp.swapaxes(cross_routes, 1, 2),
        lengths[:, :, 0], cotangent, weights,
    )
    small = narrowed(small.reshape(6, Dv, 128))
    ffn = narrowed(ffn.reshape(2, Dv, FFH))

    def f32(*shape):
        return jax.ShapeDtypeStruct(shape, F32)

    whole = pl.BlockSpec(memory_space=pltpu.VMEM)
    attention = (
        f32(experts, D), f32(el, D, hs), f32(D, hs), f32(D, hs), f32(el, hs, D),
    )
    done = pl.pallas_call(
        functools.partial(outputs_kernel, el, hs, experts),
        out_shape=(
            jax.ShapeDtypeStruct((1, 2, R, W), BF16), f32(1, 2, R, W),
            *(f32(1, D),) * 4, *attention, *(f32(D, FFH),) * 2, *attention,
        ),
        in_specs=[pl.BlockSpec(memory_space=pltpu.HBM)] * 3 + [whole, pl.BlockSpec(memory_space=pltpu.HBM)],
        out_specs=[whole] * 18,
        scratch_shapes=[
            pltpu.VMEM(small.shape, BF16), pltpu.VMEM(ffn.shape, BF16), pltpu.SemaphoreType.DMA((4,)),
        ],
        compiler_params=pltpu.CompilerParams(vmem_limit_bytes=60 * 2**20),
    )(out, grads, small, misc, ffn)
    rows, grads, n0, n1, n2, n3, gr, gq, gk, gv, go, gup, gdown, gcr, gcq, gck, gcv, gco = done
    return (
        rows, grads, *(g.reshape(D) for g in (n0, n1, n2, n3)),
        gr.T, gq, gk, gv, go, gup, gdown.T, gcr.T, gcq, gck, gcv, gco,
    )


def solution(mesh):
    rows = P("section", None, ("dp", "head"), None)
    vector, tall = P("dp"), P("dp", None)
    query, out = P("head", "dp", None), P("head", None, "dp")
    weights = (
        vector, vector, vector, vector,
        tall, query, tall, tall, out, P("dp", "head"), P("head", "dp"),
        tall, query, tall, tall, out,
    )
    return jax.shard_map(
        on_device,
        mesh=mesh,
        in_specs=(
            rows, P("section", None, "dp", None), P(None, "dp", None), P(None, None, "dp"),
            P(None, ("dp", "head"), None), *weights,
        ),
        out_specs=(rows, rows, *weights),
        check_vma=False,
    )
```

```python
import functools
import math

import jax
import jax.numpy as jnp
from jax import lax
from jax.experimental import pallas as pl
from jax.experimental.pallas import tpu as pltpu
from jax.sharding import PartitionSpec as P

EPSILON = 1e-05
FAR = -1e30
F32 = jnp.float32
BF16 = jnp.bfloat16
MESH = pl.DeviceIdType.MESH
NN = (((1,), (0,)), ((), ()))
NT = (((1,), (1,)), ((), ()))
TN = (((0,), (0,)), ((), ()))


def mm(a, b, dims=NN):
    return lax.dot_general(a, b, dims, preferred_element_type=F32)


def chunks(total, size, body):
    def step(i, carry):
        body(pl.ds(pl.multiple_of(i * size, size), size))
        return carry

    lax.fori_loop(0, total // size, step, 0)


def norm_parts(x):
    centred = x - jnp.mean(x, -1, keepdims=True)
    rstd = lax.rsqrt(jnp.mean(centred * centred, -1, keepdims=True) + EPSILON)
    return centred * rstd, rstd


def norm_back(x, gain, dz):
    xhat, rstd = norm_parts(x)
    dxh = dz * gain
    dx = (
        dxh
        - jnp.mean(dxh, -1, keepdims=True)
        - xhat * jnp.mean(dxh * xhat, -1, keepdims=True)
    ) * rstd
    return dx, jnp.sum(dz * xhat, 0, keepdims=True)


class Rows:
    def __init__(self, q, h):
        at = 0
        for name, size in (
            ("q", q), ("kv", 2 * h), ("r", 16), ("o", q),
            ("cq", q), ("cr", 16), ("ckv", 2 * h), ("co", q), ("gain", 16),
        ):
            setattr(self, name, slice(at, at + size))
            at += size
        self.total = at
        self.self_in = slice(self.q.start, self.r.stop)
        self.cross_in = slice(self.cq.start, self.cr.stop)


SELF, SHARED, CROSSED, BLOCKS = 0, 4, 6, 11
KV, MISC, CKV = 4, 5, 8


def layer_kernel(
    experts, hs, zs,
    tok, routes, xroutes, lens, ct_hbm,
    g0, g1, g2, g3, wr, wq, wk, wv, wo, wup, wdown, wcr, wcq, wck, wcv, wco,
    out_rows, out_grads, g_small, g_misc, fin,
    mine, other, msk, omsk, ct, wd, wa, ffn, a1, qT, kT, vT, kA, vA, qA, dA, gate, prob, attT, rl,
    hT, dT, dkv, mid, top, fa, b2, mem, act, gp, work, workb, gacc, gaT, kvs, kvr, sent, came,
    rx, ry, r2, rz, zx, ms, mz, sc, sxy, sg, sy, xs, sz, ssem, rsem, csem,
):
    R, W = mine.shape
    T = 2 * R
    FFH = ffn.shape[-1]
    nz, Dh = ffn.shape[2], ffn.shape[5]
    Dv = 2 * Dh
    QR = experts * hs
    rows = Rows(QR, hs)
    LC, FC = 256, 512
    NC = r2.shape[0]
    CW = FFH // NC
    ENC, DEC, CROSS = 0, 1, 2
    scale = 1.0 / math.sqrt(hs)
    base2 = scale * math.log2(math.e)

    s, d, half = lax.axis_index("section"), lax.axis_index("dp"), lax.axis_index("head")
    zv, core = d // zs, d % 2
    to_x, to_y = {"section": 1 - s}, {"head": 1 - half}
    to_xy = {"section": 1 - s, "head": 1 - half}
    to_c = {"dp": d + 1 - 2 * core}
    dz = [(zv + k) % nz * zs + d % zs for k in range(1, nz)]
    to_z = [{"dp": k} for k in dz]
    to_xz = [{"section": 1 - s, "dp": k} for k in dz]

    barrier = pltpu.get_barrier_semaphore()
    everyone = [to_x, to_y, to_xy, to_c] + to_z + to_xz
    for peer in everyone:
        pl.semaphore_signal(barrier, inc=1, device_id=peer, device_id_type=MESH)

    mine_copy = pltpu.make_async_copy(tok.at[s], mine, csem.at[1])
    mine_copy.start()
    ct_copy = pltpu.make_async_copy(ct_hbm.at[s], ct, csem.at[0])
    ct_copy.start()

    def named(ref, m):
        two = ref[m, :, pl.ds(pl.multiple_of(half * R, R), R)]
        ids = lax.broadcasted_iota(jnp.int32, (16, R), 0)
        return jnp.where((two[0:1] == ids) | (two[1:2] == ids), 1.0, 0.0)

    for m in (0, 1):
        msk[m] = named(routes, m).astype(BF16)

    def beside(a, b):
        return jnp.concatenate([a.astype(F32), b.astype(F32)], 1).astype(BF16)

    def own_block(b, value):
        wd[b, zv, core] = value.reshape(2, Dh, 128)

    row = lax.broadcasted_iota(jnp.int32, (128, Dv), 0)
    misc = jnp.zeros((128, Dv), F32)
    for ref, at in ((wr, 0), (wcr, 16)):
        for e in range(experts):
            misc = jnp.where(row == at + e, ref[e : e + 1, :].astype(F32), misc)
    for k, ref in enumerate((g0, g1, g2, g3)):
        misc = jnp.where(row == 32 + k, ref[...].astype(F32), misc)
    q_own, q_far = SELF + 2 * half, SELF + 2 * (1 - half)
    c_own, c_far = CROSSED + 3 * half, CROSSED + 3 * (1 - half)
    own_block(KV, beside(wk[...], wv[...]))
    own_block(MISC, misc.T.astype(BF16))
    own_block(q_own, beside(wq[0], wq[1]))

    pl.semaphore_wait(barrier, len(everyone))

    started = []

    def push(src, dst, peer):
        k = len(started)
        copy = pltpu.make_async_remote_copy(
            src_ref=src, dst_ref=dst, send_sem=ssem.at[k], recv_sem=rsem.at[k],
            device_id=peer, device_id_type=MESH,
        )
        copy.start()
        started.append(copy)
        return copy

    def same(part, peer):
        return push(part, part, peer)

    left = []

    def sent_off(copies):
        for copy in copies:
            if not any(copy is c for c in left):
                copy.wait_send()
                left.append(copy)

    queue = []

    def pump(n=1):
        for _ in range(n):
            if queue:
                queue.pop(0)[1]()

    def until(name):
        while any(k == name for k, _ in queue):
            queue.pop(0)[1]()

    def gather(group, own, far, shared):
        copies = [
            same(wd.at[pl.ds(b, n), zv, core], peer) for peer in to_z for b, n in own + shared
        ]
        over = {}

        def of_core(b, n):
            return wd.at[pl.ds(b, n), :, core]

        def one():
            for copy in copies:
                copy.wait_recv()
            over["y"] = [same(of_core(*b), to_y) for b in own]
            over["c"] = [same(of_core(*b), to_c) for b in own + shared]

        def two():
            for copy in over["y"]:
                copy.wait_recv()
            over["c"] += [same(of_core(*b), to_c) for b in far]

        def three():
            for copy in over["c"]:
                copy.wait_recv()

        return [(group, one), (group, two), (group, three)]

    early = gather("early", [(q_own, 1)], [(q_far, 1)], [(KV, 2)])
    tokens_in = [push(tok.at[1 - s], other, to_x), push(msk.at[1 - s], omsk, to_x)]

    def turned(ref):
        return ref[...].astype(F32).reshape(QR // 2, Dv).T.astype(BF16)

    own_block(q_own + 1, turned(wo))
    own_block(CKV, beside(wck[...], wcv[...]))
    own_block(c_own, beside(wcq[0], wcq[1]))
    own_block(c_own + 1, turned(wco))
    ffn[0, half, zv, core] = wup[...].reshape(2, Dh, FFH)
    ffn[1, half, zv, core] = wdown[...].reshape(2, Dh, FFH)
    xmask = named(xroutes, s)

    NA = 4
    AW = FFH // NA
    others = [(zv + k) % nz for k in range(1, nz)]
    go_z, go_y, go_x, go_xf = {}, {}, {}, {}
    go_c = {(j, far): [] for j in range(NA) for far in (0, 1)}

    def part(mat, h, z, j):
        return ffn.at[mat, h, z, core, :, :, j * AW : (j + 1) * AW]

    def all_z(mat, h, j):
        return ffn.at[mat, h, :, core, :, :, j * AW : (j + 1) * AW]

    def wait_all(copies):
        for copy in copies:
            copy.wait_recv()

    def ffn_send(j):
        go_z[j] = [same(part(s, half, zv, j), peer) for peer in to_z]

    def ffn_on(j):
        def run():
            wait_all(go_z[j])
            go_y[j] = [same(part(s, half, k, j), to_y) for k in others]
            go_x[j] = [same(part(s, half, k, j), to_x) for k in others]
            go_c[j, 0].append(same(all_z(s, half, j), to_c))

        return ("on%d" % j, run)

    def ffn_swap(j):
        def run():
            wait_all(go_x[j])
            go_c[j, 0].append(same(all_z(1 - s, half, j), to_c))
            if j == NA - 1:
                go_xf[j] = [same(all_z(1 - s, half, j), to_y)]

        return ("swap%d" % j, run)

    def ffn_far(j):
        def run():
            if j == 0:
                ffn_own.wait_recv()
            wait_all(go_y[j])
            if j < NA - 1:
                go_xf[j] = [same(all_z(s, 1 - half, j), to_x)]
            go_c[j, 1].append(same(all_z(s, 1 - half, j), to_c))

        return ("far%d" % j, run)

    def ffn_far_swap(j):
        def run():
            wait_all(go_xf[j])
            go_c[j, 1].append(same(all_z(1 - s, 1 - half, j), to_c))

        return ("farswap%d" % j, run)

    def ffn_end(j, far):
        return ("end%d%d" % (j, far), lambda: wait_all(go_c[j, far]))

    ffn_send(0)
    out_weights = gather("o", [(q_own + 1, 1)], [(q_far + 1, 1)], [])
    for j in range(1, NA):
        ffn_send(j)
    cross_weights = gather("cross", [(c_own, 2)], [(c_far, 2)], [(CKV, 1)])
    early[0][1]()
    ffn_own = same(ffn.at[s, half, zv, core], to_y)
    early[1][1]()
    early[2][1]()
    o1, o2, o3 = out_weights
    c1, c2, c3 = cross_weights
    on, swap, far, far_swap = (
        [make(j) for j in range(NA)] for make in (ffn_on, ffn_swap, ffn_far, ffn_far_swap)
    )
    end = [(ffn_end(j, 0), ffn_end(j, 1)) for j in range(NA)]
    queue += [on[0], o1, on[1], on[2], swap[0], o2, far[0], on[3], swap[1], o3, far[1]]
    queue += [c1, end[0][0], end[1][0]]
    queue += [swap[2], swap[3], far[2], end[2][0], end[3][0]]
    queue += [far_swap[0], far_swap[1], far[3], end[0][1], end[1][1]]
    queue += [c2, far_swap[2], far_swap[3], end[2][1], end[3][1], c3]

    def block(b):
        return wd[b].reshape(W, 128).astype(F32).T.astype(BF16)

    def head_rows(part, b0, b1):
        n = (part.stop - part.start) // 2
        wa[part.start : part.start + n, :] = block(b0)
        wa[part.start + n : part.stop, :] = block(b1)

    def exchange(slot):
        return push(kvs.at[slot % 3], kvr.at[slot], to_y)

    def gain(k):
        at = rows.gain.start
        return wa[at : at + 16, :].astype(F32)[k : k + 1, :]

    def norm_to(source, out, k):
        g = gain(k)

        def body(c):
            xhat, _ = norm_parts(source[c, :].astype(F32))
            out[c, :] = (xhat * g).astype(BF16)

        chunks(R, R, body)

    def gates(m, named, logits):
        named = named[0:experts]
        l = jnp.where(named > 0, logits[0:experts], FAR)
        p = jnp.exp(l - jnp.max(l, 0, keepdims=True)) * named
        gate[m, 0:experts, :] = p / jnp.sum(p, 0, keepdims=True)

    def set_keys(m, pairs, length, far):
        keys = slice(far * R, (far + 1) * R)
        pos = lax.broadcasted_iota(jnp.int32, (1, R), 1) + (1 - half if far else half) * R
        outside = jnp.where(pos.astype(F32) < length, 0.0, FAR)
        sub = lax.broadcasted_iota(jnp.int32, (128 - hs, R), 0)
        for to, wide, at, rest in (
            (kT, kA, 0, jnp.where(sub == 0, outside, 0.0)),
            (vT, vA, hs, jnp.where(sub < 2, 1.0, 0.0)),
        ):
            part = pairs[at : at + hs, :]
            to[m, 0:hs, keys] = part
            wide[m, keys, :] = jnp.concatenate([part.astype(F32), rest], 0).T.astype(BF16)
        vT[m, hs : hs + 16, keys] = jnp.where(sub[0:16] < 2, 1.0, 0.0).astype(BF16)

    sub = lax.broadcasted_iota(jnp.int32, (128 - hs, R), 0)
    for k in (0, 1):
        qA[k, hs:128, :] = jnp.where(sub == 0, 1.0, 0.0).astype(BF16)
        dA[k, hs:128, :] = jnp.zeros((128 - hs, R), BF16)
    gacc[...] = jnp.zeros_like(gacc)

    def over_experts(one, pumps):
        for e in range(experts):
            one(e, 0)
            pump(pumps[e] if isinstance(pumps, tuple) else pumps)

    def attend(m, reach, pumps=1):
        C = R // 2
        items = [(e, c) for e in range(experts) for c in range(2)]

        def scores_of(e, c):
            cols = slice(c * C, (c + 1) * C)
            qA[e % 2, 0:hs, cols] = qT[m, e, :, cols]
            return mm(kA[m], qA[e % 2, :, cols])

        scores = scores_of(*items[0])
        for i, (e, c) in enumerate(items):
            cols = slice(c * C, (c + 1) * C)
            ahead = scores_of(*items[i + 1]) if i + 1 < len(items) else None
            if reach is not None:
                k = lax.broadcasted_iota(jnp.int32, (T, 1), 0)
                k = jnp.where(k < R, k + half * R, k - R + (1 - half) * R)
                q = lax.broadcasted_iota(jnp.int32, (1, C), 1) + half * R + reach + c * C
                scores = jnp.where(k <= q, scores, FAR)
            p = jnp.exp2(scores - jnp.max(scores, 0, keepdims=True)).astype(BF16)
            prob[m, e, :, :, :, :, :, cols] = p.reshape(prob.shape[2:-1] + (C,))
            out = mm(vT[m, 0 : hs + 16, :], p)
            inverse = 1.0 / out[hs : hs + 1, :]
            attended = out[0:hs, :] * inverse
            attT[m, e, :, cols] = attended.astype(BF16)
            rl[m, e : e + 1, cols] = inverse
            hT[m, e * hs : (e + 1) * hs, cols] = (gate[m, e : e + 1, cols] * attended).astype(BF16)
            scores = ahead
            if c == 1:
                pump(pumps)

    def attend_back(m, dout, wo, pumps=1):
        dH = mm(wa[wo, :], dout, NT).astype(BF16)
        go = mm(hT[m], dout)
        work[0:QR, 0:R] = dH.astype(F32)

        C = R // 2

        def start(e):
            span = slice(e * hs, (e + 1) * hs)
            dh = work[span, 0:R]
            dg = jnp.sum(dh * attT[m, e].astype(F32), 0, keepdims=True)
            g = gate[m, e : e + 1, :]
            inverse = rl[m, e : e + 1, :]
            gate[m, experts + e : experts + e + 1, :] = dg
            da = (dh * (g * inverse)).astype(BF16)
            delta = g * dg * inverse
            high = delta.astype(BF16).astype(F32)
            row = lax.broadcasted_iota(jnp.int32, (16, R), 0)
            dA[e % 2, 0:hs, :] = da
            dA[e % 2, hs : hs + 16, :] = jnp.where(
                row == 0, -high, jnp.where(row == 1, high - delta, 0.0)
            ).astype(BF16)

        def slopes(e, c):
            if c == 0:
                start(e)
            return mm(vA[m], dA[e % 2, :, c * C : (c + 1) * C])

        items = [(e, c) for e in range(experts) for c in range(2)]
        x = slopes(*items[0])
        for i, (e, c) in enumerate(items):
            cols = slice(c * C, (c + 1) * C)
            ahead = slopes(*items[i + 1]) if i + 1 < len(items) else None
            p = prob[m, e, :, :, :, :, :, cols].reshape(T, C)
            ds = (p.astype(F32) * x).astype(BF16)
            dT[m, e * hs : (e + 1) * hs, cols] = (mm(kT[m, 0:hs, :], ds) * scale).astype(BF16)
            dk, dv = mm(qT[m, e, :, cols], ds, NT) * math.log(2.0), mm(dA[e % 2, 0:hs, cols], p, NT)
            if i == 0:
                dkv[0:hs, :], dkv[hs : 2 * hs, :] = dk, dv
            else:
                dkv[0:hs, :] += dk
                dkv[hs : 2 * hs, :] += dv
            x = ahead
            if c == 1:
                pump(pumps[e] if isinstance(pumps, tuple) else pumps)

        g = gate[m, 0:experts, :]
        dg = gate[m, experts : 2 * experts, :]
        dl = g * (dg - jnp.sum(g * dg, 0, keepdims=True))
        dT[m, QR : QR + 16, :] = jnp.concatenate(
            [dl, jnp.zeros((16 - experts, R), F32)], 0
        ).astype(BF16)
        return go

    def ffn_cols(mat, i):
        n = FFH // FC
        cols = pl.ds(pl.multiple_of(i % n * FC, FC), FC)
        return ffn[mat, i // n, :, :, :, :, cols].reshape(W, FC)

    def feed(m, out, i, start=None):
        c0 = math.sqrt(2.0 / math.pi)
        cols = pl.ds(pl.multiple_of(i * FC, FC), FC)
        u = mm(fa[m], ffn_cols(0, i))
        u2 = u * u
        t = jnp.tanh(c0 * u * (1.0 + 0.044715 * u2))
        half_up = 0.5 * (1.0 + t)
        a = (u * half_up).astype(BF16)
        act[m, :, cols] = a
        gp[m, :, cols] = (
            half_up + 0.5 * u * (1.0 - t * t) * (c0 * (1.0 + 3 * 0.044715 * u2))
        ).astype(BF16)
        part = mm(a, ffn_cols(1, i), NT)
        if start is None:
            out[...] += part
        else:
            out[...] = start[m] + part

    def feed_back(m, dout, out):
        for i in range(2 * FFH // FC):
            cols = slice(i * FC, (i + 1) * FC)
            dh = mm(dout[...], ffn_cols(1, i))
            dh = (dh * gp[m, :, cols].astype(F32)).astype(BF16)
            gp[m, :, cols] = dh
            part = mm(dh, ffn_cols(0, i), NT)
            if i == 0:
                out[...] = part
            else:
                out[...] += part

    def norm_back_into(x, k, dz, add, outs):
        g = gain(k)

        def body(c):
            dx, dg = norm_back(x[c, :].astype(F32), g, dz[c, :])
            gacc[k : k + 1, :] += dg
            total = dx if add is None else add[c, :].astype(F32) + dx
            for out in outs:
                out[c, :] = total.astype(out.dtype)

        chunks(R, LC, body)

    def grad_block(b, t):
        gd[b] = t.T.astype(BF16).reshape(nz, 2, 2, Dh, 128)

    def summed(parts):
        total = parts[0][...].astype(F32)
        for part in parts[1:]:
            total = total + part[...].astype(F32)
        return total.astype(BF16)

    mt = block(MISC)
    wa[rows.r, :], wa[rows.cr, :], wa[rows.gain, :] = mt[0:16], mt[16:32], mt[32:48]
    wa[rows.kv, :] = block(KV)
    head_rows(rows.q, 0, 2)

    def project(m, slot, x, named):
        norm_to(x, a1.at[m], 0)
        kvs[slot] = mm(wa[rows.kv, :], a1[m], NT).astype(BF16)
        copy = exchange(slot)
        z = mm(wa[rows.self_in, :], a1[m], NT)
        qT[m] = (z[0:QR].astype(BF16).astype(F32) * base2).astype(BF16).reshape(experts, hs, R)
        gates(m, named[...].astype(F32), z[QR + 2 * hs :])
        set_keys(m, kvs.at[slot], lens[m, s].astype(F32), 0)
        return copy

    here, there = s, 1 - s
    mine_copy.wait()
    kv_here = project(here, 0, mine, msk.at[s])
    pump()
    for copy in tokens_in:
        copy.wait_recv()
    kv_there = project(there, 1, other, omsk)
    pump(2)
    for m, slot, copy in ((here, 0, kv_here), (there, 1, kv_there)):
        copy.wait_recv()
        set_keys(m, kvr.at[slot], lens[m, s].astype(F32), 1)
        attend(m, (1 - m) * T)
    until("o")
    head_rows(rows.o, 1, 3)
    for m, x in ((here, mine), (there, other)):
        mid[m] = x[...].astype(F32) + mm(hT[m], wa[rows.o, :], TN)
    norm_to(mid.at[ENC], fa.at[ENC], 1)
    n = FFH // FC
    for k, name in enumerate(("end10", "end30", "end11", "end31")):
        until(name)
        h = half if k < 2 else 1 - half
        feed(ENC, top.at[ENC], h * n + k % 2, mid if k == 0 else None)
    until("cross")
    head_rows(rows.cq, CROSSED, CROSSED + 3)
    head_rows(rows.co, CROSSED + 1, CROSSED + 4)
    wa[rows.ckv, :] = block(CKV)
    weight_copies = list(started)
    norm_to(top.at[ENC], mem, 2)
    kvs[2] = mm(wa[rows.ckv, :], mem[...], NT).astype(BF16)
    kv_cross = exchange(2)
    norm_to(mid.at[DEC], b2, 3)
    z = mm(wa[rows.cross_in, :], b2[...], NT)
    qT[CROSS] = (z[0:QR].astype(BF16).astype(F32) * base2).astype(BF16).reshape(experts, hs, R)
    gates(CROSS, xmask, z[QR:])
    set_keys(CROSS, kvs.at[2], lens[0, s].astype(F32), 0)
    kv_cross.wait_recv()
    set_keys(CROSS, kvr.at[2], lens[0, s].astype(F32), 1)
    attend(CROSS, None)
    top[DEC] = mid[DEC] + mm(hT[CROSS], wa[rows.co, :], TN)
    norm_to(top.at[DEC], fa.at[DEC], 1)
    work[...] = top[DEC]

    for i in range(2 * n):
        feed(DEC, work, i)
    first = s == 0
    y = work[...].astype(BF16)
    sent[0] = jnp.where(first, mem[...], y)
    sent[1] = jnp.where(first, y, mem[...])
    rows_copy = pltpu.make_async_copy(sent.at[0], out_rows.at[s], csem.at[1])
    rows_copy.start()
    rows_in = push(sent.at[1], out_rows.at[s], to_x)

    sent_off(weight_copies)
    gd = wd
    ct_copy.wait()
    feed_back(DEC, ct, work)
    norm_back_into(top.at[DEC], 1, work, ct, (top.at[DEC], workb.at[DEC]))
    go = attend_back(CROSS, workb[DEC], rows.co)
    sent_off((kv_here, kv_there, kv_cross))
    kvs[0] = dkv[:, R:T].astype(BF16)
    back_cross = exchange(3)
    grad_block(CROSSED + 1, go[0:128])
    grad_block(CROSSED + 4, go[128:256])
    t = mm(dT[CROSS, 0 : QR + 16, :], b2[...])
    grad_block(CROSSED, t[0:128])
    grad_block(CROSSED + 3, t[128:256])
    gaT[16:32, :] = t[QR : QR + 16]
    work[...] = mm(dT[CROSS, 0 : QR + 16, :], wa[rows.cross_in, :], TN)
    norm_back_into(mid.at[DEC], 3, work, top.at[DEC], (top.at[DEC], workb.at[DEC]))
    back_cross.wait_recv()
    dkvc = (dkv[:, 0:R] + kvr[3].astype(F32)).astype(BF16)
    grad_block(CKV, mm(dkvc, mem[...]))

    def reduce_small(base, nb, st, n, at, place):
        mine_at, far_at = base + st * half, base + st * (1 - half)
        spare = slice(at, at + n)
        come = {}

        def p1():
            come["c"] = push(gd.at[base : base + nb, :, 1 - core], sc.at[base : base + nb], to_c)

        def p2():
            come["c"].wait_recv()
            own = gd.at[base : base + nb, :, core]
            own[...] = summed([own, sc.at[base : base + nb]])
            come["p"] = [
                push(gd.at[pl.ds(b, n), :, core, hs_], sxy.at[k, spare], peer)
                for k, (b, hs_, peer) in enumerate(
                    ((mine_at, 1 - s, to_x), (far_at, s, to_y), (far_at, 1 - s, to_xy))
                )
            ]

        def p3():
            for copy in come["p"]:
                copy.wait_recv()
            pair = gd[pl.ds(mine_at, n), :, core, s].astype(F32) + sxy[0, spare].astype(F32)
            far = sxy[1, spare].astype(F32) + sxy[2, spare].astype(F32)
            sg[spare] = (pair + far).astype(BF16)
            come["z"] = [
                push(sg.at[spare, (zv + j) % nz], sz.at[spare, s, j], peer)
                for j, peers in enumerate(zip([None] + to_z, [to_x] + to_xz))
                for peer in peers
                if peer is not None
            ]

        def p4():
            for copy in come["z"]:
                copy.wait_recv()
            sz[spare, s, 0] = sg[spare, zv]
            total = sz[spare, :, 0].astype(F32)
            for j in range(1, nz):
                total = total + sz[spare, :, j].astype(F32)
            for k in range(n):
                g_small[place(k)] = total[k].astype(BF16)

        return [("small", p) for p in (p1, p2, p3, p4)]

    def reduce_split(base, nb, n, at, place):
        mine_at, far_at = base + 2 * half, base + 2 * (1 - half)
        spare = slice(at, at + n)
        come = {}

        def p1():
            come["c"] = push(gd.at[base : base + nb, :, 1 - core], sc.at[base : base + nb], to_c)

        def p2():
            come["c"].wait_recv()
            own = gd.at[base : base + nb, :, core]
            own[...] = summed([own, sc.at[base : base + nb]])
            come["y"] = push(gd.at[pl.ds(far_at, n), :, core], sy.at[spare], to_y)

        def p3():
            come["y"].wait_recv()
            sy[spare] = summed([gd.at[pl.ds(mine_at, n), :, core], sy.at[spare]])
            come["z"] = [
                push(sy.at[spare, (zv + j) % nz], sz.at[at : at + n, :, j], to_z[j - 1])
                for j in range(1, nz)
            ]

        def p4():
            wait_all(come["z"])
            sz[spare, :, 0] = sy[spare, zv]
            xs[0, spare] = summed([sz.at[spare, :, j] for j in range(nz)])
            come["x"] = push(xs.at[0, spare], xs.at[1, spare], to_x)

        def p5():
            come["x"].wait_recv()
            total = summed([xs.at[0, spare], xs.at[1, spare]])
            for k in range(n):
                g_small[place(k)] = total[k]

        return [("small", p) for p in (p1, p2, p3, p4, p5)]

    def reduce_ffn(i):
        cols = slice(i * CW, (i + 1) * CW)
        come = {}

        def rc(i):
            return prob.at[CROSS, i, :, :, :, :, 0:Dh, 0:CW]

        ways = ("yzx" if i == NC - 2 else "xyz", "yzx")

        def p1():
            come["c"] = push(ffn.at[:, :, :, 1 - core, :, :, cols], rc(i), to_c)

        def p2():
            come["c"].wait_recv()
            own = ffn.at[:, :, :, core, :, :, cols]
            own[...] = summed([own, rc(i)])
            for mat in (0, 1):
                if ways[mat] == "xyz":
                    given = ffn.at[mat, :, :, core, 1 - s, :, cols]
                    come[mat] = push(given, rx.at[min(i, NC - 2)], to_x)
                else:
                    given = ffn.at[mat, 1 - half, :, core, :, :, cols]
                    come[mat] = push(given, ry.at[i if mat else NC], to_y)

        def z_push(mat, side, to):
            return [
                push(ffn.at[mat, half, (zv + j) % nz, core, side, :, cols], to.at[j - 1], to_z[j - 1])
                for j in range(1, nz)
            ]

        def p3():
            for mat in (0, 1):
                come[mat].wait_recv()
                if ways[mat] == "xyz":
                    own = ffn.at[mat, :, :, core, s, :, cols]
                    own[...] = summed([own, rx.at[min(i, NC - 2)]])
                    given = ffn.at[mat, 1 - half, :, core, s, :, cols]
                    come[mat] = [push(given, r2.at[i], to_y)]
                else:
                    own = ffn.at[mat, half, :, core, :, :, cols]
                    own[...] = summed([own, ry.at[i if mat else NC]])
                    come[mat] = z_push(mat, slice(None), rz.at[i, mat])

        def z_sum(mat, side, out):
            out[...] = summed(
                [ffn.at[mat, half, zv, core, side, :, cols]]
                + [rz.at[i, mat, j, side] for j in range(nz - 1)]
            )

        def p4():
            for mat in (0, 1):
                wait_all(come[mat])
                if ways[mat] == "xyz":
                    own = ffn.at[mat, half, :, core, s, :, cols]
                    own[...] = summed([own, r2.at[i]])
                    come[mat] = z_push(mat, s, rz.at[i, mat, :, s])
                else:
                    z_sum(mat, slice(None), zx.at[i, mat, 0])
                    come[mat] = [push(zx.at[i, mat, 0], zx.at[i, mat, 1], to_x)]

        def p5():
            for mat in (0, 1):
                wait_all(come[mat])
                if ways[mat] == "xyz":
                    z_sum(mat, s, fin.at[mat, s, :, cols])
                    come[mat] = [same(fin.at[mat, s, :, cols], to_x)]
                else:
                    fin[mat, :, :, cols] = summed([zx.at[i, mat, 0], zx.at[i, mat, 1]])
                    come[mat] = []

        def p6():
            for mat in (0, 1):
                wait_all(come[mat])

        return [("p%d%d" % (k + 1, i), p) for k, p in enumerate((p1, p2, p3, p4, p5, p6))]

    def reduce_misc():
        come = {}

        def p1():
            come["c"] = push(ms.at[0], ms.at[1], to_c)

        def p2():
            come["c"].wait_recv()
            ms[2] = summed([ms.at[0], ms.at[1]])
            come["p"] = [
                push(ms.at[2], ms.at[3 + k], peer) for k, peer in enumerate((to_x, to_y, to_xy))
            ]

        def p3():
            wait_all(come["p"])
            pair = ms[2].astype(F32) + ms[3].astype(F32)
            far = ms[4].astype(F32) + ms[5].astype(F32)
            mz[zv] = (pair + far).astype(BF16)
            come["z"] = [same(mz.at[zv], peer) for peer in to_z]

        def p4():
            wait_all(come["z"])
            g_misc[...] = summed([mz.at[j] for j in range(nz)])

        return [("misc", p) for p in (p1, p2, p3, p4)]

    cross_sum = reduce_split(CROSSED, 5, 3, 3, lambda k: 3 + (k + 2 * half) % 3)
    cross_sum[0][1]()
    work[...] = mm(dkvc, wa[rows.ckv, :], TN).astype(BF16).astype(F32)
    norm_back_into(top.at[ENC], 2, work, None, (top.at[ENC], workb.at[ENC]))
    cross_sum[1][1]()
    feed_back(ENC, workb.at[ENC], work)

    waves = [reduce_ffn(i) for i in range(NC)]
    p1, p2, p3, p4, p5, p6 = ([wave[k] for wave in waves] for k in range(6))

    def weight_grads(i):
        for hh in (0, 1):
            at = hh * FFH + i * CW
            cols, to = slice(at, at + CW), slice(i * CW, (i + 1) * CW)
            shape = (nz, 2, 2, Dh, CW)
            up = mm(fa[ENC], gp[ENC, :, cols], TN) + mm(fa[DEC], gp[DEC, :, cols], TN)
            ffn[0, hh, :, :, :, :, to] = up.astype(BF16).reshape(shape)
            down = mm(dout_enc[...], act[ENC, :, cols], TN) + mm(ct[...], act[DEC, :, cols], TN)
            ffn[1, hh, :, :, :, :, to] = down.astype(BF16).reshape(shape)
        run(p1[i])

    def run(*events):
        for _, event in events:
            event()

    dout_enc = b2
    dout_enc[...] = workb[ENC]
    for i in range(NC // 2):
        weight_grads(i)
        if i > 0:
            run(p2[i - 1])
    norm_back_into(mid.at[ENC], 1, work, top.at[ENC], (top.at[ENC], workb.at[ENC]))
    run(p2[NC // 2 - 1])

    at_r, at_kv = QR, QR + 16
    kv_rows = slice(at_kv, at_kv + 2 * hs)

    def self_back(m, slot, pumps):
        go = attend_back(m, workb[m], rows.o, pumps)
        kvs[slot % 3] = dkv[:, R:T].astype(BF16)
        return go, exchange(slot)

    def inner(m, slot, copy):
        copy.wait_recv()
        dT[m, kv_rows, :] = (dkv[:, 0:R] + kvr[slot].astype(F32)).astype(BF16)
        work[...] = (
            mm(dT[m, 0:at_r, :], wa[rows.q, :], TN)
            + mm(dT[m, at_r:at_kv, :], wa[rows.r, :], TN)
            + mm(dT[m, kv_rows, :], wa[rows.kv, :], TN)
        )

    queue += [cross_sum[2], p3[0]]
    go, copy_there = self_back(there, 4, (0, 1, 0, 1))
    mid[DEC, 0:QR, :] = go
    for i in range(NC // 2, NC):
        weight_grads(i)
        if i > NC // 2:
            run(p2[i - 1])
    run(p3[1], p2[NC - 1])
    inner(there, 4, copy_there)
    sent_off([rows_in])
    norm_back_into(other, 0, work, top.at[there], (sent.at[1],))
    grads_in = push(sent.at[1], came, to_x)
    queue += [cross_sum[3], p3[2], p4[0], p3[3]]
    go, copy_here = self_back(here, 5, (0, 1, 1, 2))
    go = go + mid[DEC, 0:QR, :]
    grad_block(SELF + 1, go[0:128])
    grad_block(SELF + 3, go[128:256])
    t = mm(dT[ENC, 0:at_kv, :], a1[ENC]) + mm(dT[DEC, 0:at_kv, :], a1[DEC])
    grad_block(SELF, t[0:128])
    grad_block(SELF + 2, t[128:256])
    self_sum = reduce_split(SELF, 4, 2, 0, lambda k: k)
    run(self_sum[0], p4[1], self_sum[1])
    inner(here, 5, copy_here)
    grad_block(KV, mm(dT[ENC, kv_rows, :], a1[ENC]) + mm(dT[DEC, kv_rows, :], a1[DEC]))
    kv_sum = reduce_small(KV, 1, 0, 1, 2, lambda k: 2 + k)
    run(kv_sum[0])
    norm_back_into(mine, 0, work, top.at[here], (mid.at[here],))
    grads_copy = pltpu.make_async_copy(mid.at[here], out_grads.at[s], csem.at[0])
    grads_copy.start()
    ms[0] = jnp.concatenate(
        [t[at_r : at_r + 4], gaT[16:20, :], gacc[0:4, :], jnp.zeros((4, W), F32)], 0
    ).astype(BF16)
    misc_sum = reduce_misc()
    run(misc_sum[0], kv_sum[1], misc_sum[1], p4[2], p5[0], p4[3], p5[1], self_sum[2])
    run(kv_sum[2], misc_sum[2], p5[2], p5[3], self_sum[3], cross_sum[4])
    grads_in.wait_recv()
    mid[there] = came[...].astype(F32)
    far_copy = pltpu.make_async_copy(mid.at[there], out_grads.at[1 - s], csem.at[2])
    far_copy.start()
    run(kv_sum[3], misc_sum[3], self_sum[4], *p6)
    rows_in.wait_recv()
    rows_copy.wait()
    grads_copy.wait()
    far_copy.wait()
    sent_off(started)


def outputs_kernel(
    el, hs, experts, rows_in, grads_in, small_in, misc, ffn_in,
    rows, grads, n0, n1, n2, n3, gr, gq, gk, gv, go, gup, gdown, gcr, gcq, gck, gcv, gco, small, ffn, sem,
):
    copies = [
        pltpu.make_async_copy(rows_in, rows.at[0], sem.at[0]),
        pltpu.make_async_copy(grads_in, grads.at[0], sem.at[1]),
        pltpu.make_async_copy(ffn_in, ffn, sem.at[2]),
        pltpu.make_async_copy(small_in, small, sem.at[3]),
    ]
    for copy in reversed(copies):
        copy.start()
    copies.pop().wait()
    q, o, kv, cq, co, ckv = (small[k].astype(F32) for k in range(6))
    for ref, value in ((gq, q), (gcq, cq)):
        for e in range(el):
            ref[e] = value[:, e * hs : (e + 1) * hs]
    for ref, value in ((go, o), (gco, co)):
        ref[...] = value.T.reshape(ref.shape)
    gk[...], gv[...], gck[...], gcv[...] = kv[:, 0:hs], kv[:, hs:], ckv[:, 0:hs], ckv[:, hs:]
    D, W = n0.shape[1], misc.shape[1]
    feature = lax.broadcasted_iota(jnp.int32, (W, D), 0) - lax.axis_index("dp") * D
    chosen = jnp.where(feature == lax.broadcasted_iota(jnp.int32, (W, D), 1), 1.0, 0.0)
    own = mm(misc[...], chosen.astype(BF16))
    gr[...], gcr[...] = own[0:experts], own[4 : 4 + experts]
    for k, ref in enumerate((n0, n1, n2, n3)):
        ref[...] = own[8 + k : 9 + k, :]
    copies.pop().wait()
    gup[...] = ffn[0].astype(F32)
    gdown[...] = ffn[1].astype(F32)
    for copy in copies:
        copy.wait()


def run_layers(experts, hs, nz, zs, tok, routes, xroutes, lens, ct, weights):
    _, R, W = tok.shape
    FFH = weights[9].shape[1]
    Dh = W // (4 * nz)
    T, QR, NC = 2 * R, experts * hs, 4
    CW = FFH // NC
    vm = pltpu.VMEM
    dma = pltpu.SemaphoreType.DMA
    any_, whole = pl.BlockSpec(memory_space=pl.ANY), pl.BlockSpec(memory_space=vm)
    scalars = pl.BlockSpec(memory_space=pltpu.SMEM)
    return pl.pallas_call(
        functools.partial(layer_kernel, experts, hs, zs),
        out_shape=(
            jax.ShapeDtypeStruct((2, R, W), BF16),
            jax.ShapeDtypeStruct((2, R, W), F32),
            jax.ShapeDtypeStruct((6, 2, Dh, 128), BF16),
            jax.ShapeDtypeStruct((16, W), BF16),
            jax.ShapeDtypeStruct((2, 2, Dh, FFH), BF16),
        ),
        in_specs=[any_, whole, whole, scalars, any_] + [whole] * len(weights),
        out_specs=[any_, any_, whole, whole, whole],
        scratch_shapes=[
            vm((R, W), BF16),
            vm((R, W), BF16),
            vm((2, 16, R), BF16),
            vm((16, R), BF16),
            vm((R, W), BF16),
            vm((BLOCKS, nz, 2, 2, Dh, 128), BF16),
            vm((Rows(QR, hs).total, W), BF16),
            vm((2, 2, nz, 2, 2, Dh, FFH), BF16),
            vm((2, R, W), BF16),
            vm((3, experts, hs, R), BF16),
            vm((3, hs, T), BF16),
            vm((3, hs + 16, T), BF16),
            vm((3, T, 128), BF16),
            vm((3, T, 128), BF16),
            vm((2, 128, R), BF16),
            vm((2, 128, R), BF16),
            vm((3, 2 * experts, R), F32),
            vm((3, experts, 2, 2, nz, 2, T // (8 * nz), R), BF16),
            vm((3, experts, hs, R), BF16),
            vm((3, 8, R), F32),
            vm((3, QR, R), BF16),
            vm((3, QR + 16 + 2 * hs, R), BF16),
            vm((2 * hs, T), F32),
            vm((2, R, W), F32),
            vm((2, R, W), F32),
            vm((2, R, W), BF16),
            vm((R, W), BF16),
            vm((R, W), BF16),
            vm((2, R, 2 * FFH), BF16),
            vm((2, R, 2 * FFH), BF16),
            vm((R, W), F32),
            vm((2, R, W), BF16),
            vm((16, W), F32),
            vm((32, W), F32),
            vm((3, 2 * hs, R), BF16),
            vm((6, 2 * hs, R), BF16),
            vm((2, R, W), BF16),
            vm((R, W), BF16),
            vm((NC - 1, 2, nz, Dh, CW), BF16),
            vm((NC + 1, nz, 2, Dh, CW), BF16),
            vm((NC, nz, Dh, CW), BF16),
            vm((NC, 2, max(nz - 1, 1), 2, Dh, CW), BF16),
            vm((NC, 2, 2, 2, Dh, CW), BF16),
            vm((6, 16, W), BF16),
            vm((nz, 16, W), BF16),
            vm((BLOCKS, nz, 2, Dh, 128), BF16),
            vm((3, 3, nz, Dh, 128), BF16),
            vm((3, nz, Dh, 128), BF16),
            vm((6, nz, 2, Dh, 128), BF16),
            vm((2, 6, 2, Dh, 128), BF16),
            vm((6, 2, nz, Dh, 128), BF16),
            dma((200,)),
            dma((200,)),
            dma((3,)),
        ],
        compiler_params=pltpu.CompilerParams(
            collective_id=0, has_side_effects=True, vmem_limit_bytes=63 * 2**20
        ),
    )(tok, routes, xroutes, lens, ct, *weights)


def on_device(
    tokens, self_routes, cross_routes, lengths, cotangent,
    norm_attn, norm_ffn, norm_final, norm_cross,
    router, query_weight, key_weight, value_weight, output_weight, up_weight, down_weight,
    cross_router, cross_query, cross_key, cross_value, cross_output,
):
    dp = lax.axis_size("dp")
    R, W = tokens.shape[2:]
    el, D, hs = query_weight.shape
    experts = el * lax.axis_size("head")
    FFH = up_weight.shape[1]
    nz = min(4, dp // 2)
    zs = dp // nz
    Dv = W // (2 * nz)
    blocks = [[z * zs + j for j in range(zs)] for z in range(nz)]
    core = lax.axis_index("dp") % 2

    def widened(a, axis):
        if zs == 2:
            return a
        a = lax.all_gather(a, "dp", axis=axis, tiled=True, axis_index_groups=blocks)
        return lax.dynamic_slice_in_dim(a, core * Dv, Dv, axis)

    def narrowed(a):
        if zs == 2:
            return a
        wide = jnp.zeros((a.shape[0], 2 * Dv, a.shape[2]), BF16)
        wide = lax.dynamic_update_slice_in_dim(wide, a, core * Dv, 1)
        return lax.psum_scatter(
            wide, "dp", scatter_dimension=1, axis_index_groups=blocks, tiled=True
        )

    gains = (norm_attn, norm_ffn, norm_final, norm_cross)
    weights = [widened(g, 0).reshape(1, Dv) for g in gains]
    weights += [
        widened(w, axis)
        for w, axis in (
            (router.T, 1), (query_weight, 1), (key_weight, 0), (value_weight, 0),
            (output_weight, 2), (up_weight, 0), (down_weight.T, 0),
            (cross_router.T, 1), (cross_query, 1), (cross_key, 0), (cross_value, 0),
            (cross_output, 2),
        )
    ]
    out, grads, small, misc, ffn = run_layers(
        experts, hs, nz, zs, tokens[0],
        jnp.swapaxes(self_routes[0], 1, 2), jnp.swapaxes(cross_routes, 1, 2),
        lengths[:, :, 0], cotangent, weights,
    )
    small = narrowed(small.reshape(6, Dv, 128))
    ffn = narrowed(ffn.reshape(2, Dv, FFH))

    def f32(*shape):
        return jax.ShapeDtypeStruct(shape, F32)

    whole = pl.BlockSpec(memory_space=pltpu.VMEM)
    attention = (
        f32(experts, D), f32(el, D, hs), f32(D, hs), f32(D, hs), f32(el, hs, D),
    )
    done = pl.pallas_call(
        functools.partial(outputs_kernel, el, hs, experts),
        out_shape=(
            jax.ShapeDtypeStruct((1, 2, R, W), BF16), f32(1, 2, R, W),
            *(f32(1, D),) * 4, *attention, *(f32(D, FFH),) * 2, *attention,
        ),
        in_specs=[pl.BlockSpec(memory_space=pltpu.HBM)] * 3 + [whole, pl.BlockSpec(memory_space=pltpu.HBM)],
        out_specs=[whole] * 18,
        scratch_shapes=[
            pltpu.VMEM(small.shape, BF16), pltpu.VMEM(ffn.shape, BF16), pltpu.SemaphoreType.DMA((4,)),
        ],
        compiler_params=pltpu.CompilerParams(vmem_limit_bytes=60 * 2**20),
    )(out, grads, small, misc, ffn)
    rows, grads, n0, n1, n2, n3, gr, gq, gk, gv, go, gup, gdown, gcr, gcq, gck, gcv, gco = done
    return (
        rows, grads, *(g.reshape(D) for g in (n0, n1, n2, n3)),
        gr.T, gq, gk, gv, go, gup, gdown.T, gcr.T, gcq, gck, gcv, gco,
    )


def solution(mesh):
    rows = P("section", None, ("dp", "head"), None)
    vector, tall = P("dp"), P("dp", None)
    query, out = P("head", "dp", None), P("head", None, "dp")
    weights = (
        vector, vector, vector, vector,
        tall, query, tall, tall, out, P("dp", "head"), P("head", "dp"),
        tall, query, tall, tall, out,
    )
    return jax.shard_map(
        on_device,
        mesh=mesh,
        in_specs=(
            rows, P("section", None, "dp", None), P(None, "dp", None), P(None, None, "dp"),
            P(None, ("dp", "head"), None), *weights,
        ),
        out_specs=(rows, rows, *weights),
        check_vma=False,
    )
```
